32 devices in a mesh: dp: 16 (over z, x, core), group: 2 (over y).
Axes of the slice: x: 2, y: 2, z: 4, core: 2. Of those that a mesh axis runs over, the one named last changes fastest.
Arguments:
- queries: bfloat16 [4096, 256], P('dp'), may hold values from -110 to 110
- item_features: bfloat16 [4096, 2048], P('dp', 'group'), may hold values from -6 to 6
- corpus: bfloat16 [32768, 2048], P('dp', 'group'), may hold values from -6 to 6
- sample_ids: int32 [16384], P('dp'), may hold values from 0 to 2047
- sample_shift: bfloat16 [16384], P('dp'), may hold values from -2 to 2
- w1: bfloat16 [2048, 1024], P(None, 'group'), may hold values from -0.125 to 0.125
- w2: bfloat16 [1024, 256], P('group'), may hold values from -0.1875 to 0.1875
Outputs:
- query_loss: float32 [4096], P(('dp', 'group'))
- grad_query: float32 [4096, 256], P(('dp', 'group'))
- grad_w1: float32 [2048, 1024], P(None, 'group')
- grad_w2: float32 [1024, 256], P('group')
The draws below stay inside these ranges and needn't reach their ends.
Inputs may be any that keep to these rules, and one draw needn't show every extreme that they name: sample_ids[k] is a row of the corpus block of the dp index that holds position k.
All inputs are finite; a program needn't handle non-finite values.
Results may differ from the reference program's by a relative error of at most 0.02.
The reference program's roundings to bfloat16 on the way count: a program that leaves them out, or rounds other values in their place, can miss the bound.
Values may be sent and summed in bfloat16 or wider, within the bound.
A program may use at most 128 MiB of HBM per device.

```python
import math
import jax
import jax.numpy as jnp
from jax import lax

F = 2048
H = 1024
E = 256
Q_DP = 256
NEG_DP = 1024
SLAB = 2048
PAIRS = 4096
NEGS = 16384
CORPUS = 32768
N_DP = 16


def draw_queries(key, part):
    key_base, key_scale, key_pick, key_boost = jax.random.split(key, 4)
    row_scale = jnp.exp(jax.random.uniform(key_scale, (PAIRS, 1), jnp.float32, math.log(0.5), math.log(5.0)))
    chosen = jax.random.randint(key_pick, (PAIRS, 1), 0, 16) == 0
    boost = jax.random.uniform(key_boost, (PAIRS, 1), jnp.float32, 40.0, 62.0)
    base_values = jnp.clip(jax.random.normal(key_base, (PAIRS, E), jnp.float32), -4.0, 4.0)
    drawn = base_values * row_scale
    strong = jnp.clip(base_values, -1.7, 1.7) * boost
    return jnp.where(chosen, strong, drawn).astype(jnp.bfloat16)


def set_ends(drawn, own_key, least, largest):
    longest = drawn.shape.index(max(drawn.shape))
    spots = []
    for shift in (0, 1):
        where = [jax.random.randint(jax.random.fold_in(own_key, axis), (), 0, length) for axis, length in enumerate(drawn.shape)]
        where[longest] = (where[longest] + shift) % drawn.shape[longest]
        spots.append(tuple(where))
    return drawn.at[spots[0]].set(least).at[spots[1]].set(largest)


def block_levels(key, extent, pieces, least, high):
    factor_of = 1.0
    for axis_at, parts in pieces:
        steps = jax.random.uniform(jax.random.fold_in(jax.random.fold_in(key, 6), axis_at), (parts,), jnp.float32, least / len(pieces), high / len(pieces))
        factor_of = factor_of * jnp.repeat(jnp.exp(steps), extent[axis_at] // parts).reshape((-1,) + (1,) * (len(extent) - 1 - axis_at))
    return factor_of


def scatter_about(own_key, shape, width, reach, pieces=(), held_as=jnp.bfloat16):
    values = jax.random.normal(own_key, shape, jnp.float32) * width
    if len(pieces) > 0:
        values = block_levels(own_key, shape, pieces, -0.22, 0.18) * values
    return jnp.clip(values, min=-reach, max=reach).astype(held_as)


def setup_inputs(seed: int = 0) -> dict:
    splits = jax.random.split(jax.random.key(seed), 8)
    return {
        "queries": draw_queries(jax.random.fold_in(splits[7], 71), 0),
        "item_features": scatter_about(splits[1], (PAIRS, F), 1.0, 6.0, ((0, 16), (1, 2))),
        "corpus": scatter_about(splits[2], (CORPUS, F), 1.0, 6.0, ((0, 16), (1, 2))),
        "sample_ids": set_ends(jax.random.randint(splits[3], (NEGS,), 0, SLAB), jax.random.fold_in(splits[3], 1), 0, SLAB - 1).astype(jnp.int32),
        "sample_shift": jnp.clip(jax.random.uniform(splits[4], (NEGS,), jnp.float32, -2.0, 2.0) * block_levels(splits[4], (NEGS,), ((0, 16),), -0.4, 0.0), -2.0, 2.0).astype(jnp.bfloat16),
        "w1": scatter_about(splits[5], (F, H), F ** -0.5, 0.125, ((1, 2),)),
        "w2": scatter_about(splits[6], (H, E), H ** -0.5, 0.1875, ((0, 2),)),
    }


def reference(queries, item_features, corpus, sample_ids, sample_shift, w1, w2):
    score_scale = E ** (-0.5)
    owner_rows = jnp.arange(NEGS, dtype=jnp.int32) // NEG_DP
    picked = jnp.take(corpus, owner_rows * SLAB + sample_ids.astype(jnp.int32), axis=0)
    features = jnp.concatenate([item_features, picked], 0)
    pre_act = jnp.dot(features, w1, preferred_element_type=jnp.float32)
    hidden = jnp.maximum(pre_act, 0.0).astype(jnp.bfloat16)
    embedded = jnp.dot(hidden, w2, preferred_element_type=jnp.float32)
    inverse = lax.rsqrt(lax.optimization_barrier(jnp.mean(embedded * embedded, -1, keepdims=True)) + 1e-06)
    normed = (embedded * inverse).astype(jnp.bfloat16)
    bias_wide = jnp.concatenate([jnp.zeros((PAIRS,), jnp.float32), -sample_shift.astype(jnp.float32)])
    query_blocks = queries.reshape(N_DP, Q_DP, E)
    positive_blocks = normed[:PAIRS].reshape(N_DP, Q_DP, E)

    def one_block(grad_acc, inputs):
        query_blk, positive_blk = inputs
        logits = score_scale * jnp.dot(query_blk, normed.T, preferred_element_type=jnp.float32) + bias_wide
        highest = lax.optimization_barrier(jnp.max(logits, -1, keepdims=True))
        row_sum = lax.optimization_barrier(jnp.sum(jnp.exp(logits - highest), -1, keepdims=True))
        log_total = highest + jnp.log(row_sum)
        positive = score_scale * lax.optimization_barrier(jnp.sum(query_blk.astype(jnp.float32) * positive_blk.astype(jnp.float32), -1))
        loss_blk = log_total[:, 0] - positive
        softmax = jnp.exp(logits - log_total).astype(jnp.bfloat16)
        grad_blk = score_scale * (jnp.dot(softmax, normed, preferred_element_type=jnp.float32) - positive_blk.astype(jnp.float32))
        grad_acc = grad_acc + jnp.dot(softmax.T, query_blk, preferred_element_type=jnp.float32)
        return (grad_acc, (loss_blk, grad_blk))
    grad_acc, outputs = lax.scan(one_block, jnp.zeros((PAIRS + NEGS, E), jnp.float32), (query_blocks, positive_blocks))
    loss_blocks, grad_blocks = outputs
    target = jnp.concatenate([queries.astype(jnp.float32), jnp.zeros((NEGS, E), jnp.float32)], 0)
    grad_normed = score_scale * (grad_acc - target)
    grad_embed = inverse * grad_normed - inverse ** 3 * embedded * lax.optimization_barrier(jnp.sum(grad_normed * embedded, -1, keepdims=True)) / E
    grad_back = grad_embed.astype(jnp.bfloat16)
    grad_pre = jnp.where(pre_act > 0, jnp.dot(grad_back, w2.T, preferred_element_type=jnp.float32), 0.0).astype(jnp.bfloat16)
    grad_w2 = jnp.dot(hidden.T, grad_back, preferred_element_type=jnp.float32)
    grad_w1 = jnp.dot(features.T, grad_pre, preferred_element_type=jnp.float32)
    return (loss_blocks.reshape(PAIRS), grad_blocks.reshape(PAIRS, E), grad_w1, grad_w2)
```

```python
import functools

import jax
import jax.numpy as jnp
from jax import lax
from jax.experimental import pallas as pl
from jax.experimental.pallas import tpu as pltpu
from jax.sharding import PartitionSpec as P

F32 = jnp.float32
BF16 = jnp.bfloat16
MESH = pl.DeviceIdType.MESH
ANY = pl.BlockSpec(memory_space=pl.ANY)
VMEM = pl.BlockSpec(memory_space=pltpu.VMEM)


def mm(a, b):
    return jnp.dot(a, b, preferred_element_type=F32)


def bits_of(n):
    return [1 << i for i in range(n.bit_length() - 1)]


def partner(axis, step):
    i = lax.axis_index(axis)
    bit = lax.rem(lax.div(i, step), 2)
    return bit, {axis: i + step - 2 * step * bit}


def greet(peers):
    barrier = pltpu.get_barrier_semaphore()
    for peer in peers:
        pl.semaphore_signal(barrier, inc=1, device_id=peer, device_id_type=MESH)
    pl.semaphore_wait(barrier, len(peers))


def score_kernel(groups, n_dp, local, queries_in, normed, normed_t, bias,
                 total_ref, hat_ref, part_ref, rest_ref,
                 queries, logits, stats, arrived, qsem, send_sem, recv_sem, fsend, frecv):
    tiles, cols, width = logits.shape
    emb = normed.shape[1]
    scale = emb ** (-0.5)
    member = lax.axis_index("group")
    rounds = [("dp", b) for b in bits_of(n_dp)] + [("group", b) for b in bits_of(groups)]
    peers = [partner(a, b)[1] for a, b in rounds]
    others = [lax.rem(member + s, groups) for s in range(1, groups)]
    extra = [{"group": o} for o in others] if groups > 2 else []
    fetch = pltpu.make_async_copy(queries_in, queries, qsem)
    fetch.start()
    greet(peers + extra)
    copies = []
    for s in range(1, groups):
        for t in range(1, groups):
            k = (s - 1) * (groups - 1) + t - 1
            copy = pltpu.make_async_remote_copy(
                src_ref=local.at[(s + t) % groups],
                dst_ref=rest_ref.at[s - 1, t - 1],
                send_sem=fsend.at[k], recv_sem=frecv.at[k],
                device_id={"group": others[s - 1]}, device_id_type=MESH)
            copy.start()
            copies.append(copy)

    def first(i, carry):
        q = queries[pl.ds(pl.multiple_of(i * width, width), width), :]
        block = scale * lax.dot_general(
            normed[...], q, (((1,), (1,)), ((), ())), preferred_element_type=F32) + bias[...]
        logits[i] = block
        top = jnp.max(block, 0, keepdims=True)
        stats[0, 0, pl.ds(i, 1), :] = top
        stats[0, 1, pl.ds(i, 1), :] = jnp.sum(jnp.exp(block - top), 0, keepdims=True)
        return carry

    fetch.wait()
    lax.fori_loop(0, tiles, first, 0)
    for r, peer in enumerate(peers):
        copy = pltpu.make_async_remote_copy(
            src_ref=stats.at[r], dst_ref=arrived.at[r],
            send_sem=send_sem.at[r], recv_sem=recv_sem.at[r],
            device_id=peer, device_id_type=MESH)
        copy.start()
        copy.wait()
        m0, s0, m1, s1 = stats[r, 0], stats[r, 1], arrived[r, 0], arrived[r, 1]
        top = jnp.maximum(m0, m1)
        stats[r + 1, 0] = top
        stats[r + 1, 1] = s0 * jnp.exp(m0 - top) + s1 * jnp.exp(m1 - top)
    last = len(peers)
    total_ref[...] = stats[last, 0] + jnp.log(stats[last, 1])
    hat_ref[...] = jnp.zeros_like(hat_ref)

    def second(i, carry):
        at_i = pl.ds(pl.multiple_of(i * width, width), width)
        p = jnp.exp(logits[i] - total_ref[pl.ds(i, 1), :]).astype(BF16)
        hat_ref[...] += mm(p, queries[at_i, :])
        part_ref[at_i, :] = mm(normed_t[...], p).T
        return carry

    lax.fori_loop(0, tiles, second, 0)
    for copy in copies:
        copy.wait()


def score(groups, n_dp, local, queries, normed, bias):
    rows, fg = local.shape[1:]
    width = 256
    total, emb = queries.shape
    tiles = total // width
    rounds = len(bits_of(n_dp)) + len(bits_of(groups))
    n_copies = (groups - 1) ** 2
    return pl.pallas_call(
        functools.partial(score_kernel, groups, n_dp),
        out_shape=(
            jax.ShapeDtypeStruct((tiles, width), F32),
            jax.ShapeDtypeStruct((rows, emb), F32),
            jax.ShapeDtypeStruct((total, emb), F32),
            jax.ShapeDtypeStruct((groups - 1, groups - 1, rows, fg), BF16),
        ),
        in_specs=[ANY, ANY, VMEM, VMEM, VMEM],
        out_specs=(VMEM, VMEM, VMEM, ANY),
        scratch_shapes=[
            pltpu.VMEM((total, emb), BF16),
            pltpu.VMEM((tiles, rows, width), F32),
            pltpu.VMEM((rounds + 1, 2, tiles, width), F32),
            pltpu.VMEM((rounds, 2, tiles, width), F32),
            pltpu.SemaphoreType.DMA,
            pltpu.SemaphoreType.DMA((rounds,)),
            pltpu.SemaphoreType.DMA((rounds,)),
            pltpu.SemaphoreType.DMA((n_copies,)),
            pltpu.SemaphoreType.DMA((n_copies,)),
        ],
        compiler_params=pltpu.CompilerParams(
            collective_id=0, has_side_effects=True, vmem_limit_bytes=44 << 20),
        name="score",
    )(local, queries, normed, normed.T, bias)


def reduce_kernel(plans, n_in, n_peers_of, *refs):
    n = len(plans)
    ins, refs = refs[:n_in], refs[n_in:]
    outs = refs[:n]
    accs, sends, recvs = (refs[n + i * n : 2 * n + i * n] for i in range(3))
    send_sem, recv_sem, gsend, grecv = refs[4 * n :]
    greet([partner(a, b)[1] for a, b in n_peers_of])
    live = {}

    def begin(i, r):
        rounds, bases, _, source, start, count = plans[i]
        bit, peer = partner(*rounds[r])
        half = count >> (r + 1)
        at0 = count - 2 * half

        def stage(j, carry):
            if r == 0:
                block = ins[source][start + bases(j) + (1 - bit) * bases(half)]
            else:
                block = accs[i][(1 - bit) * half + j]
            sends[i][at0 + j] = block.astype(BF16)
            return carry

        lax.fori_loop(0, half, stage, 0)
        copy = pltpu.make_async_remote_copy(
            src_ref=sends[i].at[pl.ds(at0, half)], dst_ref=recvs[i].at[pl.ds(at0, half)],
            send_sem=send_sem.at[i, r], recv_sem=recv_sem.at[i, r],
            device_id=peer, device_id_type=MESH)
        copy.start()
        live[i] = copy

    def finish(i, r):
        rounds, bases, _, source, start, count = plans[i]
        bit, _ = partner(*rounds[r])
        half = count >> (r + 1)
        at0 = count - 2 * half
        live[i].wait()

        def add(j, carry):
            if r == 0:
                block = ins[source][start + bases(j) + bit * bases(half)]
            else:
                block = accs[i][bit * half + j]
            accs[i][j] = block + recvs[i][at0 + j].astype(F32)
            return carry

        lax.fori_loop(0, half, add, 0)

    def place(i, r):
        rounds = plans[i][0]
        return sum(partner(*rounds[k])[0] * (plans[i][5] >> (k + 1)) for k in range(r + 1))

    def share(i, r):
        peer = partner(*plans[i][0][r])[1]
        span = pl.ds(place(i, r), plans[i][5] >> (r + 1))
        copy = pltpu.make_async_remote_copy(
            src_ref=outs[i].at[span], dst_ref=outs[i].at[span],
            send_sem=gsend.at[i, r], recv_sem=grecv.at[i, r],
            device_id=peer, device_id_type=MESH)
        copy.start()
        live[i] = copy

    def advance(i, step):
        rounds, _, gather = plans[i][:3]
        k = len(rounds)
        if 0 < step <= k:
            finish(i, step - 1)
        if step < k:
            begin(i, step)
        elif step == k and not gather:
            outs[i][0] = accs[i][0]
        elif gather and step <= 2 * k:
            if step == k:
                outs[i][place(i, k - 1)] = accs[i][0].astype(BF16)
            else:
                live[i].wait()
            if step < 2 * k:
                share(i, 2 * k - 1 - step)

    steps = max(len(p[0]) * (2 if p[2] else 1) for p in plans) + 1
    for step in range(steps):
        for i in range(n):
            advance(i, step)


def bit_place(steps, j):
    k = len(steps)
    out = 0
    for i, step in enumerate(steps):
        weight = 1 << (k - 1 - i)
        if isinstance(j, int):
            out += (j // weight) % 2 * step
        else:
            out = out + lax.rem(lax.div(j, weight), 2) * step
    return out


def reduce_all(groups, n_dp, xs, parts):
    plans = []
    for source, start, n, rounds, gather in parts:
        if gather:
            steps = [n >> (k + 1) for k in range(len(rounds))]
        else:
            steps = [b * groups if a == "dp" else b for a, b in rounds]
        bases = functools.partial(bit_place, steps)
        plans.append((rounds, bases, gather, source, start, n))
    shapes = [(p[5],) + xs[p[3]].shape[1:] for p in plans]
    most = max(len(p[0]) for p in plans)
    peers = [("dp", b) for b in bits_of(n_dp)] + [("group", b) for b in bits_of(groups)]
    sems = pltpu.SemaphoreType.DMA((len(plans), most))
    return pl.pallas_call(
        functools.partial(reduce_kernel, plans, len(xs), peers),
        out_shape=tuple(
            jax.ShapeDtypeStruct(shape, BF16) if p[2] else jax.ShapeDtypeStruct((1,) + shape[1:], F32)
            for shape, p in zip(shapes, plans)),
        in_specs=[VMEM] * len(xs),
        out_specs=(VMEM,) * len(plans),
        scratch_shapes=[pltpu.VMEM((s[0] // 2,) + s[1:], F32) for s in shapes]
        + [pltpu.VMEM(s, BF16) for s in shapes] * 2 + [sems] * 4,
        compiler_params=pltpu.CompilerParams(
            collective_id=1, has_side_effects=True, vmem_limit_bytes=48 << 20),
        name="reduce_all",
    )(*xs)


def nt(a, b):
    return lax.dot_general(a, b, (((1,), (1,)), ((), ())), preferred_element_type=F32)


def tn(a, b):
    return lax.dot_general(a, b, (((0,), (0,)), ((), ())), preferred_element_type=F32)


def loop(n, body):
    def step(i, carry):
        body(i)
        return carry

    lax.fori_loop(0, n, step, 0)


def weights_of(order):
    return {axis_step: 1 << (len(order) - 1 - k) for k, axis_step in enumerate(order)}


class Plan:
    def __init__(self, n_dp, queries, items, corpus, w1, w2):
        self.n_dp = n_dp
        self.query_rows, self.emb = queries.shape
        self.quota = self.query_rows // 2
        self.fg = items.shape[1]
        self.slab = corpus.shape[0]
        self.feats, self.hg = w1.shape
        bits = bits_of(n_dp)
        core, x, z = bits[0], bits[1], bits[2:]
        dp = lambda steps: [("dp", s) for s in steps]
        y = [("group", 1)]
        self.gather_order = [x] + z[::-1] + [core]
        self.q_order = dp([core, x]) + y + dp(z)
        self.w_orders = [
            dp([core]) + y + dp([x]) + dp(z),
            dp([core, x]) + y + dp(z),
            dp([core]) + dp(z) + dp([x]) + y,
        ]
        self.w2_order = self.w_orders[1]
        self.bits = bits


PART_ROWS = (0, 48, 96, 128)
CH = 128


def fused_kernel(pn, rows, queries, items, corpus, meta_in, w1, w2,
                 loss_ref, gq_ref, gw1_ref, gw2_ref,
                 big, q_all, w1v, w2v, mine, peer, far, hot, meta, pre, hid, emb, nrm, nrms, nrm_t,
                 bias, hat, logits, qpt, stats, arrived, total_ref, fac, featt, gp, ge,
                 recv, ag, qsend, qrecv, acc2, send2, recv2, ag2, lsem, ssem, rsem):
    n_dp, width, fg, hg, slab = pn.n_dp, pn.query_rows, pn.fg, pn.hg, pn.slab
    quota, e_dim = pn.quota, pn.emb
    negs = rows - quota
    chunks = negs // CH
    scale = e_dim ** (-0.5)
    m = lax.axis_index("group")
    d = lax.axis_index("dp")
    other = 1 - m
    ypeer = partner("group", 1)[1]
    core, xbit = pn.bits[0], pn.bits[1]
    rounds = [("dp", s) for s in pn.bits] + [("group", 1)]
    count = iter(range(1000))
    lcount = iter(range(100))

    def bit(step):
        return lax.rem(lax.div(d, step), 2)

    def remote(src, dst, to, k=None):
        k = next(count) if k is None else k
        return pltpu.make_async_remote_copy(
            src_ref=src, dst_ref=dst, send_sem=ssem.at[k], recv_sem=rsem.at[k],
            device_id=to, device_id_type=MESH)

    def local(src, dst):
        copy = pltpu.make_async_copy(src, dst, lsem.at[next(lcount)])
        copy.start()
        return copy

    gw = {s: 1 << k for k, s in enumerate(pn.gather_order)}
    pos = sum(bit(s) * gw[s] for s in pn.bits)
    tiles = n_dp

    c_q = local(queries, q_all.at[pos])
    c_meta = local(meta_in, meta)
    c_slab = [local(corpus.at[:, n * 256 : (n + 1) * 256], big.at[n * slab : (n + 1) * slab])
              for n in range(fg // 256)]
    c_mine = local(items.at[pl.ds(pl.multiple_of(m * quota, quota), quota)], mine.at[0:quota])
    c_w1 = local(w1, w1v.at[0])
    c_w2 = local(w2, w2v.at[0])
    greet([partner(a, b)[1] for a, b in rounds])

    e = bit(core) * 2 + bit(xbit)
    q1, q2 = w1.shape[0] // 4, w2.shape[0] // 4

    def span(n, base, size):
        return pl.ds(pl.multiple_of(base * n, n), n * size)

    wy = [remote(w1.at[span(q1, e, 1)], w1v.at[1, span(q1, e, 1)], ypeer),
          remote(w2.at[span(q2, e, 1)], w2v.at[1, span(q2, e, 1)], ypeer)]
    for c in wy:
        c.start()
    item_send = remote(items.at[pl.ds(pl.multiple_of(other * quota, quota), quota)],
                       peer.at[0:quota], ypeer)
    item_send.start()
    c_q.wait()
    q_steps = pn.gather_order

    def q_gather(k):
        size = 1 << k
        base = lax.div(pos, size) * size
        view = q_all.at[pl.ds(base, size)]
        c = remote(view, view, partner("dp", q_steps[k])[1])
        c.start()
        return c

    qg = q_gather(0)
    k_far = [next(count) for _ in range(chunks)][0]

    def rows_at(k):
        return pl.ds(pl.multiple_of(quota + k * CH, CH), CH)

    def far_copy(k):
        return remote(far.at[pl.ds(pl.multiple_of(k * CH, CH), CH)], peer.at[rows_at(k)],
                      ypeer, k_far + k)

    def column(r):
        return jnp.broadcast_to(meta[pl.ds(r, 1), :], (8, CH)).T[:, :1]

    def pick(who, k, dst, at):
        ids = column(who * chunks + k)
        where = lax.broadcasted_iota(jnp.int32, (CH, slab), 1).astype(F32)
        hot[...] = jnp.where(ids == where, 1.0, 0.0).astype(BF16)
        for n in range(fg // 256):
            dst[at, n * 256 : (n + 1) * 256] = mm(
                hot[...], big[n * slab : (n + 1) * slab, :]).astype(BF16)

    c_meta.wait()
    for c in c_slab:
        c.wait()

    def pick_far(k):
        pick(other, k, far, pl.ds(pl.multiple_of(k * CH, CH), CH))
        far_copy(k).start()

    loop(chunks, pick_far)
    qg.wait()
    qg = q_gather(1)
    loop(chunks, lambda k: pick(m, k, mine, rows_at(k)))
    bias[0:quota, :] = jnp.zeros((quota, width), F32)

    def put_bias(k):
        bias[rows_at(k), :] = jnp.broadcast_to(
            -column(2 * chunks + m * chunks + k), (CH, width))

    loop(chunks, put_bias)
    c_mine.wait()
    c_w1.wait()
    c_w2.wait()

    nj = hg // 256

    def tower_add(r0, r1, feat, half, c, first):
        for j in range(nj):
            part = mm(feat[r0:r1, :], w1v[c, pl.ds(pl.multiple_of(half * fg, fg), fg),
                                         j * 256 : (j + 1) * 256])
            if first:
                pre[c * nj + j, r0:r1, :] = part
            else:
                pre[c * nj + j, r0:r1, :] += part

    tower_add(0, rows, mine, m, 0, True)
    for c in wy:
        c.wait()
    pair = lax.div(e, 2) * 2
    wx = [remote(w1v.at[1, span(q1, e, 1)], w1v.at[1, span(q1, e, 1)], partner("dp", xbit)[1]),
          remote(w2v.at[1, span(q2, e, 1)], w2v.at[1, span(q2, e, 1)], partner("dp", xbit)[1])]
    for c in wx:
        c.start()
    for k in range(2, len(q_steps) - 1):
        qg.wait()
        qg = q_gather(k)

    def turn(src, half, n):
        at = pl.multiple_of(n * 256, 256)
        featt[pl.ds(pl.multiple_of(half * fg + at, 256), 256), :] = src[:, pl.ds(at, 256)].T

    loop(fg // 256, lambda n: turn(mine, m, n))
    for c in wx:
        c.wait()
    wc = [remote(w1v.at[1, span(q1, pair, 2)], w1v.at[1, span(q1, pair, 2)], partner("dp", core)[1]),
          remote(w2v.at[1, span(q2, pair, 2)], w2v.at[1, span(q2, pair, 2)], partner("dp", core)[1])]
    for c in wc:
        c.start()
    qg.wait()
    qg = q_gather(len(q_steps) - 1)
    for c in wc:
        c.wait()
    tower_add(0, rows, mine, m, 1, True)

    def finish_tower(r0, r1):
        loop(2, lambda c: tower_add(r0, r1, peer, other, c, False))
        emb[r0:r1, :] = jnp.zeros((r1 - r0, e_dim), F32)

        def second_layer(c):
            for j in range(nj):
                h = jnp.maximum(pre[c * nj + j, r0:r1, :], 0.0).astype(BF16)
                hid[c * nj + j, r0:r1, :] = h
                emb[r0:r1, :] += mm(h, w2v[c, j * 256 : (j + 1) * 256, :])

        loop(2, second_layer)
        em = emb[r0:r1, :]
        inv = lax.rsqrt(jnp.mean(em * em, -1, keepdims=True) + 1e-06)
        no = (em * inv).astype(BF16)
        nrm[r0:r1, :] = no
        nrms[r0:r1, :] = (no.astype(F32) * scale).astype(BF16)
        nrm_t[:, r0:r1] = no.astype(F32).T.astype(BF16)

    oq = weights_of(pn.q_order)
    gq = oq[("group", 1)]

    def shard_of(i):
        return sum(lax.rem(lax.div(i, gw[s]), 2) * oq[("dp", s)] for s in pn.bits)

    ra = rows - CH
    half_q = width // 2

    def score_a(i):
        block = nt(nrms[0:ra, :], q_all[i]) + bias[0:ra, :]
        logits[i, 0:ra, :] = block
        top = jnp.max(block, 0, keepdims=True)
        p = jnp.exp(block - top)
        stats[0, 0, pl.ds(i, 1), :] = top
        stats[0, 1, pl.ds(i, 1), :] = jnp.sum(p, 0, keepdims=True)
        part = mm(nrm_t[:, 0:ra], p.astype(BF16))
        j = shard_of(i)
        for g in range(2):
            qpt[j + g * gq] = part[:, g * half_q : (g + 1) * half_q]

    def score_b(i):
        block = nt(nrms[ra:rows, :], q_all[i]) + bias[ra:rows, :]
        logits[i, ra:rows, :] = block
        before = stats[0, 0, pl.ds(i, 1), :]
        top = jnp.maximum(before, jnp.max(block, 0, keepdims=True))
        shrink = jnp.exp(before - top)
        p = jnp.exp(block - top)
        stats[0, 0, pl.ds(i, 1), :] = top
        stats[0, 1, pl.ds(i, 1), :] = (
            stats[0, 1, pl.ds(i, 1), :] * shrink + jnp.sum(p, 0, keepdims=True))
        part = mm(nrm_t[:, ra:rows], p.astype(BF16))
        j = shard_of(i)
        for g in range(2):
            cut = slice(g * half_q, (g + 1) * half_q)
            qpt[j + g * gq] = qpt[j + g * gq] * shrink[:, cut] + part[:, cut]

    item_send.wait()
    loop(chunks - 1, lambda k: far_copy(k).wait())
    finish_tower(0, ra)
    qg.wait()
    loop(tiles, score_a)
    far_copy(chunks - 1).wait()
    finish_tower(ra, rows)
    loop(tiles, score_b)

    for r, (axis, step) in enumerate(rounds):
        copy = remote(stats.at[r], arrived.at[r], partner(axis, step)[1])
        copy.start()
        if r == 0:
            loop(fg // 256, lambda n: turn(peer, other, n))
        copy.wait()
        m0, s0, m1, s1 = stats[r, 0], stats[r, 1], arrived[r, 0], arrived[r, 1]
        top = jnp.maximum(m0, m1)
        stats[r + 1, 0] = top
        stats[r + 1, 1] = s0 * jnp.exp(m0 - top) + s1 * jnp.exp(m1 - top)
    last = len(rounds)
    total_ref[...] = stats[last, 0] + jnp.log(stats[last, 1])
    fac[...] = jnp.exp(stats[0, 0] - total_ref[...])

    class Chain:
        def __init__(self, order, put, add, send_at, recv_at):
            self.order, self.put, self.add = order, put, add
            self.send_at, self.recv_at = send_at, recv_at
            self.n = 1 << len(order)
            self.base = 0

        def begin(self, r):
            half = self.n >> (r + 1)
            at0 = self.n - 2 * half
            b, to = partner(*self.order[r])
            if r > 0:
                base = self.base
                loop(half, lambda j: self.put(at0 + j, base + (1 - b) * half + j))
            self.copy = remote(self.send_at(at0, half), self.recv_at(at0, half), to)
            self.copy.start()

        def finish(self, r):
            half = self.n >> (r + 1)
            at0 = self.n - 2 * half
            b, _ = partner(*self.order[r])
            self.copy.wait()
            if r > 0:
                self.base = self.base + b * half
            base = self.base
            loop(half, lambda j: self.add(base + j, at0 + j))

        def step(self, r):
            if r > 0:
                self.finish(r - 1)
            if r < len(self.order):
                self.begin(r)

    cb = bit(core)
    own16 = cb * n_dp

    def q_put(slot, a):
        qsend[slot] = qpt[own16 + a].astype(BF16)

    def q_add(a, slot):
        qpt[own16 + a] = qpt[own16 + a] + qrecv[slot].astype(F32)

    q_chain = Chain(pn.q_order, q_put, q_add,
                    lambda a, n: qsend.at[pl.ds(a, n)], lambda a, n: qrecv.at[pl.ds(a, n)])

    def scale_q(i):
        f = fac[pl.ds(i, 1), :]
        j = shard_of(i)
        for g in range(2):
            qpt[j + g * gq] = qpt[j + g * gq] * f[:, g * half_q : (g + 1) * half_q]

    loop(tiles, scale_q)
    loop(n_dp, lambda j: q_put(j, (1 - 2 * cb) * n_dp + j))
    q_chain.begin(0)

    hat[...] = jnp.zeros_like(hat)

    def second(i):
        p = jnp.exp(logits[i] - total_ref[pl.ds(i, 1), :]).astype(BF16)
        hat[...] += mm(p, q_all[i])

    loop(tiles, second)
    q_chain.step(1)

    q_own = q_all[pos, pl.ds(pl.multiple_of(m * quota, quota), quota), :].astype(F32)
    positive = nrm[0:quota, :].astype(F32)
    mine_total = total_ref[pl.ds(pos, 1), :]
    mine_total = jnp.where(m == 0, mine_total[:, :half_q], mine_total[:, half_q:])
    loss_ref[...] = mine_total - scale * jnp.sum((q_own * positive).T, 0, keepdims=True)

    hat[0:quota, :] = hat[0:quota, :] - q_own
    em = emb[...]
    inv = lax.rsqrt(jnp.mean(em * em, -1, keepdims=True) + 1e-06)
    gn = scale * hat[...]
    along = jnp.sum(gn * em, -1, keepdims=True)
    ge[...] = (inv * gn - inv**3 * em * along / e_dim).astype(BF16)

    def back(c):
        for j in range(nj):
            g = nt(ge[...], w2v[c, j * 256 : (j + 1) * 256, :])
            gp[c * nj + j] = jnp.where(pre[c * nj + j] > 0, g, 0.0).astype(BF16)

    loop(2, back)

    half_f = pn.feats // 2
    per_core = n_dp // 2
    n_all = 2 * n_dp

    def place(fb, g, order):
        w = weights_of(order)[("group", 1)]
        return (fb // w) * 2 * w + g * w + fb % w

    def group_of(c):
        return m if c == 0 else other

    def w1_half(cbit, sink):
        for c in range(2):
            for t in range(nj):
                r = mm(featt[pl.ds(pl.multiple_of(cbit * half_f, half_f), half_f), :], gp[c * nj + t])
                for fb in range(per_core):
                    for p, order in enumerate(pn.w_orders):
                        p0, p1 = PART_ROWS[p], PART_ROWS[p + 1]
                        sink(p, place(fb, group_of(c), order), t,
                             r[fb * CH + p0 : fb * CH + p1, :])

    def slot_at(p, slot, n):
        p0, p1 = PART_ROWS[p], PART_ROWS[p + 1]
        pr = (p1 - p0) * nj
        return pl.ds(pl.multiple_of((n_all - 1) * nj * p0 + slot * pr, 16), n * pr)

    def sink_send(p, j, t, v):
        pr = PART_ROWS[p + 1] - PART_ROWS[p]
        at = (n_all - 1) * nj * PART_ROWS[p] + j * (nj * pr) + t * pr
        big[pl.ds(pl.multiple_of(at, 16), pr), :] = v.astype(BF16)

    def sink_acc(p, j, t, v):
        p0, p1 = PART_ROWS[p], PART_ROWS[p + 1]
        logits[j, t * CH + p0 : t * CH + p1, :] = v

    def w_chain(p):
        p0, p1 = PART_ROWS[p], PART_ROWS[p + 1]
        pr = p1 - p0

        def put(slot, a):
            for t in range(nj):
                sink_send(p, slot, t, logits[a, t * CH + p0 : t * CH + p1, :])

        def add(a, slot):
            at = (n_all - 1) * nj * p0 + slot * (nj * pr)
            for t in range(nj):
                cut = slice(t * CH + p0, t * CH + p1)
                logits[a, cut, :] = logits[a, cut, :] + recv[
                    pl.ds(pl.multiple_of(at + t * pr, 16), pr), :].astype(F32)

        return Chain(pn.w_orders[p], put, add,
                     lambda s, n: big.at[slot_at(p, s, n)], lambda s, n: recv.at[slot_at(p, s, n)])

    h2 = 256 // per_core

    def w2_half(cbit, sink):
        for c in range(2):
            r = tn(hid[c * nj + cbit], ge[...])
            for fb in range(per_core):
                sink(place(fb, group_of(c), pn.w2_order), r[fb * h2 : (fb + 1) * h2, :])

    def w2_send(j, v):
        send2[j] = v.astype(BF16)

    def w2_acc(j, v):
        acc2[j] = v

    def w2_put(slot, a):
        send2[slot] = acc2[a].astype(BF16)

    def w2_add(a, slot):
        acc2[a] = acc2[a] + recv2[slot].astype(F32)

    chains = [w_chain(p) for p in range(len(pn.w_orders))]
    w2_chain = Chain(pn.w2_order, w2_put, w2_add,
                     lambda a, n: send2.at[pl.ds(a, n)], lambda a, n: recv2.at[pl.ds(a, n)])
    w1_half(1 - cb, sink_send)
    for ch in chains:
        ch.begin(0)
    w2_half(1 - cb, w2_send)
    w2_chain.begin(0)
    q_chain.step(2)
    w1_half(cb, sink_acc)
    w2_half(cb, w2_acc)
    every = chains + [w2_chain]
    steps = len(pn.w2_order)
    for r in range(1, steps + 1):
        for ch in every:
            ch.step(r)
        if r + 2 <= steps:
            q_chain.step(r + 2)

    q_sum = qpt[own16 + q_chain.base]
    gq_ref[...] = scale * (q_sum.T - positive)

    def block_of(ch):
        w = weights_of(ch.order)[("group", 1)]
        return cb * per_core + lax.div(ch.base, 2 * w) * w + lax.rem(ch.base, w)

    def ag_at(p, fb, n):
        p0, p1 = PART_ROWS[p], PART_ROWS[p + 1]
        pr = (p1 - p0) * nj
        return pl.ds(pl.multiple_of(n_dp * nj * p0 + fb * pr, 16), n * pr)

    views = []
    for p, ch in enumerate(chains):
        p0, p1 = PART_ROWS[p], PART_ROWS[p + 1]
        pr = p1 - p0
        fb = block_of(ch)
        for t in range(nj):
            at = n_dp * nj * p0 + fb * (nj * pr) + t * pr
            ag[pl.ds(pl.multiple_of(at, 16), pr), :] = logits[
                ch.base, t * CH + p0 : t * CH + p1, :].astype(BF16)
        views.append((ch, fb, functools.partial(lambda p, b, n: ag.at[ag_at(p, b, n)], p)))
    fb2 = block_of(w2_chain)
    ag2[fb2] = acc2[w2_chain.base].astype(BF16)
    views.append((w2_chain, fb2, lambda b, n: ag2.at[pl.ds(b, n)]))
    live = [None] * len(views)
    for k in range(len(pn.bits)):
        for i, (ch, fb, view) in enumerate(views):
            if live[i] is not None:
                live[i].wait()
            back_order = [a for a in ch.order if a[0] == "dp"][::-1]
            size = 1 << k
            v = view(lax.div(fb, size) * size, size)
            live[i] = remote(v, v, partner(*back_order[k])[1])
            live[i].start()
    for c in live:
        c.wait()

    for p in range(len(chains)):
        p0, p1 = PART_ROWS[p], PART_ROWS[p + 1]
        pr = p1 - p0

        def out_rows(fb):
            for t in range(nj):
                at = n_dp * nj * p0 + fb * (nj * pr) + t * pr
                gw1_ref[pl.ds(pl.multiple_of(fb * CH + p0, 16), pr), t * 256 : (t + 1) * 256] = ag[
                    pl.ds(pl.multiple_of(at, 16), pr), :].astype(F32)

        loop(n_dp, out_rows)
    gw2_ref[...] = ag2[...].reshape(gw2_ref.shape).astype(F32)


def fused(n_dp, queries, items, corpus, sample_ids, sample_shift, w1, w2):
    pn = Plan(n_dp, queries, items, corpus, w1, w2)
    width, emb = queries.shape
    negs = sample_ids.shape[0] // 2
    rows = pn.quota + negs
    fg, feats, hg = pn.fg, pn.feats, pn.hg
    nj = hg // 256
    n_all = 2 * n_dp
    rounds = n_all.bit_length() - 1
    meta = jnp.concatenate([sample_ids.astype(F32), sample_shift.astype(F32)]).reshape(-1, CH)
    half = feats // 2
    sends = (n_all - 1) * nj * CH
    big = -(-max(sends, (fg // 256) * pn.slab) // 16) * 16
    hp = hg // n_dp
    n_sem = 80
    S = pltpu.VMEM
    loss, gq, gw1, gw2 = pl.pallas_call(
        functools.partial(fused_kernel, pn, rows),
        out_shape=(
            jax.ShapeDtypeStruct((1, pn.quota), F32),
            jax.ShapeDtypeStruct((pn.quota, emb), F32),
            jax.ShapeDtypeStruct((feats, hg), F32),
            jax.ShapeDtypeStruct((hg, emb), F32),
        ),
        in_specs=[ANY] * 6,
        out_specs=(VMEM,) * 4,
        scratch_shapes=[
            S((big, 256), BF16),
            S((n_dp, width, emb), BF16),
            S((2, feats, hg), BF16),
            S((2, hg, emb), BF16),
            S((rows, fg), BF16),
            S((rows, fg), BF16),
            S((negs, fg), BF16),
            S((CH, pn.slab), BF16),
            S(meta.shape, F32),
            S((2 * nj, rows, 256), F32),
            S((2 * nj, rows, 256), BF16),
            S((rows, emb), F32),
            S((rows, emb), BF16),
            S((rows, emb), BF16),
            S((emb, rows), BF16),
            S((rows, width), F32),
            S((rows, emb), F32),
            S((n_dp, rows, width), F32),
            S((n_all, emb, width // 2), F32),
            S((rounds + 1, 2, n_dp, width), F32),
            S((rounds, 2, n_dp, width), F32),
            S((n_dp, width), F32),
            S((n_dp, width), F32),
            S((feats, rows), BF16),
            S((2 * nj, rows, 256), BF16),
            S((rows, emb), BF16),
            S((sends, 256), BF16),
            S((n_dp * nj * CH, 256), BF16),
            S((n_all - 1, emb, width // 2), BF16),
            S((n_all - 1, emb, width // 2), BF16),
            S((n_dp, hp, emb), F32),
            S((n_all - 1, hp, emb), BF16),
            S((n_all - 1, hp, emb), BF16),
            S((n_dp, hp, emb), BF16),
            pltpu.SemaphoreType.DMA((16,)),
            pltpu.SemaphoreType.DMA((n_sem,)),
            pltpu.SemaphoreType.DMA((n_sem,)),
        ],
        compiler_params=pltpu.CompilerParams(
            collective_id=2, has_side_effects=True, vmem_limit_bytes=62 << 20),
        name="fused",
    )(queries, items, corpus, meta, w1, w2)
    return loss.reshape(-1), gq, gw1, gw2


def fits(n_dp, groups, queries, items, corpus, sample_ids, w1, w2):
    negs = sample_ids.shape[0] // groups
    return (
        groups == 2 and n_dp == 16 and queries.shape == (256, 256)
        and negs % CH == 0 and negs >= 2 * CH
        and w1.shape == (n_dp * CH, 512) and w2.shape == (512, 256)
        and items.shape[1] * 2 == w1.shape[0] and corpus.shape[0] % 256 == 0
    )


def per_device(queries, item_features, corpus, sample_ids, sample_shift, w1, w2):
    groups = lax.axis_size("group")
    member = lax.axis_index("group")
    n_dp = lax.axis_size("dp")
    d = lax.axis_index("dp")
    if fits(n_dp, groups, queries, item_features, corpus, sample_ids, w1, w2):
        return fused(n_dp, queries, item_features, corpus, sample_ids, sample_shift, w1, w2)
    query_rows, emb = queries.shape
    quota = query_rows // groups
    negs = sample_ids.shape[0] // groups
    rows = quota + negs
    fg = item_features.shape[1]
    scale = emb ** (-0.5)

    def shift(x, s):
        return lax.ppermute(x, "group", [(i, (i + s) % groups) for i in range(groups)])

    def at(x, i):
        return lax.dynamic_index_in_dim(x, lax.rem(i, groups), 0, keepdims=False)

    def place_columns(parts):
        if groups == 2:
            swap = member == 0
            return jnp.concatenate(
                [jnp.where(swap, parts[0], parts[1]), jnp.where(swap, parts[1], parts[0])], 1)
        out = jnp.zeros((parts[0].shape[0], groups * fg), BF16)
        for s in range(groups):
            start = lax.rem(member + groups - s, groups) * fg
            out = lax.dynamic_update_slice_in_dim(out, parts[s], start, 1)
        return out

    q_all = lax.all_gather(queries, "dp", axis=0, tiled=True)

    def swap_dp(x, step):
        return lax.ppermute(x, "dp", [(i, i ^ step) for i in range(n_dp)])

    def beside(x, cols):
        if x.shape[1] <= cols:
            return jnp.concatenate(jnp.split(x, cols // x.shape[1], 0), 1)
        return jnp.concatenate(jnp.split(x, x.shape[1] // cols, 1), 0)

    def restored(x, cols):
        if cols <= x.shape[1]:
            return jnp.concatenate(jnp.split(x, x.shape[1] // cols, 1), 0)
        return jnp.concatenate(jnp.split(x, cols // x.shape[1], 0), 1)

    quarter = lax.rem(d, 4)
    odd, high = lax.rem(quarter, 2) == 1, quarter >= 2
    w1_rows, w2_rows = w1.shape[0] // 4, w2.shape[0] // 4
    piece = jnp.concatenate([
        lax.dynamic_slice_in_dim(w1, quarter * w1_rows, w1_rows),
        beside(lax.dynamic_slice_in_dim(w2, quarter * w2_rows, w2_rows), w1.shape[1]),
    ], 0)
    items = item_features.reshape(groups, quota, fg)
    sample_ids, piece = lax.optimization_barrier((sample_ids, piece))
    got = [shift(piece, s) for s in range(1, groups)]
    ids = sample_ids.reshape(groups, negs)
    far_rows = [
        corpus.at[at(ids, member + s)].get(mode="promise_in_bounds") for s in range(1, groups)
    ]
    far_rows, items, got = lax.optimization_barrier((far_rows, items, got))
    item_parts = [shift(at(items, member + s), s) for s in range(1, groups)]
    picked_parts = [shift(far_rows[s - 1], s) for s in range(1, groups)]
    own_rows = corpus.at[at(ids, member)].get(mode="promise_in_bounds")
    blocks = [jnp.concatenate([at(items, member), own_rows], 0)]
    for s in range(1, groups):
        blocks.append(jnp.concatenate([at(items, member + s), far_rows[s - 1]], 0))
    local = jnp.stack(blocks[:1] if groups == 2 else blocks)

    w1s, w2s = [w1], [w2]
    for p0 in got:
        p2 = swap_dp(p0, 2)
        p1, p3 = swap_dp(p0, 1), swap_dp(p2, 1)
        low = [jnp.where(odd, p1, p0), jnp.where(odd, p0, p1)]
        upp = [jnp.where(odd, p3, p2), jnp.where(odd, p2, p3)]
        placed = [jnp.where(high, u, l) for u, l in zip(upp, low)]
        placed += [jnp.where(high, l, u) for u, l in zip(upp, low)]
        w1s.append(jnp.concatenate([p[:w1_rows] for p in placed], 0))
        w2s.append(jnp.concatenate([restored(p[w1_rows:], emb) for p in placed], 0))

    feats = place_columns(
        blocks[:1]
        + [jnp.concatenate([a, b], 0) for a, b in zip(item_parts, picked_parts)]
    )

    embedded = jnp.zeros((rows, emb), F32)
    pre_own = None
    for s in range(groups):
        pre = mm(feats, w1s[s])
        hid = jnp.maximum(pre, 0.0).astype(BF16)
        if s == 0:
            pre_own, hid_own = pre, hid
        embedded = embedded + mm(hid, w2s[s])
    inverse = lax.rsqrt(jnp.mean(embedded * embedded, -1, keepdims=True) + 1e-06)
    normed = (embedded * inverse).astype(BF16)
    shift_own = lax.dynamic_slice_in_dim(sample_shift, member * negs, negs).astype(F32)
    bias = jnp.concatenate([jnp.zeros((quota,), F32), -shift_own])

    log_total, grad_hat, query_part, landed = score(
        groups, n_dp, local, q_all, normed, bias[:, None])
    log_total = log_total.reshape(-1)
    rest = place_columns(
        [jnp.concatenate(blocks[1:], 0)] + [landed[s - 1].reshape(-1, fg) for s in range(1, groups)]
    )

    query_own = lax.dynamic_slice_in_dim(queries, member * quota, quota).astype(F32)
    positive_own = normed[:quota].astype(F32)
    positive = scale * jnp.sum(query_own * positive_own, -1)
    query_loss = (
        lax.dynamic_slice_in_dim(log_total, d * query_rows + member * quota, quota) - positive
    )
    target = jnp.concatenate([query_own, jnp.zeros((negs, emb), F32)], 0)
    grad_normed = scale * (grad_hat - target)
    along = jnp.sum(grad_normed * embedded, -1, keepdims=True)
    grad_embed = (
        inverse * grad_normed - inverse**3 * embedded * along / emb
    ).astype(BF16)

    pre_rest = mm(rest, w1)
    hid_rest = jnp.maximum(pre_rest, 0.0).astype(BF16)
    back = jnp.concatenate(
        [grad_embed] + [shift(grad_embed, (groups - t) % groups) for t in range(1, groups)], 0
    )
    mask = jnp.concatenate([pre_own, pre_rest], 0) > 0
    grad_pre = jnp.where(mask, mm(back, w2.T), 0.0).astype(BF16)
    hid_all = jnp.concatenate([hid_own, hid_rest], 0)
    over_rows = (((0,), (0,)), ((), ()))
    grad_w2 = lax.dot_general(hid_all, back, over_rows, preferred_element_type=F32)
    feats_all = jnp.concatenate([feats, rest], 0)
    grad_w1 = lax.dot_general(feats_all, grad_pre, over_rows, preferred_element_type=F32)
    dp_bits = bits_of(n_dp)
    near, far = dp_bits[:1], dp_bits[:1:-1]
    along_first = [("dp", b) for b in near + dp_bits[1:2] + far]
    along_last = [("dp", b) for b in near + far + dp_bits[1:2]]
    query_order = (
        [("dp", near[0])]
        + [("group", b) for b in bits_of(groups)]
        + [("dp", b) for b in dp_bits[1:2] + far]
    )
    pad = -grad_w2.shape[0] % (16 * n_dp)
    padded = jnp.pad(grad_w2, ((0, pad), (0, 0)))
    xs = [
        grad_w1.reshape(2 * n_dp, -1, grad_w1.shape[1]),
        padded.reshape(n_dp, -1, emb),
        query_part.reshape(n_dp * groups, quota, emb),
    ]
    out_a, out_b, out_w2, query_sum = reduce_all(groups, n_dp, xs, [
        (0, 0, n_dp, along_last, True),
        (0, n_dp, n_dp, along_first, True),
        (1, 0, n_dp, along_first, True),
        (2, 0, n_dp * groups, query_order, False),
    ])
    grad_query = scale * (query_sum[0] - positive_own)
    grad_w1 = jnp.concatenate([out_a, out_b], 0).reshape(grad_w1.shape).astype(F32)
    grad_w2 = out_w2.reshape(padded.shape)[: grad_w2.shape[0]].astype(F32)
    return (query_loss, grad_query, grad_w1, grad_w2)


def solution(mesh):
    in_specs = (
        P("dp", None),
        P("dp", "group"),
        P("dp", "group"),
        P("dp"),
        P("dp"),
        P(None, "group"),
        P("group", None),
    )
    out_specs = (P(("dp", "group")), P(("dp", "group"), None), P(None, "group"), P("group", None))
    return jax.shard_map(
        per_device, mesh=mesh, in_specs=in_specs, out_specs=out_specs, check_vma=False
    )
```

```python
import functools

import jax
import jax.numpy as jnp
from jax import lax
from jax.experimental import pallas as pl
from jax.experimental.pallas import tpu as pltpu
from jax.sharding import PartitionSpec as P

F32 = jnp.float32
BF16 = jnp.bfloat16
MESH = pl.DeviceIdType.MESH
ANY = pl.BlockSpec(memory_space=pl.ANY)
VMEM = pl.BlockSpec(memory_space=pltpu.VMEM)


def mm(a, b):
    return jnp.dot(a, b, preferred_element_type=F32)


def bits_of(n):
    return [1 << i for i in range(n.bit_length() - 1)]


def partner(axis, step):
    i = lax.axis_index(axis)
    bit = lax.rem(lax.div(i, step), 2)
    return bit, {axis: i + step - 2 * step * bit}


def greet(peers):
    barrier = pltpu.get_barrier_semaphore()
    for peer in peers:
        pl.semaphore_signal(barrier, inc=1, device_id=peer, device_id_type=MESH)
    pl.semaphore_wait(barrier, len(peers))


def score_kernel(groups, n_dp, local, queries_in, normed, normed_t, bias,
                 total_ref, hat_ref, part_ref, rest_ref,
                 queries, logits, stats, arrived, qsem, send_sem, recv_sem, fsend, frecv):
    tiles, cols, width = logits.shape
    emb = normed.shape[1]
    scale = emb ** (-0.5)
    member = lax.axis_index("group")
    rounds = [("dp", b) for b in bits_of(n_dp)] + [("group", b) for b in bits_of(groups)]
    peers = [partner(a, b)[1] for a, b in rounds]
    others = [lax.rem(member + s, groups) for s in range(1, groups)]
    extra = [{"group": o} for o in others] if groups > 2 else []
    fetch = pltpu.make_async_copy(queries_in, queries, qsem)
    fetch.start()
    greet(peers + extra)
    copies = []
    for s in range(1, groups):
        for t in range(1, groups):
            k = (s - 1) * (groups - 1) + t - 1
            copy = pltpu.make_async_remote_copy(
                src_ref=local.at[(s + t) % groups],
                dst_ref=rest_ref.at[s - 1, t - 1],
                send_sem=fsend.at[k], recv_sem=frecv.at[k],
                device_id={"group": others[s - 1]}, device_id_type=MESH)
            copy.start()
            copies.append(copy)

    def first(i, carry):
        q = queries[pl.ds(pl.multiple_of(i * width, width), width), :]
        block = scale * lax.dot_general(
            normed[...], q, (((1,), (1,)), ((), ())), preferred_element_type=F32) + bias[...]
        logits[i] = block
        top = jnp.max(block, 0, keepdims=True)
        stats[0, 0, pl.ds(i, 1), :] = top
        stats[0, 1, pl.ds(i, 1), :] = jnp.sum(jnp.exp(block - top), 0, keepdims=True)
        return carry

    fetch.wait()
    lax.fori_loop(0, tiles, first, 0)
    for r, peer in enumerate(peers):
        copy = pltpu.make_async_remote_copy(
            src_ref=stats.at[r], dst_ref=arrived.at[r],
            send_sem=send_sem.at[r], recv_sem=recv_sem.at[r],
            device_id=peer, device_id_type=MESH)
        copy.start()
        copy.wait()
        m0, s0, m1, s1 = stats[r, 0], stats[r, 1], arrived[r, 0], arrived[r, 1]
        top = jnp.maximum(m0, m1)
        stats[r + 1, 0] = top
        stats[r + 1, 1] = s0 * jnp.exp(m0 - top) + s1 * jnp.exp(m1 - top)
    last = len(peers)
    total_ref[...] = stats[last, 0] + jnp.log(stats[last, 1])
    hat_ref[...] = jnp.zeros_like(hat_ref)

    def second(i, carry):
        at_i = pl.ds(pl.multiple_of(i * width, width), width)
        p = jnp.exp(logits[i] - total_ref[pl.ds(i, 1), :]).astype(BF16)
        hat_ref[...] += mm(p, queries[at_i, :])
        part_ref[at_i, :] = mm(normed_t[...], p).T
        return carry

    lax.fori_loop(0, tiles, second, 0)
    for copy in copies:
        copy.wait()


def score(groups, n_dp, local, queries, normed, bias):
    rows, fg = local.shape[1:]
    width = 256
    total, emb = queries.shape
    tiles = total // width
    rounds = len(bits_of(n_dp)) + len(bits_of(groups))
    n_copies = (groups - 1) ** 2
    return pl.pallas_call(
        functools.partial(score_kernel, groups, n_dp),
        out_shape=(
            jax.ShapeDtypeStruct((tiles, width), F32),
            jax.ShapeDtypeStruct((rows, emb), F32),
            jax.ShapeDtypeStruct((total, emb), F32),
            jax.ShapeDtypeStruct((groups - 1, groups - 1, rows, fg), BF16),
        ),
        in_specs=[ANY, ANY, VMEM, VMEM, VMEM],
        out_specs=(VMEM, VMEM, VMEM, ANY),
        scratch_shapes=[
            pltpu.VMEM((total, emb), BF16),
            pltpu.VMEM((tiles, rows, width), F32),
            pltpu.VMEM((rounds + 1, 2, tiles, width), F32),
            pltpu.VMEM((rounds, 2, tiles, width), F32),
            pltpu.SemaphoreType.DMA,
            pltpu.SemaphoreType.DMA((rounds,)),
            pltpu.SemaphoreType.DMA((rounds,)),
            pltpu.SemaphoreType.DMA((n_copies,)),
            pltpu.SemaphoreType.DMA((n_copies,)),
        ],
        compiler_params=pltpu.CompilerParams(
            collective_id=0, has_side_effects=True, vmem_limit_bytes=44 << 20),
        name="score",
    )(local, queries, normed, normed.T, bias)


def reduce_kernel(plans, n_in, n_peers_of, *refs):
    n = len(plans)
    ins, refs = refs[:n_in], refs[n_in:]
    outs = refs[:n]
    accs, sends, recvs = (refs[n + i * n : 2 * n + i * n] for i in range(3))
    send_sem, recv_sem, gsend, grecv = refs[4 * n :]
    greet([partner(a, b)[1] for a, b in n_peers_of])
    live = {}

    def begin(i, r):
        rounds, bases, _, source, start, count = plans[i]
        bit, peer = partner(*rounds[r])
        half = count >> (r + 1)
        at0 = count - 2 * half

        def stage(j, carry):
            if r == 0:
                block = ins[source][start + bases(j) + (1 - bit) * bases(half)]
            else:
                block = accs[i][(1 - bit) * half + j]
            sends[i][at0 + j] = block.astype(BF16)
            return carry

        lax.fori_loop(0, half, stage, 0)
        copy = pltpu.make_async_remote_copy(
            src_ref=sends[i].at[pl.ds(at0, half)], dst_ref=recvs[i].at[pl.ds(at0, half)],
            send_sem=send_sem.at[i, r], recv_sem=recv_sem.at[i, r],
            device_id=peer, device_id_type=MESH)
        copy.start()
        live[i] = copy

    def finish(i, r):
        rounds, bases, _, source, start, count = plans[i]
        bit, _ = partner(*rounds[r])
        half = count >> (r + 1)
        at0 = count - 2 * half
        live[i].wait()

        def add(j, carry):
            if r == 0:
                block = ins[source][start + bases(j) + bit * bases(half)]
            else:
                block = accs[i][bit * half + j]
            accs[i][j] = block + recvs[i][at0 + j].astype(F32)
            return carry

        lax.fori_loop(0, half, add, 0)

    def place(i, r):
        rounds = plans[i][0]
        return sum(partner(*rounds[k])[0] * (plans[i][5] >> (k + 1)) for k in range(r + 1))

    def share(i, r):
        peer = partner(*plans[i][0][r])[1]
        span = pl.ds(place(i, r), plans[i][5] >> (r + 1))
        copy = pltpu.make_async_remote_copy(
            src_ref=outs[i].at[span], dst_ref=outs[i].at[span],
            send_sem=gsend.at[i, r], recv_sem=grecv.at[i, r],
            device_id=peer, device_id_type=MESH)
        copy.start()
        live[i] = copy

    def advance(i, step):
        rounds, _, gather = plans[i][:3]
        k = len(rounds)
        if 0 < step <= k:
            finish(i, step - 1)
        if step < k:
            begin(i, step)
        elif step == k and not gather:
            outs[i][0] = accs[i][0]
        elif gather and step <= 2 * k:
            if step == k:
                outs[i][place(i, k - 1)] = accs[i][0].astype(BF16)
            else:
                live[i].wait()
            if step < 2 * k:
                share(i, 2 * k - 1 - step)

    steps = max(len(p[0]) * (2 if p[2] else 1) for p in plans) + 1
    for step in range(steps):
        for i in range(n):
            advance(i, step)


def bit_place(steps, j):
    k = len(steps)
    out = 0
    for i, step in enumerate(steps):
        weight = 1 << (k - 1 - i)
        if isinstance(j, int):
            out += (j // weight) % 2 * step
        else:
            out = out + lax.rem(lax.div(j, weight), 2) * step
    return out


def reduce_all(groups, n_dp, xs, parts):
    plans = []
    for source, start, n, rounds, gather in parts:
        if gather:
            steps = [n >> (k + 1) for k in range(len(rounds))]
        else:
            steps = [b * groups if a == "dp" else b for a, b in rounds]
        bases = functools.partial(bit_place, steps)
        plans.append((rounds, bases, gather, source, start, n))
    shapes = [(p[5],) + xs[p[3]].shape[1:] for p in plans]
    most = max(len(p[0]) for p in plans)
    peers = [("dp", b) for b in bits_of(n_dp)] + [("group", b) for b in bits_of(groups)]
    sems = pltpu.SemaphoreType.DMA((len(plans), most))
    return pl.pallas_call(
        functools.partial(reduce_kernel, plans, len(xs), peers),
        out_shape=tuple(
            jax.ShapeDtypeStruct(shape, BF16) if p[2] else jax.ShapeDtypeStruct((1,) + shape[1:], F32)
            for shape, p in zip(shapes, plans)),
        in_specs=[VMEM] * len(xs),
        out_specs=(VMEM,) * len(plans),
        scratch_shapes=[pltpu.VMEM((s[0] // 2,) + s[1:], F32) for s in shapes]
        + [pltpu.VMEM(s, BF16) for s in shapes] * 2 + [sems] * 4,
        compiler_params=pltpu.CompilerParams(
            collective_id=1, has_side_effects=True, vmem_limit_bytes=48 << 20),
        name="reduce_all",
    )(*xs)


def nt(a, b):
    return lax.dot_general(a, b, (((1,), (1,)), ((), ())), preferred_element_type=F32)


def tn(a, b):
    return lax.dot_general(a, b, (((0,), (0,)), ((), ())), preferred_element_type=F32)


def loop(n, body):
    def step(i, carry):
        body(i)
        return carry

    lax.fori_loop(0, n, step, 0)


def weights_of(order):
    return {axis_step: 1 << (len(order) - 1 - k) for k, axis_step in enumerate(order)}


class Plan:
    def __init__(self, n_dp, queries, items, corpus, w1, w2):
        self.n_dp = n_dp
        self.query_rows, self.emb = queries.shape
        self.quota = self.query_rows // 2
        self.fg = items.shape[1]
        self.slab = corpus.shape[0]
        self.feats, self.hg = w1.shape
        bits = bits_of(n_dp)
        core, x, z = bits[0], bits[1], bits[2:]
        dp = lambda steps: [("dp", s) for s in steps]
        y = [("group", 1)]
        self.gather_orders = [[x] + z[::-1] + [core], z[::-1] + [x, core]]
        self.w_gather = [z[0], x, core]
        self.q_order = dp([core, x]) + y + dp(z)
        self.w_orders = [
            dp([core]) + y + dp([x]) + dp(z),
            dp([core, x]) + y + dp(z),
            dp([core]) + dp(z) + dp([x]) + y,
        ]
        self.w2_order = self.w_orders[1]
        self.bits = bits


PART_ROWS = (0, 48, 96, 128)
ROW_PARTS = (0, 384, 512, 640)
CH = 128


def fused_kernel(pn, rows, queries, items, corpus, ids_in, shift_in, w1, w2,
                 loss_ref, gq_ref, gw1_ref, gw2_ref,
                 big, q_all, w1v, w2v, mine, peer, far, hot, ids_v, shift_v, pre, hid, emb, nrm, nrms, nrm_t,
                 bias, hat, logits, qpt, stats, arrived, total_ref, fac, featt, gp, ge,
                 recv, ag, qsend, qrecv, acc2, send2, recv2, ag2, lsem, ssem, rsem):
    n_dp, width, fg, hg, slab = pn.n_dp, pn.query_rows, pn.fg, pn.hg, pn.slab
    quota, e_dim = pn.quota, pn.emb
    negs = rows - quota
    chunks = negs // CH
    scale = e_dim ** (-0.5)
    m = lax.axis_index("group")
    d = lax.axis_index("dp")
    other = 1 - m
    ypeer = partner("group", 1)[1]
    core, xbit = pn.bits[0], pn.bits[1]
    rounds = [("dp", s) for s in pn.bits] + [("group", 1)]
    count = iter(range(1000))
    lcount = iter(range(100))

    def bit(step):
        return lax.rem(lax.div(d, step), 2)

    def remote(src, dst, to, k=None):
        k = next(count) if k is None else k
        return pltpu.make_async_remote_copy(
            src_ref=src, dst_ref=dst, send_sem=ssem.at[k], recv_sem=rsem.at[k],
            device_id=to, device_id_type=MESH)

    def local(src, dst):
        copy = pltpu.make_async_copy(src, dst, lsem.at[next(lcount)])
        copy.start()
        return copy

    gws = [{s: 1 << k for k, s in enumerate(order)} for order in pn.gather_orders]
    poss = [sum(bit(s) * gw[s] for s in pn.bits) for gw in gws]
    tiles = n_dp

    c_q = [local(queries.at[g * quota : (g + 1) * quota], q_all.at[g, poss[g]]) for g in range(2)]
    c_meta = [local(ids_in, ids_v), local(shift_in, shift_v)]
    c_slab = [local(corpus.at[:, n * 256 : (n + 1) * 256], big.at[n * slab : (n + 1) * slab])
              for n in range(fg // 256)]
    c_mine = local(items.at[pl.ds(pl.multiple_of(m * quota, quota), quota)], mine.at[0:quota])
    c_w1 = local(w1, w1v.at[0])
    c_w2 = local(w2, w2v.at[0])
    greet([partner(a, b)[1] for a, b in rounds])

    class Spread:
        def __init__(self, first, follow, n):
            self.follow, self.n, self.k = follow, n, 0
            self.live = first
            for c in first:
                c.start()

        def go(self):
            for c in self.live:
                c.wait()
            self.live = []
            if self.k < self.n:
                self.live = self.follow(self.k)
                for c in self.live:
                    c.start()
                self.k += 1

    n_piece = 1 << len(pn.w_gather)
    e = sum(bit(s) << k for k, s in enumerate(pn.w_gather))
    q1, q2 = fg // n_piece, hg // 2 // n_piece

    def w_rows(half, size):
        base = lax.div(e, size) * size
        return (pl.ds(pl.multiple_of(half * fg + base * q1, q1), size * q1),
                pl.ds(pl.multiple_of(half * (hg // 2) + base * q2, q2), size * q2))

    def w_spread(half, far_half):
        a, b = w_rows(far_half, 1)

        def follow(k):
            at1, at2 = w_rows(half, 1 << k)
            to = partner("dp", pn.w_gather[k])[1]
            return [remote(w1v.at[1, at1], w1v.at[1, at1], to),
                    remote(w2v.at[1, at2], w2v.at[1, at2], to)]

        return Spread([remote(w1.at[a], w1v.at[1, a], ypeer), remote(w2.at[b], w2v.at[1, b], ypeer)],
                      follow, len(pn.w_gather))

    def q_spread(g):
        def follow(k):
            view = q_all.at[g, pl.ds(lax.div(poss[g], 1 << k) * (1 << k), 1 << k)]
            return [remote(view, view, partner("dp", pn.gather_orders[g][k])[1])]

        return Spread(follow(0), lambda k: follow(k + 1), len(pn.bits) - 1)

    ws = [w_spread(m, other), w_spread(other, m)]
    for c in c_q:
        c.wait()
    qs = [q_spread(0), q_spread(1)]
    item_send = remote(items.at[pl.ds(pl.multiple_of(other * quota, quota), quota)],
                       peer.at[0:quota], ypeer)
    k_far = [next(count) for _ in range(chunks)][0]

    def rows_at(k):
        return pl.ds(pl.multiple_of(quota + k * CH, CH), CH)

    def far_copy(k):
        return remote(far.at[pl.ds(pl.multiple_of(k * CH, CH), CH)], peer.at[rows_at(k)],
                      ypeer, k_far + k)

    def column(ref, r):
        return jnp.broadcast_to(ref[pl.ds(r, 1), :].astype(F32), (8, CH)).T[:, :1]

    def pick(who, k, dst, at):
        ids = column(ids_v, who * chunks + k)
        where = lax.broadcasted_iota(jnp.int32, (CH, slab), 1).astype(F32)
        hot[...] = jnp.where(ids == where, 1.0, 0.0).astype(BF16)
        for n in range(fg // 256):
            dst[at, n * 256 : (n + 1) * 256] = mm(
                hot[...], big[n * slab : (n + 1) * slab, :]).astype(BF16)

    for c in c_meta + c_slab:
        c.wait()
    loop(chunks, lambda k: pick(other, k, far, pl.ds(pl.multiple_of(k * CH, CH), CH)))
    qs[0].go()
    qs[1].go()
    ws[0].go()
    ws[1].go()
    item_send.start()
    loop(chunks, lambda k: far_copy(k).start())
    loop(chunks, lambda k: pick(m, k, mine, rows_at(k)))
    qs[1].go()
    ws[0].go()
    qs[0].go()
    bias[0:quota, :] = jnp.zeros((quota, width), F32)

    def put_bias(k):
        bias[rows_at(k), :] = jnp.broadcast_to(
            -column(shift_v, m * chunks + k), (CH, width))

    loop(chunks, put_bias)
    c_mine.wait()
    c_w1.wait()
    c_w2.wait()
    ws[1].go()

    nj = hg // 256

    def tower_add(r0, r1, feat, half, c, first):
        for j in range(nj):
            part = mm(feat[r0:r1, :], w1v[c, pl.ds(pl.multiple_of(half * fg, fg), fg),
                                         j * 256 : (j + 1) * 256])
            if first:
                pre[c * nj + j, r0:r1, :] = part
            else:
                pre[c * nj + j, r0:r1, :] += part

    tower_add(0, rows, mine, m, 0, True)
    qs[1].go()
    qs[0].go()

    def turn(src, half, n):
        at = pl.multiple_of(n * 256, 256)
        featt[pl.ds(pl.multiple_of(half * fg + at, 256), 256), :] = src[:, pl.ds(at, 256)].T

    ws[0].go()
    loop(fg // 256, lambda n: turn(mine, m, n))
    ws[1].go()
    ws[0].go()
    tower_add(0, rows, mine, m, 1, True)
    ws[1].go()

    def finish_tower(r0, r1):
        loop(2, lambda c: tower_add(r0, r1, peer, other, c, False))
        emb[r0:r1, :] = jnp.zeros((r1 - r0, e_dim), F32)

        def second_layer(c):
            for j in range(nj):
                h = jnp.maximum(pre[c * nj + j, r0:r1, :], 0.0).astype(BF16)
                hid[c * nj + j, r0:r1, :] = h
                emb[r0:r1, :] += mm(h, w2v[c, j * 256 : (j + 1) * 256, :])

        loop(2, second_layer)
        em = emb[r0:r1, :]
        inv = lax.rsqrt(jnp.mean(em * em, -1, keepdims=True) + 1e-06)
        no = (em * inv).astype(BF16)
        nrm[r0:r1, :] = no
        nrms[r0:r1, :] = (no.astype(F32) * scale).astype(BF16)
        nrm_t[:, r0:r1] = no.astype(F32).T.astype(BF16)

    oq = weights_of(pn.q_order)
    gq = oq[("group", 1)]

    def shard_of(i, g):
        return g * gq + sum(
            lax.rem(lax.div(i, gws[g][s]), 2) * oq[("dp", s)] for s in pn.bits)

    half_q = width // 2

    def queries_at(i):
        return jnp.concatenate([q_all[0, i], q_all[1, i]], 0)

    def score(r0, r1):
        def one(i):
            block = nt(nrms[r0:r1, :], queries_at(i)) + bias[r0:r1, :]
            logits[i, r0:r1, :] = block
            top = jnp.max(block, 0, keepdims=True)
            at = pl.ds(i, 1)
            if r0 == 0:
                stats[0, 1, at, :] = jnp.sum(jnp.exp(block - top), 0, keepdims=True)
            else:
                before = stats[0, 0, at, :]
                top = jnp.maximum(before, top)
                stats[0, 1, at, :] = stats[0, 1, at, :] * jnp.exp(before - top) + jnp.sum(
                    jnp.exp(block - top), 0, keepdims=True)
            stats[0, 0, at, :] = top

        loop(tiles, one)

    item_send.wait()
    done = 0
    for r0, r1 in zip(ROW_PARTS[:-1], ROW_PARTS[1:]):
        upto = (r1 - quota) // CH
        for k in range(done, upto):
            far_copy(k).wait()
        done = upto
        finish_tower(r0, r1)
        if r0 == 0:
            qs[0].go()
            qs[1].go()
        score(r0, r1)

    def query_part(i):
        p = jnp.exp(logits[i] - stats[0, 0, pl.ds(i, 1), :])
        part = mm(nrm_t[...], p.astype(BF16))
        for g in range(2):
            qpt[shard_of(i, g)] = part[:, g * half_q : (g + 1) * half_q]

    for r, (axis, step) in enumerate(rounds):
        copy = remote(stats.at[r], arrived.at[r], partner(axis, step)[1])
        copy.start()
        if r < 4:
            loop(tiles // 4, lambda i: query_part(r * (tiles // 4) + i))
        else:
            loop(fg // 256, lambda n: turn(peer, other, n))
        copy.wait()
        m0, s0, m1, s1 = stats[r, 0], stats[r, 1], arrived[r, 0], arrived[r, 1]
        top = jnp.maximum(m0, m1)
        stats[r + 1, 0] = top
        stats[r + 1, 1] = s0 * jnp.exp(m0 - top) + s1 * jnp.exp(m1 - top)
    last = len(rounds)
    total_ref[...] = stats[last, 0] + jnp.log(stats[last, 1])
    fac[...] = jnp.exp(stats[0, 0] - total_ref[...])

    class Chain:
        def __init__(self, order, put, add, send_at, recv_at):
            self.order, self.put, self.add = order, put, add
            self.send_at, self.recv_at = send_at, recv_at
            self.n = 1 << len(order)
            self.base = 0

        def begin(self, r):
            half = self.n >> (r + 1)
            at0 = self.n - 2 * half
            b, to = partner(*self.order[r])
            if r > 0:
                base = self.base
                loop(half, lambda j: self.put(at0 + j, base + (1 - b) * half + j))
            self.copy = remote(self.send_at(at0, half), self.recv_at(at0, half), to)
            self.copy.start()

        def finish(self, r):
            half = self.n >> (r + 1)
            at0 = self.n - 2 * half
            b, _ = partner(*self.order[r])
            self.copy.wait()
            if r > 0:
                self.base = self.base + b * half
            base = self.base
            loop(half, lambda j: self.add(base + j, at0 + j))

        def step(self, r):
            if r > 0:
                self.finish(r - 1)
            if r < len(self.order):
                self.begin(r)

    cb = bit(core)
    own16 = cb * n_dp

    def q_put(slot, a):
        qsend[slot] = qpt[own16 + a].astype(BF16)

    def q_add(a, slot):
        qpt[own16 + a] = qpt[own16 + a] + qrecv[slot].astype(F32)

    q_chain = Chain(pn.q_order, q_put, q_add,
                    lambda a, n: qsend.at[pl.ds(a, n)], lambda a, n: qrecv.at[pl.ds(a, n)])

    def scale_q(i):
        f = fac[pl.ds(i, 1), :]
        for g in range(2):
            j = shard_of(i, g)
            qpt[j] = qpt[j] * f[:, g * half_q : (g + 1) * half_q]

    loop(tiles, scale_q)
    loop(n_dp, lambda j: q_put(j, (1 - 2 * cb) * n_dp + j))
    q_chain.begin(0)

    hat[...] = jnp.zeros_like(hat)

    def second(i):
        p = jnp.exp(logits[i] - total_ref[pl.ds(i, 1), :]).astype(BF16)
        hat[...] += mm(p, queries_at(i))

    loop(tiles // 2, second)
    q_chain.step(1)
    loop(tiles // 2, lambda i: second(tiles // 2 + i))

    pos = jnp.where(m == 0, poss[0], poss[1])
    q_own = q_all[m, pos].astype(F32)
    positive = nrm[0:quota, :].astype(F32)
    mine_total = total_ref[pl.ds(pos, 1), :]
    mine_total = jnp.where(m == 0, mine_total[:, :half_q], mine_total[:, half_q:])
    loss_ref[...] = mine_total - scale * jnp.sum((q_own * positive).T, 0, keepdims=True)

    hat[0:quota, :] = hat[0:quota, :] - q_own
    em = emb[...]
    inv = lax.rsqrt(jnp.mean(em * em, -1, keepdims=True) + 1e-06)
    gn = scale * hat[...]
    along = jnp.sum(gn * em, -1, keepdims=True)
    ge[...] = (inv * gn - inv**3 * em * along / e_dim).astype(BF16)

    def back(c):
        for j in range(nj):
            g = nt(ge[...], w2v[c, j * 256 : (j + 1) * 256, :])
            gp[c * nj + j] = jnp.where(pre[c * nj + j] > 0, g, 0.0).astype(BF16)

    loop(2, back)

    half_f = pn.feats // 2
    per_core = n_dp // 2
    n_all = 2 * n_dp

    def place(fb, g, order):
        w = weights_of(order)[("group", 1)]
        return (fb // w) * 2 * w + g * w + fb % w

    def group_of(c):
        return m if c == 0 else other

    def w1_half(cbit, sink):
        for c in range(2):
            for t in range(nj):
                r = mm(featt[pl.ds(pl.multiple_of(cbit * half_f, half_f), half_f), :], gp[c * nj + t])
                for fb in range(per_core):
                    for p, order in enumerate(pn.w_orders):
                        p0, p1 = PART_ROWS[p], PART_ROWS[p + 1]
                        sink(p, place(fb, group_of(c), order), t,
                             r[fb * CH + p0 : fb * CH + p1, :])

    def slot_at(p, slot, n):
        p0, p1 = PART_ROWS[p], PART_ROWS[p + 1]
        pr = (p1 - p0) * nj
        return pl.ds(pl.multiple_of((n_all - 1) * nj * p0 + slot * pr, 16), n * pr)

    def sink_send(p, j, t, v):
        pr = PART_ROWS[p + 1] - PART_ROWS[p]
        at = (n_all - 1) * nj * PART_ROWS[p] + j * (nj * pr) + t * pr
        big[pl.ds(pl.multiple_of(at, 16), pr), :] = v.astype(BF16)

    def sink_acc(p, j, t, v):
        p0, p1 = PART_ROWS[p], PART_ROWS[p + 1]
        logits[j, t * CH + p0 : t * CH + p1, :] = v

    def w_chain(p):
        p0, p1 = PART_ROWS[p], PART_ROWS[p + 1]
        pr = p1 - p0

        def put(slot, a):
            for t in range(nj):
                sink_send(p, slot, t, logits[a, t * CH + p0 : t * CH + p1, :])

        def add(a, slot):
            at = (n_all - 1) * nj * p0 + slot * (nj * pr)
            for t in range(nj):
                cut = slice(t * CH + p0, t * CH + p1)
                logits[a, cut, :] = logits[a, cut, :] + recv[
                    pl.ds(pl.multiple_of(at + t * pr, 16), pr), :].astype(F32)

        return Chain(pn.w_orders[p], put, add,
                     lambda s, n: big.at[slot_at(p, s, n)], lambda s, n: recv.at[slot_at(p, s, n)])

    h2 = 256 // per_core

    def w2_half(cbit, sink):
        for c in range(2):
            r = tn(hid[c * nj + cbit], ge[...])
            for fb in range(per_core):
                sink(place(fb, group_of(c), pn.w2_order), r[fb * h2 : (fb + 1) * h2, :])

    def w2_send(j, v):
        send2[j] = v.astype(BF16)

    def w2_acc(j, v):
        acc2[j] = v

    def w2_put(slot, a):
        send2[slot] = acc2[a].astype(BF16)

    def w2_add(a, slot):
        acc2[a] = acc2[a] + recv2[slot].astype(F32)

    chains = [w_chain(p) for p in range(len(pn.w_orders))]
    w2_chain = Chain(pn.w2_order, w2_put, w2_add,
                     lambda a, n: send2.at[pl.ds(a, n)], lambda a, n: recv2.at[pl.ds(a, n)])
    w1_half(1 - cb, sink_send)
    for ch in chains:
        ch.begin(0)
    w2_half(1 - cb, w2_send)
    w2_chain.begin(0)
    w1_half(cb, sink_acc)
    w2_half(cb, w2_acc)
    q_chain.step(2)
    every = chains + [w2_chain]
    steps = len(pn.w2_order)
    for r in range(1, steps + 1):
        for ch in every:
            ch.step(r)
        if r + 2 <= steps:
            q_chain.step(r + 2)

    q_sum = qpt[own16 + q_chain.base]
    gq_ref[...] = scale * (q_sum.T - positive)

    def block_of(ch):
        w = weights_of(ch.order)[("group", 1)]
        return cb * per_core + lax.div(ch.base, 2 * w) * w + lax.rem(ch.base, w)

    def ag_at(p, fb, n):
        p0, p1 = PART_ROWS[p], PART_ROWS[p + 1]
        pr = (p1 - p0) * nj
        return pl.ds(pl.multiple_of(n_dp * nj * p0 + fb * pr, 16), n * pr)

    views = []
    for p, ch in enumerate(chains):
        p0, p1 = PART_ROWS[p], PART_ROWS[p + 1]
        pr = p1 - p0
        fb = block_of(ch)
        for t in range(nj):
            at = n_dp * nj * p0 + fb * (nj * pr) + t * pr
            ag[pl.ds(pl.multiple_of(at, 16), pr), :] = logits[
                ch.base, t * CH + p0 : t * CH + p1, :].astype(BF16)
        views.append((ch, fb, functools.partial(lambda p, b, n: ag.at[ag_at(p, b, n)], p)))
    fb2 = block_of(w2_chain)
    ag2[fb2] = acc2[w2_chain.base].astype(BF16)
    views.append((w2_chain, fb2, lambda b, n: ag2.at[pl.ds(b, n)]))
    live = [None] * len(views)
    for k in range(len(pn.bits)):
        for i, (ch, fb, view) in enumerate(views):
            if live[i] is not None:
                live[i].wait()
            back_order = [a for a in ch.order if a[0] == "dp"][::-1]
            size = 1 << k
            v = view(lax.div(fb, size) * size, size)
            live[i] = remote(v, v, partner(*back_order[k])[1])
            live[i].start()
    for c in live:
        c.wait()

    for p in range(len(chains)):
        p0, p1 = PART_ROWS[p], PART_ROWS[p + 1]
        pr = p1 - p0

        def out_rows(fb):
            for t in range(nj):
                at = n_dp * nj * p0 + fb * (nj * pr) + t * pr
                gw1_ref[pl.ds(pl.multiple_of(fb * CH + p0, 16), pr), t * 256 : (t + 1) * 256] = ag[
                    pl.ds(pl.multiple_of(at, 16), pr), :]

        loop(n_dp, out_rows)
    gw2_ref[...] = ag2[...].reshape(gw2_ref.shape)


def fused(n_dp, queries, items, corpus, sample_ids, sample_shift, w1, w2):
    pn = Plan(n_dp, queries, items, corpus, w1, w2)
    width, emb = queries.shape
    negs = sample_ids.shape[0] // 2
    rows = pn.quota + negs
    fg, feats, hg = pn.fg, pn.feats, pn.hg
    nj = hg // 256
    n_all = 2 * n_dp
    rounds = n_all.bit_length() - 1
    ids = sample_ids.reshape(-1, CH)
    shifts = sample_shift.astype(F32).reshape(-1, CH)
    half = feats // 2
    sends = (n_all - 1) * nj * CH
    big = -(-max(sends, (fg // 256) * pn.slab) // 16) * 16
    hp = hg // n_dp
    n_sem = 80
    S = pltpu.VMEM
    loss, gq, gw1, gw2 = pl.pallas_call(
        functools.partial(fused_kernel, pn, rows),
        out_shape=(
            jax.ShapeDtypeStruct((1, pn.quota), F32),
            jax.ShapeDtypeStruct((pn.quota, emb), F32),
            jax.ShapeDtypeStruct((feats, hg), BF16),
            jax.ShapeDtypeStruct((hg, emb), BF16),
        ),
        in_specs=[ANY] * 7,
        out_specs=(VMEM,) * 4,
        scratch_shapes=[
            S((big, 256), BF16),
            S((2, n_dp, width // 2, emb), BF16),
            S((2, feats, hg), BF16),
            S((2, hg, emb), BF16),
            S((rows, fg), BF16),
            S((rows, fg), BF16),
            S((negs, fg), BF16),
            S((CH, pn.slab), BF16),
            S(ids.shape, jnp.int32),
            S(shifts.shape, F32),
            S((2 * nj, rows, 256), F32),
            S((2 * nj, rows, 256), BF16),
            S((rows, emb), F32),
            S((rows, emb), BF16),
            S((rows, emb), BF16),
            S((emb, rows), BF16),
            S((rows, width), F32),
            S((rows, emb), F32),
            S((n_dp, rows, width), F32),
            S((n_all, emb, width // 2), F32),
            S((rounds + 1, 2, n_dp, width), F32),
            S((rounds, 2, n_dp, width), F32),
            S((n_dp, width), F32),
            S((n_dp, width), F32),
            S((feats, rows), BF16),
            S((2 * nj, rows, 256), BF16),
            S((rows, emb), BF16),
            S((sends, 256), BF16),
            S((n_dp * nj * CH, 256), BF16),
            S((n_all - 1, emb, width // 2), BF16),
            S((n_all - 1, emb, width // 2), BF16),
            S((n_dp, hp, emb), F32),
            S((n_all - 1, hp, emb), BF16),
            S((n_all - 1, hp, emb), BF16),
            S((n_dp, hp, emb), BF16),
            pltpu.SemaphoreType.DMA((16,)),
            pltpu.SemaphoreType.DMA((n_sem,)),
            pltpu.SemaphoreType.DMA((n_sem,)),
        ],
        compiler_params=pltpu.CompilerParams(
            collective_id=2, has_side_effects=True, vmem_limit_bytes=62 << 20),
        name="fused",
    )(queries, items, corpus, ids, shifts, w1, w2)
    return widen(loss, gq, gw1, gw2)


def widen_kernel(*refs):
    n = len(refs) // 2
    for a, b in zip(refs[:n], refs[n:]):
        b[...] = a[...].astype(F32)


def widen(loss, *grads):
    parts = 4
    specs = [pl.BlockSpec(loss.shape, lambda i: (0, 0))] + [
        pl.BlockSpec((x.shape[0] // parts, x.shape[1]), lambda i: (i, 0)) for x in grads]
    loss, *grads = pl.pallas_call(
        widen_kernel,
        grid=(parts,),
        out_shape=tuple(jax.ShapeDtypeStruct(x.shape, F32) for x in (loss, *grads)),
        in_specs=specs,
        out_specs=tuple(specs),
        name="widen",
    )(loss, *grads)
    return (loss.reshape(-1), *grads)


def fits(n_dp, groups, queries, items, corpus, sample_ids, w1, w2):
    negs = sample_ids.shape[0] // groups
    return (
        groups == 2 and n_dp == 16 and queries.shape == (256, 256)
        and (256 // groups + negs) == ROW_PARTS[-1]
        and w1.shape == (n_dp * CH, 512) and w2.shape == (512, 256)
        and items.shape[1] * 2 == w1.shape[0] and corpus.shape[0] % 256 == 0
    )


def per_device(queries, item_features, corpus, sample_ids, sample_shift, w1, w2):
    groups = lax.axis_size("group")
    member = lax.axis_index("group")
    n_dp = lax.axis_size("dp")
    d = lax.axis_index("dp")
    if fits(n_dp, groups, queries, item_features, corpus, sample_ids, w1, w2):
        return fused(n_dp, queries, item_features, corpus, sample_ids, sample_shift, w1, w2)
    query_rows, emb = queries.shape
    quota = query_rows // groups
    negs = sample_ids.shape[0] // groups
    rows = quota + negs
    fg = item_features.shape[1]
    scale = emb ** (-0.5)

    def shift(x, s):
        return lax.ppermute(x, "group", [(i, (i + s) % groups) for i in range(groups)])

    def at(x, i):
        return lax.dynamic_index_in_dim(x, lax.rem(i, groups), 0, keepdims=False)

    def place_columns(parts):
        if groups == 2:
            swap = member == 0
            return jnp.concatenate(
                [jnp.where(swap, parts[0], parts[1]), jnp.where(swap, parts[1], parts[0])], 1)
        out = jnp.zeros((parts[0].shape[0], groups * fg), BF16)
        for s in range(groups):
            start = lax.rem(member + groups - s, groups) * fg
            out = lax.dynamic_update_slice_in_dim(out, parts[s], start, 1)
        return out

    q_all = lax.all_gather(queries, "dp", axis=0, tiled=True)

    def swap_dp(x, step):
        return lax.ppermute(x, "dp", [(i, i ^ step) for i in range(n_dp)])

    def beside(x, cols):
        if x.shape[1] <= cols:
            return jnp.concatenate(jnp.split(x, cols // x.shape[1], 0), 1)
        return jnp.concatenate(jnp.split(x, x.shape[1] // cols, 1), 0)

    def restored(x, cols):
        if cols <= x.shape[1]:
            return jnp.concatenate(jnp.split(x, x.shape[1] // cols, 1), 0)
        return jnp.concatenate(jnp.split(x, cols // x.shape[1], 0), 1)

    quarter = lax.rem(d, 4)
    odd, high = lax.rem(quarter, 2) == 1, quarter >= 2
    w1_rows, w2_rows = w1.shape[0] // 4, w2.shape[0] // 4
    piece = jnp.concatenate([
        lax.dynamic_slice_in_dim(w1, quarter * w1_rows, w1_rows),
        beside(lax.dynamic_slice_in_dim(w2, quarter * w2_rows, w2_rows), w1.shape[1]),
    ], 0)
    items = item_features.reshape(groups, quota, fg)
    sample_ids, piece = lax.optimization_barrier((sample_ids, piece))
    got = [shift(piece, s) for s in range(1, groups)]
    ids = sample_ids.reshape(groups, negs)
    far_rows = [
        corpus.at[at(ids, member + s)].get(mode="promise_in_bounds") for s in range(1, groups)
    ]
    far_rows, items, got = lax.optimization_barrier((far_rows, items, got))
    item_parts = [shift(at(items, member + s), s) for s in range(1, groups)]
    picked_parts = [shift(far_rows[s - 1], s) for s in range(1, groups)]
    own_rows = corpus.at[at(ids, member)].get(mode="promise_in_bounds")
    blocks = [jnp.concatenate([at(items, member), own_rows], 0)]
    for s in range(1, groups):
        blocks.append(jnp.concatenate([at(items, member + s), far_rows[s - 1]], 0))
    local = jnp.stack(blocks[:1] if groups == 2 else blocks)

    w1s, w2s = [w1], [w2]
    for p0 in got:
        p2 = swap_dp(p0, 2)
        p1, p3 = swap_dp(p0, 1), swap_dp(p2, 1)
        low = [jnp.where(odd, p1, p0), jnp.where(odd, p0, p1)]
        upp = [jnp.where(odd, p3, p2), jnp.where(odd, p2, p3)]
        placed = [jnp.where(high, u, l) for u, l in zip(upp, low)]
        placed += [jnp.where(high, l, u) for u, l in zip(upp, low)]
        w1s.append(jnp.concatenate([p[:w1_rows] for p in placed], 0))
        w2s.append(jnp.concatenate([restored(p[w1_rows:], emb) for p in placed], 0))

    feats = place_columns(
        blocks[:1]
        + [jnp.concatenate([a, b], 0) for a, b in zip(item_parts, picked_parts)]
    )

    embedded = jnp.zeros((rows, emb), F32)
    pre_own = None
    for s in range(groups):
        pre = mm(feats, w1s[s])
        hid = jnp.maximum(pre, 0.0).astype(BF16)
        if s == 0:
            pre_own, hid_own = pre, hid
        embedded = embedded + mm(hid, w2s[s])
    inverse = lax.rsqrt(jnp.mean(embedded * embedded, -1, keepdims=True) + 1e-06)
    normed = (embedded * inverse).astype(BF16)
    shift_own = lax.dynamic_slice_in_dim(sample_shift, member * negs, negs).astype(F32)
    bias = jnp.concatenate([jnp.zeros((quota,), F32), -shift_own])

    log_total, grad_hat, query_part, landed = score(
        groups, n_dp, local, q_all, normed, bias[:, None])
    log_total = log_total.reshape(-1)
    rest = place_columns(
        [jnp.concatenate(blocks[1:], 0)] + [landed[s - 1].reshape(-1, fg) for s in range(1, groups)]
    )

    query_own = lax.dynamic_slice_in_dim(queries, member * quota, quota).astype(F32)
    positive_own = normed[:quota].astype(F32)
    positive = scale * jnp.sum(query_own * positive_own, -1)
    query_loss = (
        lax.dynamic_slice_in_dim(log_total, d * query_rows + member * quota, quota) - positive
    )
    target = jnp.concatenate([query_own, jnp.zeros((negs, emb), F32)], 0)
    grad_normed = scale * (grad_hat - target)
    along = jnp.sum(grad_normed * embedded, -1, keepdims=True)
    grad_embed = (
        inverse * grad_normed - inverse**3 * embedded * along / emb
    ).astype(BF16)

    pre_rest = mm(rest, w1)
    hid_rest = jnp.maximum(pre_rest, 0.0).astype(BF16)
    back = jnp.concatenate(
        [grad_embed] + [shift(grad_embed, (groups - t) % groups) for t in range(1, groups)], 0
    )
    mask = jnp.concatenate([pre_own, pre_rest], 0) > 0
    grad_pre = jnp.where(mask, mm(back, w2.T), 0.0).astype(BF16)
    hid_all = jnp.concatenate([hid_own, hid_rest], 0)
    over_rows = (((0,), (0,)), ((), ()))
    grad_w2 = lax.dot_general(hid_all, back, over_rows, preferred_element_type=F32)
    feats_all = jnp.concatenate([feats, rest], 0)
    grad_w1 = lax.dot_general(feats_all, grad_pre, over_rows, preferred_element_type=F32)
    dp_bits = bits_of(n_dp)
    near, far = dp_bits[:1], dp_bits[:1:-1]
    along_first = [("dp", b) for b in near + dp_bits[1:2] + far]
    along_last = [("dp", b) for b in near + far + dp_bits[1:2]]
    query_order = (
        [("dp", near[0])]
        + [("group", b) for b in bits_of(groups)]
        + [("dp", b) for b in dp_bits[1:2] + far]
    )
    pad = -grad_w2.shape[0] % (16 * n_dp)
    padded = jnp.pad(grad_w2, ((0, pad), (0, 0)))
    xs = [
        grad_w1.reshape(2 * n_dp, -1, grad_w1.shape[1]),
        padded.reshape(n_dp, -1, emb),
        query_part.reshape(n_dp * groups, quota, emb),
    ]
    out_a, out_b, out_w2, query_sum = reduce_all(groups, n_dp, xs, [
        (0, 0, n_dp, along_last, True),
        (0, n_dp, n_dp, along_first, True),
        (1, 0, n_dp, along_first, True),
        (2, 0, n_dp * groups, query_order, False),
    ])
    grad_query = scale * (query_sum[0] - positive_own)
    grad_w1 = jnp.concatenate([out_a, out_b], 0).reshape(grad_w1.shape).astype(F32)
    grad_w2 = out_w2.reshape(padded.shape)[: grad_w2.shape[0]].astype(F32)
    return (query_loss, grad_query, grad_w1, grad_w2)


def solution(mesh):
    in_specs = (
        P("dp", None),
        P("dp", "group"),
        P("dp", "group"),
        P("dp"),
        P("dp"),
        P(None, "group"),
        P("group", None),
    )
    out_specs = (P(("dp", "group")), P(("dp", "group"), None), P(None, "group"), P("group", None))
    return jax.shard_map(
        per_device, mesh=mesh, in_specs=in_specs, out_specs=out_specs, check_vma=False
    )
```

```python
import functools

import jax
import jax.numpy as jnp
from jax import lax
from jax.experimental import pallas as pl
from jax.experimental.pallas import tpu as pltpu
from jax.sharding import PartitionSpec as P

F32 = jnp.float32
BF16 = jnp.bfloat16
MESH = pl.DeviceIdType.MESH
ANY = pl.BlockSpec(memory_space=pl.ANY)
VMEM = pl.BlockSpec(memory_space=pltpu.VMEM)


def mm(a, b):
    return jnp.dot(a, b, preferred_element_type=F32)


def bits_of(n):
    return [1 << i for i in range(n.bit_length() - 1)]


def partner(axis, step):
    i = lax.axis_index(axis)
    bit = lax.rem(lax.div(i, step), 2)
    return bit, {axis: i + step - 2 * step * bit}


def greet(peers):
    barrier = pltpu.get_barrier_semaphore()
    for peer in peers:
        pl.semaphore_signal(barrier, inc=1, device_id=peer, device_id_type=MESH)
    pl.semaphore_wait(barrier, len(peers))


def score_kernel(groups, n_dp, local, queries_in, normed, normed_t, bias,
                 total_ref, hat_ref, part_ref, rest_ref,
                 queries, logits, stats, arrived, qsem, send_sem, recv_sem, fsend, frecv):
    tiles, cols, width = logits.shape
    emb = normed.shape[1]
    scale = emb ** (-0.5)
    member = lax.axis_index("group")
    rounds = [("dp", b) for b in bits_of(n_dp)] + [("group", b) for b in bits_of(groups)]
    peers = [partner(a, b)[1] for a, b in rounds]
    others = [lax.rem(member + s, groups) for s in range(1, groups)]
    extra = [{"group": o} for o in others] if groups > 2 else []
    fetch = pltpu.make_async_copy(queries_in, queries, qsem)
    fetch.start()
    greet(peers + extra)
    copies = []
    for s in range(1, groups):
        for t in range(1, groups):
            k = (s - 1) * (groups - 1) + t - 1
            copy = pltpu.make_async_remote_copy(
                src_ref=local.at[(s + t) % groups],
                dst_ref=rest_ref.at[s - 1, t - 1],
                send_sem=fsend.at[k], recv_sem=frecv.at[k],
                device_id={"group": others[s - 1]}, device_id_type=MESH)
            copy.start()
            copies.append(copy)

    def first(i, carry):
        q = queries[pl.ds(pl.multiple_of(i * width, width), width), :]
        block = scale * lax.dot_general(
            normed[...], q, (((1,), (1,)), ((), ())), preferred_element_type=F32) + bias[...]
        logits[i] = block
        top = jnp.max(block, 0, keepdims=True)
        stats[0, 0, pl.ds(i, 1), :] = top
        stats[0, 1, pl.ds(i, 1), :] = jnp.sum(jnp.exp(block - top), 0, keepdims=True)
        return carry

    fetch.wait()
    lax.fori_loop(0, tiles, first, 0)
    for r, peer in enumerate(peers):
        copy = pltpu.make_async_remote_copy(
            src_ref=stats.at[r], dst_ref=arrived.at[r],
            send_sem=send_sem.at[r], recv_sem=recv_sem.at[r],
            device_id=peer, device_id_type=MESH)
        copy.start()
        copy.wait()
        m0, s0, m1, s1 = stats[r, 0], stats[r, 1], arrived[r, 0], arrived[r, 1]
        top = jnp.maximum(m0, m1)
        stats[r + 1, 0] = top
        stats[r + 1, 1] = s0 * jnp.exp(m0 - top) + s1 * jnp.exp(m1 - top)
    last = len(peers)
    total_ref[...] = stats[last, 0] + jnp.log(stats[last, 1])
    hat_ref[...] = jnp.zeros_like(hat_ref)

    def second(i, carry):
        at_i = pl.ds(pl.multiple_of(i * width, width), width)
        p = jnp.exp(logits[i] - total_ref[pl.ds(i, 1), :]).astype(BF16)
        hat_ref[...] += mm(p, queries[at_i, :])
        part_ref[at_i, :] = mm(normed_t[...], p).T
        return carry

    lax.fori_loop(0, tiles, second, 0)
    for copy in copies:
        copy.wait()


def score(groups, n_dp, local, queries, normed, bias):
    rows, fg = local.shape[1:]
    width = 256
    total, emb = queries.shape
    tiles = total // width
    rounds = len(bits_of(n_dp)) + len(bits_of(groups))
    n_copies = (groups - 1) ** 2
    return pl.pallas_call(
        functools.partial(score_kernel, groups, n_dp),
        out_shape=(
            jax.ShapeDtypeStruct((tiles, width), F32),
            jax.ShapeDtypeStruct((rows, emb), F32),
            jax.ShapeDtypeStruct((total, emb), F32),
            jax.ShapeDtypeStruct((groups - 1, groups - 1, rows, fg), BF16),
        ),
        in_specs=[ANY, ANY, VMEM, VMEM, VMEM],
        out_specs=(VMEM, VMEM, VMEM, ANY),
        scratch_shapes=[
            pltpu.VMEM((total, emb), BF16),
            pltpu.VMEM((tiles, rows, width), F32),
            pltpu.VMEM((rounds + 1, 2, tiles, width), F32),
            pltpu.VMEM((rounds, 2, tiles, width), F32),
            pltpu.SemaphoreType.DMA,
            pltpu.SemaphoreType.DMA((rounds,)),
            pltpu.SemaphoreType.DMA((rounds,)),
            pltpu.SemaphoreType.DMA((n_copies,)),
            pltpu.SemaphoreType.DMA((n_copies,)),
        ],
        compiler_params=pltpu.CompilerParams(
            collective_id=0, has_side_effects=True, vmem_limit_bytes=44 << 20),
        name="score",
    )(local, queries, normed, normed.T, bias)


def reduce_kernel(plans, n_in, n_peers_of, *refs):
    n = len(plans)
    ins, refs = refs[:n_in], refs[n_in:]
    outs = refs[:n]
    accs, sends, recvs = (refs[n + i * n : 2 * n + i * n] for i in range(3))
    send_sem, recv_sem, gsend, grecv = refs[4 * n :]
    greet([partner(a, b)[1] for a, b in n_peers_of])
    live = {}

    def begin(i, r):
        rounds, bases, _, source, start, count = plans[i]
        bit, peer = partner(*rounds[r])
        half = count >> (r + 1)
        at0 = count - 2 * half

        def stage(j, carry):
            if r == 0:
                block = ins[source][start + bases(j) + (1 - bit) * bases(half)]
            else:
                block = accs[i][(1 - bit) * half + j]
            sends[i][at0 + j] = block.astype(BF16)
            return carry

        lax.fori_loop(0, half, stage, 0)
        copy = pltpu.make_async_remote_copy(
            src_ref=sends[i].at[pl.ds(at0, half)], dst_ref=recvs[i].at[pl.ds(at0, half)],
            send_sem=send_sem.at[i, r], recv_sem=recv_sem.at[i, r],
            device_id=peer, device_id_type=MESH)
        copy.start()
        live[i] = copy

    def finish(i, r):
        rounds, bases, _, source, start, count = plans[i]
        bit, _ = partner(*rounds[r])
        half = count >> (r + 1)
        at0 = count - 2 * half
        live[i].wait()

        def add(j, carry):
            if r == 0:
                block = ins[source][start + bases(j) + bit * bases(half)]
            else:
                block = accs[i][bit * half + j]
            accs[i][j] = block + recvs[i][at0 + j].astype(F32)
            return carry

        lax.fori_loop(0, half, add, 0)

    def place(i, r):
        rounds = plans[i][0]
        return sum(partner(*rounds[k])[0] * (plans[i][5] >> (k + 1)) for k in range(r + 1))

    def share(i, r):
        peer = partner(*plans[i][0][r])[1]
        span = pl.ds(place(i, r), plans[i][5] >> (r + 1))
        copy = pltpu.make_async_remote_copy(
            src_ref=outs[i].at[span], dst_ref=outs[i].at[span],
            send_sem=gsend.at[i, r], recv_sem=grecv.at[i, r],
            device_id=peer, device_id_type=MESH)
        copy.start()
        live[i] = copy

    def advance(i, step):
        rounds, _, gather = plans[i][:3]
        k = len(rounds)
        if 0 < step <= k:
            finish(i, step - 1)
        if step < k:
            begin(i, step)
        elif step == k and not gather:
            outs[i][0] = accs[i][0]
        elif gather and step <= 2 * k:
            if step == k:
                outs[i][place(i, k - 1)] = accs[i][0].astype(BF16)
            else:
                live[i].wait()
            if step < 2 * k:
                share(i, 2 * k - 1 - step)

    steps = max(len(p[0]) * (2 if p[2] else 1) for p in plans) + 1
    for step in range(steps):
        for i in range(n):
            advance(i, step)


def bit_place(steps, j):
    k = len(steps)
    out = 0
    for i, step in enumerate(steps):
        weight = 1 << (k - 1 - i)
        if isinstance(j, int):
            out += (j // weight) % 2 * step
        else:
            out = out + lax.rem(lax.div(j, weight), 2) * step
    return out


def reduce_all(groups, n_dp, xs, parts):
    plans = []
    for source, start, n, rounds, gather in parts:
        if gather:
            steps = [n >> (k + 1) for k in range(len(rounds))]
        else:
            steps = [b * groups if a == "dp" else b for a, b in rounds]
        bases = functools.partial(bit_place, steps)
        plans.append((rounds, bases, gather, source, start, n))
    shapes = [(p[5],) + xs[p[3]].shape[1:] for p in plans]
    most = max(len(p[0]) for p in plans)
    peers = [("dp", b) for b in bits_of(n_dp)] + [("group", b) for b in bits_of(groups)]
    sems = pltpu.SemaphoreType.DMA((len(plans), most))
    return pl.pallas_call(
        functools.partial(reduce_kernel, plans, len(xs), peers),
        out_shape=tuple(
            jax.ShapeDtypeStruct(shape, BF16) if p[2] else jax.ShapeDtypeStruct((1,) + shape[1:], F32)
            for shape, p in zip(shapes, plans)),
        in_specs=[VMEM] * len(xs),
        out_specs=(VMEM,) * len(plans),
        scratch_shapes=[pltpu.VMEM((s[0] // 2,) + s[1:], F32) for s in shapes]
        + [pltpu.VMEM(s, BF16) for s in shapes] * 2 + [sems] * 4,
        compiler_params=pltpu.CompilerParams(
            collective_id=1, has_side_effects=True, vmem_limit_bytes=48 << 20),
        name="reduce_all",
    )(*xs)


def nt(a, b):
    return lax.dot_general(a, b, (((1,), (1,)), ((), ())), preferred_element_type=F32)


def tn(a, b):
    return lax.dot_general(a, b, (((0,), (0,)), ((), ())), preferred_element_type=F32)


def loop(n, body):
    def step(i, carry):
        body(i)
        return carry

    lax.fori_loop(0, n, step, 0)


def loop_by(k, n, body):
    def step(i, carry):
        for u in range(k):
            body(i * k + u)
        return carry

    lax.fori_loop(0, n // k, step, 0)


def weights_of(order):
    return {axis_step: 1 << (len(order) - 1 - k) for k, axis_step in enumerate(order)}


class Plan:
    def __init__(self, n_dp, queries, items, corpus, w1, w2):
        self.n_dp = n_dp
        self.query_rows, self.emb = queries.shape
        self.quota = self.query_rows // 2
        self.fg = items.shape[1]
        self.slab = corpus.shape[0]
        self.feats, self.hg = w1.shape
        bits = bits_of(n_dp)
        core, x, z = bits[0], bits[1], bits[2:]
        dp = lambda steps: [("dp", s) for s in steps]
        y = [("group", 1)]
        self.gather_orders = [[x] + z[::-1] + [core], z[::-1] + [x, core]]
        self.w_gather = [z[0], x, core]
        self.q_orders = [dp([core, x]) + y + dp(z), dp([core]) + y + dp([x]) + dp(z)]
        zn, zf = z[:1], z[1:]
        self.parts = [
            (48, dp([core]) + y + dp(zn + [x] + zf), z[::-1] + [x, core]),
            (16, dp([core, x]) + y + dp(z), z[::-1] + [x, core]),
            (32, dp([core, x]) + y + dp(z), [x] + z[::-1] + [core]),
            (32, dp([core] + zn + [x] + zf) + y, zf[::-1] + [x] + zn + [core]),
        ]
        self.w2_part = (dp([core] + zn + [x]) + y + dp(zf), z[::-1] + [x, core])
        self.bits = bits


ROW_PARTS = (0, 384, 512, 640)
CH = 128


def fused_kernel(pn, rows, queries, items, corpus, ids_in, shift_in, w1, w2,
                 loss_ref, gq_ref, gw1_ref, gw2_ref,
                 big, q_all, w1v, w2v, mine, peer, far, hot, ids_v, shift_v, pre, hid, emb, nrm, nrms, nrm_t,
                 bias, hat, logits, qpt, stats, arrived, total_ref, fac, featt, gp, ge,
                 recv, ag, qsend, qrecv, acc2, send2, recv2, ag2, lsem, ssem, rsem):
    n_dp, width, fg, hg, slab = pn.n_dp, pn.query_rows, pn.fg, pn.hg, pn.slab
    quota, e_dim = pn.quota, pn.emb
    negs = rows - quota
    chunks = negs // CH
    scale = e_dim ** (-0.5)
    m = lax.axis_index("group")
    d = lax.axis_index("dp")
    other = 1 - m
    ypeer = partner("group", 1)[1]
    core, xbit = pn.bits[0], pn.bits[1]
    rounds = [("dp", s) for s in pn.bits] + [("group", 1)]
    count = iter(range(1000))
    lcount = iter(range(100))

    def bit(step):
        return lax.rem(lax.div(d, step), 2)

    def remote(src, dst, to, k=None):
        k = next(count) if k is None else k
        return pltpu.make_async_remote_copy(
            src_ref=src, dst_ref=dst, send_sem=ssem.at[k], recv_sem=rsem.at[k],
            device_id=to, device_id_type=MESH)

    def local(src, dst):
        copy = pltpu.make_async_copy(src, dst, lsem.at[next(lcount)])
        copy.start()
        return copy

    gws = [{s: 1 << k for k, s in enumerate(order)} for order in pn.gather_orders]
    poss = [sum(bit(s) * gw[s] for s in pn.bits) for gw in gws]
    tiles = n_dp

    c_q = [local(queries.at[g * quota : (g + 1) * quota], q_all.at[g, poss[g]]) for g in range(2)]
    c_meta = [local(ids_in, ids_v), local(shift_in, shift_v)]
    c_slab = [local(corpus.at[:, n * 256 : (n + 1) * 256], big.at[n * slab : (n + 1) * slab])
              for n in range(fg // 256)]
    c_mine = local(items.at[pl.ds(pl.multiple_of(m * quota, quota), quota)], mine.at[0:quota])
    c_w1 = local(w1, w1v.at[0])
    c_w2 = local(w2, w2v.at[0])
    greet([partner(a, b)[1] for a, b in rounds])

    class Spread:
        def __init__(self, first, follow, n):
            self.follow, self.n, self.k = follow, n, 0
            self.live = first
            for c in first:
                c.start()

        def go(self):
            for c in self.live:
                c.wait()
            self.live = []
            if self.k < self.n:
                self.live = self.follow(self.k)
                for c in self.live:
                    c.start()
                self.k += 1

    n_piece = 1 << len(pn.w_gather)
    e = sum(bit(s) << k for k, s in enumerate(pn.w_gather))
    q1, q2 = fg // n_piece, hg // 2 // n_piece

    def w_rows(half, size):
        base = lax.div(e, size) * size
        return (pl.ds(pl.multiple_of(half * fg + base * q1, q1), size * q1),
                pl.ds(pl.multiple_of(half * (hg // 2) + base * q2, q2), size * q2))

    def w_spread(half, far_half):
        a, b = w_rows(far_half, 1)

        def follow(k):
            at1, at2 = w_rows(half, 1 << k)
            to = partner("dp", pn.w_gather[k])[1]
            return [remote(w1v.at[1, at1], w1v.at[1, at1], to),
                    remote(w2v.at[1, at2], w2v.at[1, at2], to)]

        return Spread([remote(w1.at[a], w1v.at[1, a], ypeer), remote(w2.at[b], w2v.at[1, b], ypeer)],
                      follow, len(pn.w_gather))

    def q_spread(g):
        def follow(k):
            view = q_all.at[g, pl.ds(lax.div(poss[g], 1 << k) * (1 << k), 1 << k)]
            return [remote(view, view, partner("dp", pn.gather_orders[g][k])[1])]

        return Spread(follow(0), lambda k: follow(k + 1), len(pn.bits) - 1)

    ws = [w_spread(m, other), w_spread(other, m)]
    for c in c_q:
        c.wait()
    qs = [q_spread(0), q_spread(1)]
    item_send = remote(items.at[pl.ds(pl.multiple_of(other * quota, quota), quota)],
                       peer.at[0:quota], ypeer)
    item_send.start()
    k_far = [next(count) for _ in range(chunks)][0]

    def rows_at(k):
        return pl.ds(pl.multiple_of(quota + k * CH, CH), CH)

    def far_copy(k):
        return remote(far.at[pl.ds(pl.multiple_of(k * CH, CH), CH)], peer.at[rows_at(k)],
                      ypeer, k_far + k)

    def column(ref, r):
        return jnp.broadcast_to(ref[pl.ds(r, 1), :].astype(F32), (8, CH)).T[:, :1]

    def pick(who, k, dst, at):
        ids = column(ids_v, who * chunks + k)
        where = lax.broadcasted_iota(jnp.int32, (CH, slab), 1).astype(F32)
        hot[...] = jnp.where(ids == where, 1.0, 0.0).astype(BF16)
        for n in range(fg // 256):
            dst[at, n * 256 : (n + 1) * 256] = mm(
                hot[...], big[n * slab : (n + 1) * slab, :]).astype(BF16)

    for c in c_meta + c_slab:
        c.wait()
    loop(chunks, lambda k: pick(other, k, far, pl.ds(pl.multiple_of(k * CH, CH), CH)))
    qs[0].go()
    qs[1].go()
    ws[0].go()
    ws[1].go()
    loop(chunks, lambda k: far_copy(k).start())
    loop(chunks, lambda k: pick(m, k, mine, rows_at(k)))
    qs[1].go()
    ws[0].go()
    qs[0].go()
    bias[0:quota, :] = jnp.zeros((quota, width), F32)

    def put_bias(k):
        bias[rows_at(k), :] = jnp.broadcast_to(
            -column(shift_v, m * chunks + k), (CH, width))

    loop(chunks, put_bias)
    c_mine.wait()
    c_w1.wait()
    c_w2.wait()
    ws[1].go()

    nj = hg // 256

    def tower_add(r0, r1, feat, half, c, first):
        for j in range(nj):
            part = mm(feat[r0:r1, :], w1v[c, pl.ds(pl.multiple_of(half * fg, fg), fg),
                                         j * 256 : (j + 1) * 256])
            if first:
                pre[c * nj + j, r0:r1, :] = part
            else:
                pre[c * nj + j, r0:r1, :] += part

    tower_add(0, rows, mine, m, 0, True)
    qs[1].go()
    qs[0].go()

    def turn(src, half, n):
        at = pl.multiple_of(n * 256, 256)
        featt[pl.ds(pl.multiple_of(half * fg + at, 256), 256), :] = src[:, pl.ds(at, 256)].T

    ws[0].go()
    loop(fg // 256, lambda n: turn(mine, m, n))
    ws[1].go()
    ws[0].go()
    tower_add(0, rows, mine, m, 1, True)
    ws[1].go()

    def finish_tower(r0, r1):
        loop(2, lambda c: tower_add(r0, r1, peer, other, c, False))
        emb[r0:r1, :] = jnp.zeros((r1 - r0, e_dim), F32)

        def second_layer(c):
            for j in range(nj):
                h = jnp.maximum(pre[c * nj + j, r0:r1, :], 0.0).astype(BF16)
                hid[c * nj + j, r0:r1, :] = h
                emb[r0:r1, :] += mm(h, w2v[c, j * 256 : (j + 1) * 256, :])

        loop(2, second_layer)
        em = emb[r0:r1, :]
        inv = lax.rsqrt(jnp.mean(em * em, -1, keepdims=True) + 1e-06)
        no = (em * inv).astype(BF16)
        nrm[r0:r1, :] = no
        nrms[r0:r1, :] = (no.astype(F32) * scale).astype(BF16)
        nrm_t[:, r0:r1] = no.astype(F32).T.astype(BF16)

    oqs = [weights_of(order) for order in pn.q_orders]
    he = e_dim // 2

    def shard_of(i, g, h):
        return g * oqs[h][("group", 1)] + sum(
            lax.rem(lax.div(i, gws[g][s]), 2) * oqs[h][("dp", s)] for s in pn.bits)

    half_q = width // 2

    def queries_at(i):
        return jnp.concatenate([q_all[0, i], q_all[1, i]], 0)

    def score(r0, r1):
        def one(i):
            block = nt(nrms[r0:r1, :], queries_at(i)) + bias[r0:r1, :]
            logits[i, r0:r1, :] = block
            top = jnp.max(block, 0, keepdims=True)
            at = pl.ds(i, 1)
            if r0 == 0:
                stats[0, 1, at, :] = jnp.sum(jnp.exp(block - top), 0, keepdims=True)
            else:
                before = stats[0, 0, at, :]
                top = jnp.maximum(before, top)
                stats[0, 1, at, :] = stats[0, 1, at, :] * jnp.exp(before - top) + jnp.sum(
                    jnp.exp(block - top), 0, keepdims=True)
            stats[0, 0, at, :] = top

        loop_by(4, tiles, one)

    item_send.wait()
    done = 0
    for r0, r1 in zip(ROW_PARTS[:-1], ROW_PARTS[1:]):
        upto = (r1 - quota) // CH
        for k in range(done, upto):
            far_copy(k).wait()
        done = upto
        finish_tower(r0, r1)
        if r0 == 0:
            qs[0].go()
            qs[1].go()
        score(r0, r1)

    def query_part(i):
        p = jnp.exp(logits[i] - stats[0, 0, pl.ds(i, 1), :])
        part = mm(nrm_t[...], p.astype(BF16))
        for g in range(2):
            for h in range(2):
                qpt[h, shard_of(i, g, h)] = part[
                    h * he : (h + 1) * he, g * half_q : (g + 1) * half_q]

    for r, (axis, step) in enumerate(rounds):
        copy = remote(stats.at[r], arrived.at[r], partner(axis, step)[1])
        copy.start()
        if r < 4:
            loop_by(2, tiles // 4, lambda i: query_part(r * (tiles // 4) + i))
        else:
            loop(fg // 256, lambda n: turn(peer, other, n))
        copy.wait()
        m0, s0, m1, s1 = stats[r, 0], stats[r, 1], arrived[r, 0], arrived[r, 1]
        top = jnp.maximum(m0, m1)
        stats[r + 1, 0] = top
        stats[r + 1, 1] = s0 * jnp.exp(m0 - top) + s1 * jnp.exp(m1 - top)
    last = len(rounds)
    total_ref[...] = stats[last, 0] + jnp.log(stats[last, 1])
    fac[...] = jnp.exp(stats[0, 0] - total_ref[...])

    class Chain:
        def __init__(self, order, put, add, send_at, recv_at):
            self.order, self.put, self.add = order, put, add
            self.send_at, self.recv_at = send_at, recv_at
            self.n = 1 << len(order)
            self.base = 0

        def launch(self, r):
            half = self.n >> (r + 1)
            at0 = self.n - 2 * half
            self.copy = remote(self.send_at(at0, half), self.recv_at(at0, half),
                               partner(*self.order[r])[1])
            self.copy.start()

        def send(self, r):
            half = self.n >> (r + 1)
            at0, came = self.n - 2 * half, self.n - 4 * half
            self.copy.wait()
            skip = (1 - partner(*self.order[r])[0]) * half
            base = self.base + skip
            loop_by(min(4, half), half, lambda j: self.put(at0 + j, base + j, came + skip + j))
            self.launch(r)

        def keep(self, r):
            half = self.n >> (r + 1)
            came = self.n - 4 * half
            skip = partner(*self.order[r])[0] * half
            base = self.base + skip
            loop_by(min(4, half), half, lambda j: self.add(base + j, came + skip + j))
            self.base = base

        def finish(self):
            self.copy.wait()
            self.add(self.base, self.n - 2)

    def advance(some, r):
        for ch in some:
            if r < len(ch.order):
                ch.send(r)
            else:
                ch.finish()
        for ch in some:
            if r < len(ch.order):
                ch.keep(r)

    cb = bit(core)
    own16 = cb * n_dp

    def q_chain(h):
        def put(slot, a, got):
            qsend[h, slot] = (qpt[h, own16 + a] + qrecv[h, got].astype(F32)).astype(BF16)

        def add(a, got):
            qpt[h, own16 + a] = qpt[h, own16 + a] + qrecv[h, got].astype(F32)

        return Chain(pn.q_orders[h], put, add,
                     lambda a, n: qsend.at[h, pl.ds(a, n)], lambda a, n: qrecv.at[h, pl.ds(a, n)])

    q_chains = [q_chain(0), q_chain(1)]

    def scale_q(i):
        f = fac[pl.ds(i, 1), :]
        for g in range(2):
            for h in range(2):
                j = shard_of(i, g, h)
                qpt[h, j] = qpt[h, j] * f[:, g * half_q : (g + 1) * half_q]

    def q_first(h, j):
        qsend[h, j] = qpt[h, (1 - cb) * n_dp + j].astype(BF16)

    loop_by(4, tiles, scale_q)
    for h in range(2):
        loop_by(4, n_dp, functools.partial(q_first, h))
        q_chains[h].launch(0)

    hat[...] = jnp.zeros_like(hat)

    def second(i):
        p = jnp.exp(logits[i] - total_ref[pl.ds(i, 1), :]).astype(BF16)
        hat[...] += mm(p, queries_at(i))

    loop_by(4, tiles // 2, second)
    advance(q_chains, 1)
    loop_by(4, tiles // 2, lambda i: second(tiles // 2 + i))

    pos = jnp.where(m == 0, poss[0], poss[1])
    q_own = q_all[m, pos].astype(F32)
    positive = nrm[0:quota, :].astype(F32)
    mine_total = total_ref[pl.ds(pos, 1), :]
    mine_total = jnp.where(m == 0, mine_total[:, :half_q], mine_total[:, half_q:])
    loss_ref[...] = mine_total - scale * jnp.sum((q_own * positive).T, 0, keepdims=True)

    hat[0:quota, :] = hat[0:quota, :] - q_own
    em = emb[...]
    inv = lax.rsqrt(jnp.mean(em * em, -1, keepdims=True) + 1e-06)
    gn = scale * hat[...]
    along = jnp.sum(gn * em, -1, keepdims=True)
    ge[...] = (inv * gn - inv**3 * em * along / e_dim).astype(BF16)

    def back(c):
        for j in range(nj):
            g = nt(ge[...], w2v[c, j * 256 : (j + 1) * 256, :])
            gp[c * nj + j] = jnp.where(pre[c * nj + j] > 0, g, 0.0).astype(BF16)

    loop(2, back)

    half_f = pn.feats // 2
    per_core = n_dp // 2
    n_all = 2 * n_dp

    def place(fb, g, order, spread):
        w = weights_of(order)
        return g * w[("group", 1)] + sum(
            (fb >> k) % 2 * w[("dp", s)] for k, s in enumerate(spread[:-1]))

    def group_of(c):
        return m if c == 0 else other

    starts = [sum(p[0] for p in pn.parts[:k]) for k in range(len(pn.parts))]

    def w1_half(cbit, sink):
        for c in range(2):
            for t in range(nj):
                r = mm(featt[pl.ds(pl.multiple_of(cbit * half_f, half_f), half_f), :], gp[c * nj + t])
                for fb in range(per_core):
                    for p, (pr, order, spread) in enumerate(pn.parts):
                        at = fb * CH + starts[p]
                        sink(p, place(fb, group_of(c), order, spread), t, r[at : at + pr, :])

    def piece_at(p, n, slot, t, size):
        pr = pn.parts[p][0]
        return pl.ds(pl.multiple_of(n * nj * starts[p] + slot * (nj * pr) + t * pr, 16), size * pr)

    def sink_send(p, j, t, v):
        big[piece_at(p, n_all - 1, j, t, 1), :] = v.astype(BF16)

    def cut_of(p, t):
        return slice(t * CH + starts[p], t * CH + starts[p] + pn.parts[p][0])

    def sink_acc(p, j, t, v):
        logits[j, cut_of(p, t), :] = v

    def w_chain(p):
        def total(a, got, t):
            return logits[a, cut_of(p, t), :] + recv[
                piece_at(p, n_all - 1, got, t, 1), :].astype(F32)

        def put(slot, a, got):
            for t in range(nj):
                sink_send(p, slot, t, total(a, got, t))

        def add(a, got):
            for t in range(nj):
                logits[a, cut_of(p, t), :] = total(a, got, t)

        return Chain(pn.parts[p][1], put, add,
                     lambda s, n: big.at[piece_at(p, n_all - 1, s, 0, n * nj)],
                     lambda s, n: recv.at[piece_at(p, n_all - 1, s, 0, n * nj)])

    h2 = 256 // per_core

    def w2_half(cbit, sink):
        for c in range(2):
            r = tn(hid[c * nj + cbit], ge[...])
            for fb in range(per_core):
                sink(place(fb, group_of(c), *pn.w2_part), r[fb * h2 : (fb + 1) * h2, :])

    def w2_send(j, v):
        send2[j] = v.astype(BF16)

    def w2_acc(j, v):
        acc2[j] = v

    def w2_put(slot, a, got):
        send2[slot] = (acc2[a] + recv2[got].astype(F32)).astype(BF16)

    def w2_add(a, got):
        acc2[a] = acc2[a] + recv2[got].astype(F32)

    chains = [w_chain(p) for p in range(len(pn.parts))]
    w2_chain = Chain(pn.w2_part[0], w2_put, w2_add,
                     lambda a, n: send2.at[pl.ds(a, n)], lambda a, n: recv2.at[pl.ds(a, n)])
    w1_half(1 - cb, sink_send)
    for ch in chains:
        ch.launch(0)
    w2_half(1 - cb, w2_send)
    w2_chain.launch(0)
    advance(q_chains, 2)
    w1_half(cb, sink_acc)
    w2_half(cb, w2_acc)
    every = chains + [w2_chain]
    steps = len(rounds)
    for r in range(1, steps + 1):
        advance(every, r)
        if r + 2 <= steps:
            advance(q_chains, r + 2)

    for h in range(2):
        gq_ref[:, h * he : (h + 1) * he] = scale * (
            qpt[h, own16 + q_chains[h].base].T - positive[:, h * he : (h + 1) * he])

    def block_of(spread):
        return sum(bit(s) << k for k, s in enumerate(spread))

    views = []
    for p, ch in enumerate(chains):
        spread = pn.parts[p][2]
        fb = block_of(spread)
        for t in range(nj):
            ag[piece_at(p, n_dp, fb, t, 1), :] = logits[ch.base, cut_of(p, t), :].astype(BF16)
        views.append((spread, fb, functools.partial(
            lambda p, b, n: ag.at[piece_at(p, n_dp, b, 0, n * nj)], p)))
    fb2 = block_of(pn.w2_part[1])
    ag2[fb2] = acc2[w2_chain.base].astype(BF16)
    views.append((pn.w2_part[1], fb2, lambda b, n: ag2.at[pl.ds(b, n)]))
    live = [None] * len(views)
    for k in range(len(pn.bits)):
        for i, (spread, fb, view) in enumerate(views):
            if live[i] is not None:
                live[i].wait()
            size = 1 << k
            v = view(lax.div(fb, size) * size, size)
            live[i] = remote(v, v, partner("dp", spread[k])[1])
            live[i].start()
    for c in live:
        c.wait()

    for p in range(len(chains)):
        def out_rows(fb):
            for t in range(nj):
                gw1_ref[pl.ds(pl.multiple_of(fb * CH + starts[p], 16), pn.parts[p][0]),
                        t * 256 : (t + 1) * 256] = ag[piece_at(p, n_dp, fb, t, 1), :]

        loop_by(4, n_dp, out_rows)
    gw2_ref[...] = ag2[...].reshape(gw2_ref.shape)


def fused(n_dp, queries, items, corpus, sample_ids, sample_shift, w1, w2):
    pn = Plan(n_dp, queries, items, corpus, w1, w2)
    width, emb = queries.shape
    negs = sample_ids.shape[0] // 2
    rows = pn.quota + negs
    fg, feats, hg = pn.fg, pn.feats, pn.hg
    nj = hg // 256
    n_all = 2 * n_dp
    rounds = n_all.bit_length() - 1
    ids = sample_ids.reshape(-1, CH)
    shifts = sample_shift.astype(F32).reshape(-1, CH)
    half = feats // 2
    sends = (n_all - 1) * nj * CH
    big = -(-max(sends, (fg // 256) * pn.slab) // 16) * 16
    hp = hg // n_dp
    n_sem = 96
    S = pltpu.VMEM
    loss, gq, gw1, gw2 = pl.pallas_call(
        functools.partial(fused_kernel, pn, rows),
        out_shape=(
            jax.ShapeDtypeStruct((1, pn.quota), F32),
            jax.ShapeDtypeStruct((pn.quota, emb), F32),
            jax.ShapeDtypeStruct((feats, hg), BF16),
            jax.ShapeDtypeStruct((hg, emb), BF16),
        ),
        in_specs=[ANY] * 7,
        out_specs=(VMEM,) * 4,
        scratch_shapes=[
            S((big, 256), BF16),
            S((2, n_dp, width // 2, emb), BF16),
            S((2, feats, hg), BF16),
            S((2, hg, emb), BF16),
            S((rows, fg), BF16),
            S((rows, fg), BF16),
            S((negs, fg), BF16),
            S((CH, pn.slab), BF16),
            S(ids.shape, jnp.int32),
            S(shifts.shape, F32),
            S((2 * nj, rows, 256), F32),
            S((2 * nj, rows, 256), BF16),
            S((rows, emb), F32),
            S((rows, emb), BF16),
            S((rows, emb), BF16),
            S((emb, rows), BF16),
            S((rows, width), F32),
            S((rows, emb), F32),
            S((n_dp, rows, width), F32),
            S((2, n_all, emb // 2, width // 2), F32),
            S((rounds + 1, 2, n_dp, width), F32),
            S((rounds, 2, n_dp, width), F32),
            S((n_dp, width), F32),
            S((n_dp, width), F32),
            S((feats, rows), BF16),
            S((2 * nj, rows, 256), BF16),
            S((rows, emb), BF16),
            S((sends, 256), BF16),
            S((n_dp * nj * CH, 256), BF16),
            S((2, n_all - 1, emb // 2, width // 2), BF16),
            S((2, n_all - 1, emb // 2, width // 2), BF16),
            S((n_dp, hp, emb), F32),
            S((n_all - 1, hp, emb), BF16),
            S((n_all - 1, hp, emb), BF16),
            S((n_dp, hp, emb), BF16),
            pltpu.SemaphoreType.DMA((16,)),
            pltpu.SemaphoreType.DMA((n_sem,)),
            pltpu.SemaphoreType.DMA((n_sem,)),
        ],
        compiler_params=pltpu.CompilerParams(
            collective_id=2, has_side_effects=True, vmem_limit_bytes=62 << 20),
        name="fused",
    )(queries, items, corpus, ids, shifts, w1, w2)
    return widen(loss, gq, gw1, gw2)


def widen_kernel(*refs):
    n = len(refs) // 2
    for a, b in zip(refs[:n], refs[n:]):
        b[...] = a[...].astype(F32)


def widen(loss, *grads):
    parts = 4
    specs = [pl.BlockSpec(loss.shape, lambda i: (0, 0))] + [
        pl.BlockSpec((x.shape[0] // parts, x.shape[1]), lambda i: (i, 0)) for x in grads]
    loss, *grads = pl.pallas_call(
        widen_kernel,
        grid=(parts,),
        out_shape=tuple(jax.ShapeDtypeStruct(x.shape, F32) for x in (loss, *grads)),
        in_specs=specs,
        out_specs=tuple(specs),
        name="widen",
    )(loss, *grads)
    return (loss.reshape(-1), *grads)


def fits(n_dp, groups, queries, items, corpus, sample_ids, w1, w2):
    negs = sample_ids.shape[0] // groups
    return (
        groups == 2 and n_dp == 16 and queries.shape == (256, 256)
        and (256 // groups + negs) == ROW_PARTS[-1]
        and w1.shape == (n_dp * CH, 512) and w2.shape == (512, 256)
        and items.shape[1] * 2 == w1.shape[0] and corpus.shape[0] % 256 == 0
    )


def per_device(queries, item_features, corpus, sample_ids, sample_shift, w1, w2):
    groups = lax.axis_size("group")
    member = lax.axis_index("group")
    n_dp = lax.axis_size("dp")
    d = lax.axis_index("dp")
    if fits(n_dp, groups, queries, item_features, corpus, sample_ids, w1, w2):
        return fused(n_dp, queries, item_features, corpus, sample_ids, sample_shift, w1, w2)
    query_rows, emb = queries.shape
    quota = query_rows // groups
    negs = sample_ids.shape[0] // groups
    rows = quota + negs
    fg = item_features.shape[1]
    scale = emb ** (-0.5)

    def shift(x, s):
        return lax.ppermute(x, "group", [(i, (i + s) % groups) for i in range(groups)])

    def at(x, i):
        return lax.dynamic_index_in_dim(x, lax.rem(i, groups), 0, keepdims=False)

    def place_columns(parts):
        if groups == 2:
            swap = member == 0
            return jnp.concatenate(
                [jnp.where(swap, parts[0], parts[1]), jnp.where(swap, parts[1], parts[0])], 1)
        out = jnp.zeros((parts[0].shape[0], groups * fg), BF16)
        for s in range(groups):
            start = lax.rem(member + groups - s, groups) * fg
            out = lax.dynamic_update_slice_in_dim(out, parts[s], start, 1)
        return out

    q_all = lax.all_gather(queries, "dp", axis=0, tiled=True)

    def swap_dp(x, step):
        return lax.ppermute(x, "dp", [(i, i ^ step) for i in range(n_dp)])

    def beside(x, cols):
        if x.shape[1] <= cols:
            return jnp.concatenate(jnp.split(x, cols // x.shape[1], 0), 1)
        return jnp.concatenate(jnp.split(x, x.shape[1] // cols, 1), 0)

    def restored(x, cols):
        if cols <= x.shape[1]:
            return jnp.concatenate(jnp.split(x, x.shape[1] // cols, 1), 0)
        return jnp.concatenate(jnp.split(x, cols // x.shape[1], 0), 1)

    quarter = lax.rem(d, 4)
    odd, high = lax.rem(quarter, 2) == 1, quarter >= 2
    w1_rows, w2_rows = w1.shape[0] // 4, w2.shape[0] // 4
    piece = jnp.concatenate([
        lax.dynamic_slice_in_dim(w1, quarter * w1_rows, w1_rows),
        beside(lax.dynamic_slice_in_dim(w2, quarter * w2_rows, w2_rows), w1.shape[1]),
    ], 0)
    items = item_features.reshape(groups, quota, fg)
    sample_ids, piece = lax.optimization_barrier((sample_ids, piece))
    got = [shift(piece, s) for s in range(1, groups)]
    ids = sample_ids.reshape(groups, negs)
    far_rows = [
        corpus.at[at(ids, member + s)].get(mode="promise_in_bounds") for s in range(1, groups)
    ]
    far_rows, items, got = lax.optimization_barrier((far_rows, items, got))
    item_parts = [shift(at(items, member + s), s) for s in range(1, groups)]
    picked_parts = [shift(far_rows[s - 1], s) for s in range(1, groups)]
    own_rows = corpus.at[at(ids, member)].get(mode="promise_in_bounds")
    blocks = [jnp.concatenate([at(items, member), own_rows], 0)]
    for s in range(1, groups):
        blocks.append(jnp.concatenate([at(items, member + s), far_rows[s - 1]], 0))
    local = jnp.stack(blocks[:1] if groups == 2 else blocks)

    w1s, w2s = [w1], [w2]
    for p0 in got:
        p2 = swap_dp(p0, 2)
        p1, p3 = swap_dp(p0, 1), swap_dp(p2, 1)
        low = [jnp.where(odd, p1, p0), jnp.where(odd, p0, p1)]
        upp = [jnp.where(odd, p3, p2), jnp.where(odd, p2, p3)]
        placed = [jnp.where(high, u, l) for u, l in zip(upp, low)]
        placed += [jnp.where(high, l, u) for u, l in zip(upp, low)]
        w1s.append(jnp.concatenate([p[:w1_rows] for p in placed], 0))
        w2s.append(jnp.concatenate([restored(p[w1_rows:], emb) for p in placed], 0))

    feats = place_columns(
        blocks[:1]
        + [jnp.concatenate([a, b], 0) for a, b in zip(item_parts, picked_parts)]
    )

    embedded = jnp.zeros((rows, emb), F32)
    pre_own = None
    for s in range(groups):
        pre = mm(feats, w1s[s])
        hid = jnp.maximum(pre, 0.0).astype(BF16)
        if s == 0:
            pre_own, hid_own = pre, hid
        embedded = embedded + mm(hid, w2s[s])
    inverse = lax.rsqrt(jnp.mean(embedded * embedded, -1, keepdims=True) + 1e-06)
    normed = (embedded * inverse).astype(BF16)
    shift_own = lax.dynamic_slice_in_dim(sample_shift, member * negs, negs).astype(F32)
    bias = jnp.concatenate([jnp.zeros((quota,), F32), -shift_own])

    log_total, grad_hat, query_part, landed = score(
        groups, n_dp, local, q_all, normed, bias[:, None])
    log_total = log_total.reshape(-1)
    rest = place_columns(
        [jnp.concatenate(blocks[1:], 0)] + [landed[s - 1].reshape(-1, fg) for s in range(1, groups)]
    )

    query_own = lax.dynamic_slice_in_dim(queries, member * quota, quota).astype(F32)
    positive_own = normed[:quota].astype(F32)
    positive = scale * jnp.sum(query_own * positive_own, -1)
    query_loss = (
        lax.dynamic_slice_in_dim(log_total, d * query_rows + member * quota, quota) - positive
    )
    target = jnp.concatenate([query_own, jnp.zeros((negs, emb), F32)], 0)
    grad_normed = scale * (grad_hat - target)
    along = jnp.sum(grad_normed * embedded, -1, keepdims=True)
    grad_embed = (
        inverse * grad_normed - inverse**3 * embedded * along / emb
    ).astype(BF16)

    pre_rest = mm(rest, w1)
    hid_rest = jnp.maximum(pre_rest, 0.0).astype(BF16)
    back = jnp.concatenate(
        [grad_embed] + [shift(grad_embed, (groups - t) % groups) for t in range(1, groups)], 0
    )
    mask = jnp.concatenate([pre_own, pre_rest], 0) > 0
    grad_pre = jnp.where(mask, mm(back, w2.T), 0.0).astype(BF16)
    hid_all = jnp.concatenate([hid_own, hid_rest], 0)
    over_rows = (((0,), (0,)), ((), ()))
    grad_w2 = lax.dot_general(hid_all, back, over_rows, preferred_element_type=F32)
    feats_all = jnp.concatenate([feats, rest], 0)
    grad_w1 = lax.dot_general(feats_all, grad_pre, over_rows, preferred_element_type=F32)
    dp_bits = bits_of(n_dp)
    near, far = dp_bits[:1], dp_bits[:1:-1]
    along_first = [("dp", b) for b in near + dp_bits[1:2] + far]
    along_last = [("dp", b) for b in near + far + dp_bits[1:2]]
    query_order = (
        [("dp", near[0])]
        + [("group", b) for b in bits_of(groups)]
        + [("dp", b) for b in dp_bits[1:2] + far]
    )
    pad = -grad_w2.shape[0] % (16 * n_dp)
    padded = jnp.pad(grad_w2, ((0, pad), (0, 0)))
    xs = [
        grad_w1.reshape(2 * n_dp, -1, grad_w1.shape[1]),
        padded.reshape(n_dp, -1, emb),
        query_part.reshape(n_dp * groups, quota, emb),
    ]
    out_a, out_b, out_w2, query_sum = reduce_all(groups, n_dp, xs, [
        (0, 0, n_dp, along_last, True),
        (0, n_dp, n_dp, along_first, True),
        (1, 0, n_dp, along_first, True),
        (2, 0, n_dp * groups, query_order, False),
    ])
    grad_query = scale * (query_sum[0] - positive_own)
    grad_w1 = jnp.concatenate([out_a, out_b], 0).reshape(grad_w1.shape).astype(F32)
    grad_w2 = out_w2.reshape(padded.shape)[: grad_w2.shape[0]].astype(F32)
    return (query_loss, grad_query, grad_w1, grad_w2)


def solution(mesh):
    in_specs = (
        P("dp", None),
        P("dp", "group"),
        P("dp", "group"),
        P("dp"),
        P("dp"),
        P(None, "group"),
        P("group", None),
    )
    out_specs = (P(("dp", "group")), P(("dp", "group"), None), P(None, "group"), P("group", None))
    return jax.shard_map(
        per_device, mesh=mesh, in_specs=in_specs, out_specs=out_specs, check_vma=False
    )
```

```python
import functools

import jax
import jax.numpy as jnp
from jax import lax
from jax.experimental import pallas as pl
from jax.experimental.pallas import tpu as pltpu
from jax.sharding import PartitionSpec as P

F32 = jnp.float32
BF16 = jnp.bfloat16
MESH = pl.DeviceIdType.MESH
ANY = pl.BlockSpec(memory_space=pl.ANY)
VMEM = pl.BlockSpec(memory_space=pltpu.VMEM)


def mm(a, b):
    return jnp.dot(a, b, preferred_element_type=F32)


def bits_of(n):
    return [1 << i for i in range(n.bit_length() - 1)]


def partner(axis, step):
    i = lax.axis_index(axis)
    bit = lax.rem(lax.div(i, step), 2)
    return bit, {axis: i + step - 2 * step * bit}


def greet(peers):
    barrier = pltpu.get_barrier_semaphore()
    for peer in peers:
        pl.semaphore_signal(barrier, inc=1, device_id=peer, device_id_type=MESH)
    pl.semaphore_wait(barrier, len(peers))


def score_kernel(groups, n_dp, local, queries_in, normed, normed_t, bias,
                 total_ref, hat_ref, part_ref, rest_ref,
                 queries, logits, stats, arrived, qsem, send_sem, recv_sem, fsend, frecv):
    tiles, cols, width = logits.shape
    emb = normed.shape[1]
    scale = emb ** (-0.5)
    member = lax.axis_index("group")
    rounds = [("dp", b) for b in bits_of(n_dp)] + [("group", b) for b in bits_of(groups)]
    peers = [partner(a, b)[1] for a, b in rounds]
    others = [lax.rem(member + s, groups) for s in range(1, groups)]
    extra = [{"group": o} for o in others] if groups > 2 else []
    fetch = pltpu.make_async_copy(queries_in, queries, qsem)
    fetch.start()
    greet(peers + extra)
    copies = []
    for s in range(1, groups):
        for t in range(1, groups):
            k = (s - 1) * (groups - 1) + t - 1
            copy = pltpu.make_async_remote_copy(
                src_ref=local.at[(s + t) % groups],
                dst_ref=rest_ref.at[s - 1, t - 1],
                send_sem=fsend.at[k], recv_sem=frecv.at[k],
                device_id={"group": others[s - 1]}, device_id_type=MESH)
            copy.start()
            copies.append(copy)

    def first(i, carry):
        q = queries[pl.ds(pl.multiple_of(i * width, width), width), :]
        block = scale * lax.dot_general(
            normed[...], q, (((1,), (1,)), ((), ())), preferred_element_type=F32) + bias[...]
        logits[i] = block
        top = jnp.max(block, 0, keepdims=True)
        stats[0, 0, pl.ds(i, 1), :] = top
        stats[0, 1, pl.ds(i, 1), :] = jnp.sum(jnp.exp(block - top), 0, keepdims=True)
        return carry

    fetch.wait()
    lax.fori_loop(0, tiles, first, 0)
    for r, peer in enumerate(peers):
        copy = pltpu.make_async_remote_copy(
            src_ref=stats.at[r], dst_ref=arrived.at[r],
            send_sem=send_sem.at[r], recv_sem=recv_sem.at[r],
            device_id=peer, device_id_type=MESH)
        copy.start()
        copy.wait()
        m0, s0, m1, s1 = stats[r, 0], stats[r, 1], arrived[r, 0], arrived[r, 1]
        top = jnp.maximum(m0, m1)
        stats[r + 1, 0] = top
        stats[r + 1, 1] = s0 * jnp.exp(m0 - top) + s1 * jnp.exp(m1 - top)
    last = len(peers)
    total_ref[...] = stats[last, 0] + jnp.log(stats[last, 1])
    hat_ref[...] = jnp.zeros_like(hat_ref)

    def second(i, carry):
        at_i = pl.ds(pl.multiple_of(i * width, width), width)
        p = jnp.exp(logits[i] - total_ref[pl.ds(i, 1), :]).astype(BF16)
        hat_ref[...] += mm(p, queries[at_i, :])
        part_ref[at_i, :] = mm(normed_t[...], p).T
        return carry

    lax.fori_loop(0, tiles, second, 0)
    for copy in copies:
        copy.wait()


def score(groups, n_dp, local, queries, normed, bias):
    rows, fg = local.shape[1:]
    width = 256
    total, emb = queries.shape
    tiles = total // width
    rounds = len(bits_of(n_dp)) + len(bits_of(groups))
    n_copies = (groups - 1) ** 2
    return pl.pallas_call(
        functools.partial(score_kernel, groups, n_dp),
        out_shape=(
            jax.ShapeDtypeStruct((tiles, width), F32),
            jax.ShapeDtypeStruct((rows, emb), F32),
            jax.ShapeDtypeStruct((total, emb), F32),
            jax.ShapeDtypeStruct((groups - 1, groups - 1, rows, fg), BF16),
        ),
        in_specs=[ANY, ANY, VMEM, VMEM, VMEM],
        out_specs=(VMEM, VMEM, VMEM, ANY),
        scratch_shapes=[
            pltpu.VMEM((total, emb), BF16),
            pltpu.VMEM((tiles, rows, width), F32),
            pltpu.VMEM((rounds + 1, 2, tiles, width), F32),
            pltpu.VMEM((rounds, 2, tiles, width), F32),
            pltpu.SemaphoreType.DMA,
            pltpu.SemaphoreType.DMA((rounds,)),
            pltpu.SemaphoreType.DMA((rounds,)),
            pltpu.SemaphoreType.DMA((n_copies,)),
            pltpu.SemaphoreType.DMA((n_copies,)),
        ],
        compiler_params=pltpu.CompilerParams(
            collective_id=0, has_side_effects=True, vmem_limit_bytes=44 << 20),
        name="score",
    )(local, queries, normed, normed.T, bias)


def reduce_kernel(plans, n_in, n_peers_of, *refs):
    n = len(plans)
    ins, refs = refs[:n_in], refs[n_in:]
    outs = refs[:n]
    accs, sends, recvs = (refs[n + i * n : 2 * n + i * n] for i in range(3))
    send_sem, recv_sem, gsend, grecv = refs[4 * n :]
    greet([partner(a, b)[1] for a, b in n_peers_of])
    live = {}

    def begin(i, r):
        rounds, bases, _, source, start, count = plans[i]
        bit, peer = partner(*rounds[r])
        half = count >> (r + 1)
        at0 = count - 2 * half

        def stage(j, carry):
            if r == 0:
                block = ins[source][start + bases(j) + (1 - bit) * bases(half)]
            else:
                block = accs[i][(1 - bit) * half + j]
            sends[i][at0 + j] = block.astype(BF16)
            return carry

        lax.fori_loop(0, half, stage, 0)
        copy = pltpu.make_async_remote_copy(
            src_ref=sends[i].at[pl.ds(at0, half)], dst_ref=recvs[i].at[pl.ds(at0, half)],
            send_sem=send_sem.at[i, r], recv_sem=recv_sem.at[i, r],
            device_id=peer, device_id_type=MESH)
        copy.start()
        live[i] = copy

    def finish(i, r):
        rounds, bases, _, source, start, count = plans[i]
        bit, _ = partner(*rounds[r])
        half = count >> (r + 1)
        at0 = count - 2 * half
        live[i].wait()

        def add(j, carry):
            if r == 0:
                block = ins[source][start + bases(j) + bit * bases(half)]
            else:
                block = accs[i][bit * half + j]
            accs[i][j] = block + recvs[i][at0 + j].astype(F32)
            return carry

        lax.fori_loop(0, half, add, 0)

    def place(i, r):
        rounds = plans[i][0]
        return sum(partner(*rounds[k])[0] * (plans[i][5] >> (k + 1)) for k in range(r + 1))

    def share(i, r):
        peer = partner(*plans[i][0][r])[1]
        span = pl.ds(place(i, r), plans[i][5] >> (r + 1))
        copy = pltpu.make_async_remote_copy(
            src_ref=outs[i].at[span], dst_ref=outs[i].at[span],
            send_sem=gsend.at[i, r], recv_sem=grecv.at[i, r],
            device_id=peer, device_id_type=MESH)
        copy.start()
        live[i] = copy

    def advance(i, step):
        rounds, _, gather = plans[i][:3]
        k = len(rounds)
        if 0 < step <= k:
            finish(i, step - 1)
        if step < k:
            begin(i, step)
        elif step == k and not gather:
            outs[i][0] = accs[i][0]
        elif gather and step <= 2 * k:
            if step == k:
                outs[i][place(i, k - 1)] = accs[i][0].astype(BF16)
            else:
                live[i].wait()
            if step < 2 * k:
                share(i, 2 * k - 1 - step)

    steps = max(len(p[0]) * (2 if p[2] else 1) for p in plans) + 1
    for step in range(steps):
        for i in range(n):
            advance(i, step)


def bit_place(steps, j):
    k = len(steps)
    out = 0
    for i, step in enumerate(steps):
        weight = 1 << (k - 1 - i)
        if isinstance(j, int):
            out += (j // weight) % 2 * step
        else:
            out = out + lax.rem(lax.div(j, weight), 2) * step
    return out


def reduce_all(groups, n_dp, xs, parts):
    plans = []
    for source, start, n, rounds, gather in parts:
        if gather:
            steps = [n >> (k + 1) for k in range(len(rounds))]
        else:
            steps = [b * groups if a == "dp" else b for a, b in rounds]
        bases = functools.partial(bit_place, steps)
        plans.append((rounds, bases, gather, source, start, n))
    shapes = [(p[5],) + xs[p[3]].shape[1:] for p in plans]
    most = max(len(p[0]) for p in plans)
    peers = [("dp", b) for b in bits_of(n_dp)] + [("group", b) for b in bits_of(groups)]
    sems = pltpu.SemaphoreType.DMA((len(plans), most))
    return pl.pallas_call(
        functools.partial(reduce_kernel, plans, len(xs), peers),
        out_shape=tuple(
            jax.ShapeDtypeStruct(shape, BF16) if p[2] else jax.ShapeDtypeStruct((1,) + shape[1:], F32)
            for shape, p in zip(shapes, plans)),
        in_specs=[VMEM] * len(xs),
        out_specs=(VMEM,) * len(plans),
        scratch_shapes=[pltpu.VMEM((s[0] // 2,) + s[1:], F32) for s in shapes]
        + [pltpu.VMEM(s, BF16) for s in shapes] * 2 + [sems] * 4,
        compiler_params=pltpu.CompilerParams(
            collective_id=1, has_side_effects=True, vmem_limit_bytes=48 << 20),
        name="reduce_all",
    )(*xs)


def nt(a, b):
    return lax.dot_general(a, b, (((1,), (1,)), ((), ())), preferred_element_type=F32)


def tn(a, b):
    return lax.dot_general(a, b, (((0,), (0,)), ((), ())), preferred_element_type=F32)


def loop(n, body):
    def step(i, carry):
        body(i)
        return carry

    lax.fori_loop(0, n, step, 0)


def loop_by(k, n, body):
    def step(i, carry):
        for u in range(k):
            body(i * k + u)
        return carry

    lax.fori_loop(0, n // k, step, 0)


def weights_of(order):
    return {axis_step: 1 << (len(order) - 1 - k) for k, axis_step in enumerate(order)}


class Plan:
    def __init__(self, n_dp, queries, items, corpus, w1, w2):
        self.n_dp = n_dp
        self.query_rows, self.emb = queries.shape
        self.quota = self.query_rows // 2
        self.fg = items.shape[1]
        self.slab = corpus.shape[0]
        self.feats, self.hg = w1.shape
        bits = bits_of(n_dp)
        core, x, z = bits[0], bits[1], bits[2:]
        dp = lambda steps: [("dp", s) for s in steps]
        y = [("group", 1)]
        self.gather_orders = [[x] + z[::-1] + [core], z[::-1] + [x, core]]
        self.w_gathers = [[x, z[0], core], [z[0], x, core]]
        self.phases = [dp([core, x]), dp(z[:1]) + y, dp(z[1:])]
        self.q_orders = [dp([core, x]) + y + dp(z), dp([core]) + y + dp([x]) + dp(z)]
        zn, zf = z[:1], z[1:]
        far_first, x_first = z[::-1] + [x, core], [x] + z[::-1] + [core]
        y_red = dp([core]) + y + dp(zn + [x] + zf)
        x_red = dp([core, x]) + y + dp(z)
        z_red = dp([core] + zn + [x] + zf) + y
        z_gat = zf[::-1] + [x] + zn + [core]
        self.groups = [
            [(32, y_red, far_first), (16, x_red, far_first), (16, z_red, z_gat)],
            [(16, y_red, far_first), (32, x_red, x_first), (16, z_red, z_gat)],
        ]
        self.parts = self.groups[0] + self.groups[1]
        self.w2_part = (dp([core] + zn + [x]) + y + dp(zf), z[::-1] + [x, core])
        self.bits = bits


ROW_PARTS = (0, 384, 512, 640)
CH = 128


def fused_kernel(pn, rows, queries, items, corpus, ids_in, shift_in, w1, w2,
                 loss_ref, gq_ref, gw1_ref, gw2_ref,
                 big, q_all, w1v, w2v, mine, peer, far, hot, ids_v, shift_v, pre, hid, emb, nrm, nrms, nrm_t,
                 bias, hat, logits, qpt, stats, arrived, total_ref, fac, featt, gp, ge,
                 recv, ag, qsend, qrecv, acc2, send2, recv2, ag2, lsem, ssem, rsem):
    n_dp, width, fg, hg, slab = pn.n_dp, pn.query_rows, pn.fg, pn.hg, pn.slab
    quota, e_dim = pn.quota, pn.emb
    negs = rows - quota
    chunks = negs // CH
    scale = e_dim ** (-0.5)
    m = lax.axis_index("group")
    d = lax.axis_index("dp")
    other = 1 - m
    ypeer = partner("group", 1)[1]
    core, xbit = pn.bits[0], pn.bits[1]
    rounds = [("dp", s) for s in pn.bits] + [("group", 1)]
    count = iter(range(1000))

    def across(subset):
        to = {}
        for axis, step in subset:
            at = to.get(axis, lax.axis_index(axis))
            to[axis] = at + step - 2 * step * lax.rem(lax.div(lax.axis_index(axis), step), 2)
        return to

    def subsets(phase):
        return [[r for k, r in enumerate(phase) if mask >> k & 1] for mask in range(1, 1 << len(phase))]

    met = [across(sub) for phase in pn.phases for sub in subsets(phase)]
    lcount = iter(range(100))

    def bit(step):
        return lax.rem(lax.div(d, step), 2)

    def remote(src, dst, to, k=None):
        k = next(count) if k is None else k
        return pltpu.make_async_remote_copy(
            src_ref=src, dst_ref=dst, send_sem=ssem.at[k], recv_sem=rsem.at[k],
            device_id=to, device_id_type=MESH)

    def local(src, dst):
        copy = pltpu.make_async_copy(src, dst, lsem.at[next(lcount)])
        copy.start()
        return copy

    gws = [{s: 1 << k for k, s in enumerate(order)} for order in pn.gather_orders]
    poss = [sum(bit(s) * gw[s] for s in pn.bits) for gw in gws]
    tiles = n_dp

    c_q = [local(queries.at[g * quota : (g + 1) * quota], q_all.at[g, poss[g]]) for g in range(2)]
    c_meta = [local(ids_in, ids_v), local(shift_in, shift_v)]
    c_slab = [local(corpus.at[:, n * 256 : (n + 1) * 256], big.at[n * slab : (n + 1) * slab])
              for n in range(fg // 256)]
    c_mine = local(items.at[pl.ds(pl.multiple_of(m * quota, quota), quota)], mine.at[0:quota])
    c_w1 = local(w1, w1v.at[0])
    c_w2 = local(w2, w2v.at[0])
    greet(met)

    class Spread:
        def __init__(self, first, follow, n):
            self.follow, self.n, self.k = follow, n, 0
            self.live = first
            for c in first:
                c.start()

        def go(self):
            for c in self.live:
                c.wait()
            self.live = []
            if self.k < self.n:
                self.live = self.follow(self.k)
                for c in self.live:
                    c.start()
                self.k += 1

    n_piece = 1 << len(pn.w_gathers[0])
    es = [sum(bit(s) << k for k, s in enumerate(gather)) for gather in pn.w_gathers]
    q1, q2 = fg // n_piece, hg // 2 // n_piece

    def w_rows(u, half, size):
        base = lax.div(es[u], size) * size
        return (pl.ds(pl.multiple_of(half * fg + base * q1, q1), size * q1),
                pl.ds(pl.multiple_of(half * (hg // 2) + base * q2, q2), size * q2))

    def w_spread(u, half, far_half):
        a, b = w_rows(u, far_half, 1)

        def follow(k):
            at1, at2 = w_rows(u, half, 1 << k)
            to = partner("dp", pn.w_gathers[u][k])[1]
            return [remote(w1v.at[1, at1], w1v.at[1, at1], to),
                    remote(w2v.at[1, at2], w2v.at[1, at2], to)]

        return Spread([remote(w1.at[a], w1v.at[1, a], ypeer), remote(w2.at[b], w2v.at[1, b], ypeer)],
                      follow, len(pn.w_gathers[u]))

    def q_spread(g):
        def follow(k):
            view = q_all.at[g, pl.ds(lax.div(poss[g], 1 << k) * (1 << k), 1 << k)]
            return [remote(view, view, partner("dp", pn.gather_orders[g][k])[1])]

        return Spread(follow(0), lambda k: follow(k + 1), len(pn.bits) - 1)

    ws = [w_spread(0, m, other), w_spread(1, other, m)]
    for c in c_q:
        c.wait()
    qs = [q_spread(0), q_spread(1)]
    item_send = remote(items.at[pl.ds(pl.multiple_of(other * quota, quota), quota)],
                       peer.at[0:quota], ypeer)
    item_send.start()
    k_far = [next(count) for _ in range(chunks)][0]

    def rows_at(k):
        return pl.ds(pl.multiple_of(quota + k * CH, CH), CH)

    def far_copy(k):
        return remote(far.at[pl.ds(pl.multiple_of(k * CH, CH), CH)], peer.at[rows_at(k)],
                      ypeer, k_far + k)

    def column(ref, r):
        return jnp.broadcast_to(ref[pl.ds(r, 1), :].astype(F32), (8, CH)).T[:, :1]

    def pick(who, k, dst, at):
        ids = column(ids_v, who * chunks + k)
        where = lax.broadcasted_iota(jnp.int32, (CH, slab), 1).astype(F32)
        hot[...] = jnp.where(ids == where, 1.0, 0.0).astype(BF16)
        for n in range(fg // 256):
            dst[at, n * 256 : (n + 1) * 256] = mm(
                hot[...], big[n * slab : (n + 1) * slab, :]).astype(BF16)

    for c in c_meta + c_slab:
        c.wait()
    loop(chunks, lambda k: pick(other, k, far, pl.ds(pl.multiple_of(k * CH, CH), CH)))
    qs[0].go()
    qs[1].go()
    ws[0].go()
    ws[1].go()
    loop(chunks, lambda k: far_copy(k).start())
    loop(chunks, lambda k: pick(m, k, mine, rows_at(k)))
    ws[0].go()
    qs[0].go()
    ws[1].go()
    bias[0:quota, :] = jnp.zeros((quota, width), F32)

    def put_bias(k):
        bias[rows_at(k), :] = jnp.broadcast_to(
            -column(shift_v, m * chunks + k), (CH, width))

    loop(chunks, put_bias)
    c_mine.wait()
    c_w1.wait()
    c_w2.wait()

    nj = hg // 256

    def tower_add(r0, r1, feat, half, c, first):
        for j in range(nj):
            part = mm(feat[r0:r1, :], w1v[c, pl.ds(pl.multiple_of(half * fg, fg), fg),
                                         j * 256 : (j + 1) * 256])
            if first:
                pre[c * nj + j, r0:r1, :] = part
            else:
                pre[c * nj + j, r0:r1, :] += part

    tower_add(0, rows, mine, m, 0, True)
    qs[1].go()

    hb = CH // 2

    def turn(src, half, n):
        at = pl.multiple_of(n * 256, 256)
        block = src[:, pl.ds(at, 256)].T
        for b in range(256 // CH):
            for k in range(2):
                row = half * fg + k * (fg // 2) + (n * (256 // CH) + b) * hb
                featt[pl.ds(pl.multiple_of(row, hb), hb), :] = block[
                    b * CH + k * hb : b * CH + (k + 1) * hb, :]

    loop(fg // 256, lambda n: turn(mine, m, n))
    ws[0].go()
    ws[1].go()
    qs[0].go()
    qs[1].go()
    ws[0].go()
    tower_add(0, rows, mine, m, 1, True)
    ws[1].go()

    def finish_tower(r0, r1):
        loop(2, lambda c: tower_add(r0, r1, peer, other, c, False))
        emb[r0:r1, :] = jnp.zeros((r1 - r0, e_dim), F32)

        def second_layer(c):
            for j in range(nj):
                h = jnp.maximum(pre[c * nj + j, r0:r1, :], 0.0).astype(BF16)
                hid[c * nj + j, r0:r1, :] = h
                emb[r0:r1, :] += mm(h, w2v[c, j * 256 : (j + 1) * 256, :])

        loop(2, second_layer)
        em = emb[r0:r1, :]
        inv = lax.rsqrt(jnp.mean(em * em, -1, keepdims=True) + 1e-06)
        no = (em * inv).astype(BF16)
        nrm[r0:r1, :] = no
        nrms[r0:r1, :] = (no.astype(F32) * scale).astype(BF16)
        nrm_t[:, r0:r1] = no.astype(F32).T.astype(BF16)

    oqs = [weights_of(order) for order in pn.q_orders]
    he = e_dim // 2

    def shard_of(i, g, h):
        return g * oqs[h][("group", 1)] + sum(
            lax.rem(lax.div(i, gws[g][s]), 2) * oqs[h][("dp", s)] for s in pn.bits)

    half_q = width // 2

    def queries_at(i):
        return jnp.concatenate([q_all[0, i], q_all[1, i]], 0)

    def score(r0, r1):
        def one(i):
            block = nt(nrms[r0:r1, :], queries_at(i)) + bias[r0:r1, :]
            logits[i, r0:r1, :] = block
            top = jnp.max(block, 0, keepdims=True)
            at = pl.ds(i, 1)
            if r0 == 0:
                stats[0, 1, at, :] = jnp.sum(jnp.exp(block - top), 0, keepdims=True)
            else:
                before = stats[0, 0, at, :]
                top = jnp.maximum(before, top)
                stats[0, 1, at, :] = stats[0, 1, at, :] * jnp.exp(before - top) + jnp.sum(
                    jnp.exp(block - top), 0, keepdims=True)
            stats[0, 0, at, :] = top

        loop_by(4, tiles, one)

    item_send.wait()
    done = 0
    for r0, r1 in zip(ROW_PARTS[:-1], ROW_PARTS[1:]):
        upto = (r1 - quota) // CH
        for k in range(done, upto):
            far_copy(k).wait()
        done = upto
        finish_tower(r0, r1)
        if r0 == 0:
            qs[0].go()
            qs[1].go()
        score(r0, r1)

    def query_part(i):
        p = jnp.exp(logits[i] - stats[0, 0, pl.ds(i, 1), :])
        part = mm(nrm_t[...], p.astype(BF16))
        for g in range(2):
            for h in range(2):
                qpt[h, shard_of(i, g, h)] = part[
                    h * he : (h + 1) * he, g * half_q : (g + 1) * half_q]

    slot = 0
    for ph, phase in enumerate(pn.phases):
        copies = []
        for sub in subsets(phase):
            copies.append(remote(stats.at[ph], arrived.at[slot + len(copies)], across(sub)))
            copies[-1].start()
        if ph < 2:
            loop_by(4, tiles // 2, lambda i: query_part(ph * (tiles // 2) + i))
        else:
            loop(fg // 256, lambda n: turn(peer, other, n))
        for c in copies:
            c.wait()
        held = [(stats[ph, 0], stats[ph, 1])] + [
            (arrived[slot + k, 0], arrived[slot + k, 1]) for k in range(len(copies))]
        slot += len(copies)
        top = functools.reduce(jnp.maximum, [a for a, _ in held])
        stats[ph + 1, 0] = top
        stats[ph + 1, 1] = sum(b * jnp.exp(a - top) for a, b in held)
    last = len(pn.phases)
    total_ref[...] = stats[last, 0] + jnp.log(stats[last, 1])
    fac[...] = jnp.exp(stats[0, 0] - total_ref[...])

    class Chain:
        def __init__(self, order, put, add, send_at, recv_at):
            self.order, self.put, self.add = order, put, add
            self.send_at, self.recv_at = send_at, recv_at
            self.n = 1 << len(order)
            self.base = 0

        def launch(self, r):
            half = self.n >> (r + 1)
            at0 = self.n - 2 * half
            self.copy = remote(self.send_at(at0, half), self.recv_at(at0, half),
                               partner(*self.order[r])[1])
            self.copy.start()

        def send(self, r):
            half = self.n >> (r + 1)
            at0, came = self.n - 2 * half, self.n - 4 * half
            self.copy.wait()
            skip = (1 - partner(*self.order[r])[0]) * half
            base = self.base + skip
            loop_by(min(4, half), half, lambda j: self.put(at0 + j, base + j, came + skip + j))
            self.launch(r)

        def keep(self, r):
            half = self.n >> (r + 1)
            came = self.n - 4 * half
            skip = partner(*self.order[r])[0] * half
            base = self.base + skip
            loop_by(min(4, half), half, lambda j: self.add(base + j, came + skip + j))
            self.base = base

        def finish(self):
            self.copy.wait()
            self.add(self.base, self.n - 2)

    def advance(some, r):
        for ch in some:
            if r < len(ch.order):
                ch.send(r)
            else:
                ch.finish()
        for ch in some:
            if r < len(ch.order):
                ch.keep(r)

    cb = bit(core)
    own16 = cb * n_dp

    def q_chain(h):
        def put(slot, a, got):
            qsend[h, slot] = (qpt[h, own16 + a] + qrecv[h, got].astype(F32)).astype(BF16)

        def add(a, got):
            qpt[h, own16 + a] = qpt[h, own16 + a] + qrecv[h, got].astype(F32)

        return Chain(pn.q_orders[h], put, add,
                     lambda a, n: qsend.at[h, pl.ds(a, n)], lambda a, n: qrecv.at[h, pl.ds(a, n)])

    q_chains = [q_chain(0), q_chain(1)]

    def scale_q(i):
        f = fac[pl.ds(i, 1), :]
        for g in range(2):
            for h in range(2):
                j = shard_of(i, g, h)
                qpt[h, j] = qpt[h, j] * f[:, g * half_q : (g + 1) * half_q]

    def q_first(h, j):
        qsend[h, j] = qpt[h, (1 - cb) * n_dp + j].astype(BF16)

    loop_by(4, tiles, scale_q)
    for h in range(2):
        loop_by(4, n_dp, functools.partial(q_first, h))
        q_chains[h].launch(0)

    hat[...] = jnp.zeros_like(hat)

    def second(i):
        p = jnp.exp(logits[i] - total_ref[pl.ds(i, 1), :]).astype(BF16)
        hat[...] += mm(p, queries_at(i))

    loop_by(4, tiles // 2, second)
    advance(q_chains, 1)
    loop_by(4, tiles // 2, lambda i: second(tiles // 2 + i))

    pos = jnp.where(m == 0, poss[0], poss[1])
    q_own = q_all[m, pos].astype(F32)
    positive = nrm[0:quota, :].astype(F32)
    mine_total = total_ref[pl.ds(pos, 1), :]
    mine_total = jnp.where(m == 0, mine_total[:, :half_q], mine_total[:, half_q:])
    loss_ref[...] = mine_total - scale * jnp.sum((q_own * positive).T, 0, keepdims=True)

    hat[0:quota, :] = hat[0:quota, :] - q_own
    em = emb[...]
    inv = lax.rsqrt(jnp.mean(em * em, -1, keepdims=True) + 1e-06)
    gn = scale * hat[...]
    along = jnp.sum(gn * em, -1, keepdims=True)
    ge[...] = (inv * gn - inv**3 * em * along / e_dim).astype(BF16)

    def back(c):
        for j in range(nj):
            g = nt(ge[...], w2v[c, j * 256 : (j + 1) * 256, :])
            gp[c * nj + j] = jnp.where(pre[c * nj + j] > 0, g, 0.0).astype(BF16)

    loop(2, back)

    half_f = pn.feats // 2
    per_core = n_dp // 2
    n_all = 2 * n_dp

    def place(fb, g, order, spread):
        w = weights_of(order)
        return g * w[("group", 1)] + sum(
            (fb >> k) % 2 * w[("dp", s)] for k, s in enumerate(spread[:-1]))

    def group_of(c):
        return m if c == 0 else other

    starts = [sum(p[0] for p in pn.parts[:k]) for k in range(len(pn.parts))]

    def w1_half(cbit, k, sink):
        own = range(k * len(pn.groups[0]), (k + 1) * len(pn.groups[0]))
        span = pl.ds(pl.multiple_of(cbit * half_f + k * (half_f // 2), half_f // 2), half_f // 2)
        for c in range(2):
            for t in range(nj):
                r = mm(featt[span, :], gp[c * nj + t])
                for fb in range(per_core):
                    for p in own:
                        pr, order, spread = pn.parts[p]
                        at = fb * hb + starts[p] - k * hb
                        sink(p, place(fb, group_of(c), order, spread), t, r[at : at + pr, :])

    def piece_at(p, n, slot, t, size):
        pr = pn.parts[p][0]
        return pl.ds(pl.multiple_of(n * nj * starts[p] + slot * (nj * pr) + t * pr, 16), size * pr)

    def sink_send(p, j, t, v):
        big[piece_at(p, n_all - 1, j, t, 1), :] = v.astype(BF16)

    def cut_of(p, t):
        return slice(t * CH + starts[p], t * CH + starts[p] + pn.parts[p][0])

    def sink_acc(p, j, t, v):
        logits[j, cut_of(p, t), :] = v

    def w_chain(p):
        def total(a, got, t):
            return logits[a, cut_of(p, t), :] + recv[
                piece_at(p, n_all - 1, got, t, 1), :].astype(F32)

        def put(slot, a, got):
            for t in range(nj):
                sink_send(p, slot, t, total(a, got, t))

        def add(a, got):
            for t in range(nj):
                logits[a, cut_of(p, t), :] = total(a, got, t)

        return Chain(pn.parts[p][1], put, add,
                     lambda s, n: big.at[piece_at(p, n_all - 1, s, 0, n * nj)],
                     lambda s, n: recv.at[piece_at(p, n_all - 1, s, 0, n * nj)])

    h2 = 256 // per_core

    def w2_half(cbit, sink):
        for c in range(2):
            r = tn(hid[c * nj + cbit], ge[...])
            for fb in range(per_core):
                sink(place(fb, group_of(c), *pn.w2_part), r[fb * h2 : (fb + 1) * h2, :])

    def w2_send(j, v):
        send2[j] = v.astype(BF16)

    def w2_acc(j, v):
        acc2[j] = v

    def w2_put(slot, a, got):
        send2[slot] = (acc2[a] + recv2[got].astype(F32)).astype(BF16)

    def w2_add(a, got):
        acc2[a] = acc2[a] + recv2[got].astype(F32)

    chains = [w_chain(p) for p in range(len(pn.parts))]
    w2_chain = Chain(pn.w2_part[0], w2_put, w2_add,
                     lambda a, n: send2.at[pl.ds(a, n)], lambda a, n: recv2.at[pl.ds(a, n)])
    teams = [chains[:3], chains[3:] + [w2_chain]]
    for k in range(2):
        w1_half(1 - cb, k, sink_send)
        for ch in chains[3 * k : 3 * k + 3]:
            ch.launch(0)
    w2_half(1 - cb, w2_send)
    w2_chain.launch(0)
    advance(q_chains, 2)
    w1_half(cb, 0, sink_acc)
    advance(teams[0], 1)
    w1_half(cb, 1, sink_acc)
    w2_half(cb, w2_acc)
    advance(teams[1], 1)
    advance(q_chains, 3)
    every = chains + [w2_chain]
    steps = len(rounds)
    for r in range(2, steps):
        for team in teams:
            advance(team, r)
        if r + 2 <= steps:
            advance(q_chains, r + 2)

    def block_of(spread):
        return sum(bit(s) << k for k, s in enumerate(spread))

    def w1_view(p, b, n):
        return ag.at[piece_at(p, n_dp, b, 0, n * nj)]

    def start_gather(i):
        p = every.index(i)
        if i is w2_chain:
            spread = pn.w2_part[1]
            fb = block_of(spread)
            ag2[fb] = acc2[i.base].astype(BF16)
            return spread, fb, lambda b, n: ag2.at[pl.ds(b, n)]
        spread = pn.parts[p][2]
        fb = block_of(spread)
        for t in range(nj):
            ag[piece_at(p, n_dp, fb, t, 1), :] = logits[i.base, cut_of(p, t), :].astype(BF16)
        return spread, fb, functools.partial(w1_view, p)

    def share(one, k):
        spread, fb, view = one
        size = 1 << k
        v = view(lax.div(fb, size) * size, size)
        c = remote(v, v, partner("dp", spread[k])[1])
        c.start()
        return c

    live, views = [], []
    for team in teams:
        group = []
        for ch in team:
            ch.finish()
            group.append(start_gather(ch))
        views.append(group)
        live.append([share(one, 0) for one in group])
    for k in range(1, len(pn.bits) + 1):
        for i, group in enumerate(views):
            for j, one in enumerate(group):
                live[i][j].wait()
                if k < len(pn.bits):
                    live[i][j] = share(one, k)

    for h in range(2):
        gq_ref[:, h * he : (h + 1) * he] = scale * (
            qpt[h, own16 + q_chains[h].base].T - positive[:, h * he : (h + 1) * he])

    for p in range(len(chains)):
        def out_rows(fb):
            for t in range(nj):
                gw1_ref[pl.ds(pl.multiple_of(fb * CH + starts[p], 16), pn.parts[p][0]),
                        t * 256 : (t + 1) * 256] = ag[piece_at(p, n_dp, fb, t, 1), :]

        loop_by(4, n_dp, out_rows)
    gw2_ref[...] = ag2[...].reshape(gw2_ref.shape)


def fused(n_dp, queries, items, corpus, sample_ids, sample_shift, w1, w2):
    pn = Plan(n_dp, queries, items, corpus, w1, w2)
    width, emb = queries.shape
    negs = sample_ids.shape[0] // 2
    rows = pn.quota + negs
    fg, feats, hg = pn.fg, pn.feats, pn.hg
    nj = hg // 256
    n_all = 2 * n_dp
    rounds = n_all.bit_length() - 1
    ids = sample_ids.reshape(-1, CH)
    shifts = sample_shift.astype(F32).reshape(-1, CH)
    half = feats // 2
    sends = (n_all - 1) * nj * CH
    big = -(-max(sends, (fg // 256) * pn.slab) // 16) * 16
    hp = hg // n_dp
    n_sem = 128
    S = pltpu.VMEM
    loss, gq, gw1, gw2 = pl.pallas_call(
        functools.partial(fused_kernel, pn, rows),
        out_shape=(
            jax.ShapeDtypeStruct((1, pn.quota), F32),
            jax.ShapeDtypeStruct((pn.quota, emb), F32),
            jax.ShapeDtypeStruct((feats, hg), BF16),
            jax.ShapeDtypeStruct((hg, emb), BF16),
        ),
        in_specs=[ANY] * 7,
        out_specs=(VMEM,) * 4,
        scratch_shapes=[
            S((big, 256), BF16),
            S((2, n_dp, width // 2, emb), BF16),
            S((2, feats, hg), BF16),
            S((2, hg, emb), BF16),
            S((rows, fg), BF16),
            S((rows, fg), BF16),
            S((negs, fg), BF16),
            S((CH, pn.slab), BF16),
            S(ids.shape, jnp.int32),
            S(shifts.shape, F32),
            S((2 * nj, rows, 256), F32),
            S((2 * nj, rows, 256), BF16),
            S((rows, emb), F32),
            S((rows, emb), BF16),
            S((rows, emb), BF16),
            S((emb, rows), BF16),
            S((rows, width), F32),
            S((rows, emb), F32),
            S((n_dp, rows, width), F32),
            S((2, n_all, emb // 2, width // 2), F32),
            S((rounds + 1, 2, n_dp, width), F32),
            S((sum((1 << len(p)) - 1 for p in pn.phases), 2, n_dp, width), F32),
            S((n_dp, width), F32),
            S((n_dp, width), F32),
            S((feats, rows), BF16),
            S((2 * nj, rows, 256), BF16),
            S((rows, emb), BF16),
            S((sends, 256), BF16),
            S((n_dp * nj * CH, 256), BF16),
            S((2, n_all - 1, emb // 2, width // 2), BF16),
            S((2, n_all - 1, emb // 2, width // 2), BF16),
            S((n_dp, hp, emb), F32),
            S((n_all - 1, hp, emb), BF16),
            S((n_all - 1, hp, emb), BF16),
            S((n_dp, hp, emb), BF16),
            pltpu.SemaphoreType.DMA((16,)),
            pltpu.SemaphoreType.DMA((n_sem,)),
            pltpu.SemaphoreType.DMA((n_sem,)),
        ],
        compiler_params=pltpu.CompilerParams(
            collective_id=2, has_side_effects=True, vmem_limit_bytes=62 << 20),
        name="fused",
    )(queries, items, corpus, ids, shifts, w1, w2)
    return widen(loss, gq, gw1, gw2)


def widen_kernel(*refs):
    n = len(refs) // 2
    for a, b in zip(refs[:n], refs[n:]):
        b[...] = a[...].astype(F32)


def widen(loss, *grads):
    parts = 2
    specs = [pl.BlockSpec(loss.shape, lambda i: (0, 0))] + [
        pl.BlockSpec((x.shape[0] // parts, x.shape[1]), lambda i: (i, 0)) for x in grads]
    loss, *grads = pl.pallas_call(
        widen_kernel,
        grid=(parts,),
        out_shape=tuple(jax.ShapeDtypeStruct(x.shape, F32) for x in (loss, *grads)),
        in_specs=specs,
        out_specs=tuple(specs),
        name="widen",
    )(loss, *grads)
    return (loss.reshape(-1), *grads)


def fits(n_dp, groups, queries, items, corpus, sample_ids, w1, w2):
    negs = sample_ids.shape[0] // groups
    return (
        groups == 2 and n_dp == 16 and queries.shape == (256, 256)
        and (256 // groups + negs) == ROW_PARTS[-1]
        and w1.shape == (n_dp * CH, 512) and w2.shape == (512, 256)
        and items.shape[1] * 2 == w1.shape[0] and corpus.shape[0] % 256 == 0
    )


def per_device(queries, item_features, corpus, sample_ids, sample_shift, w1, w2):
    groups = lax.axis_size("group")
    member = lax.axis_index("group")
    n_dp = lax.axis_size("dp")
    d = lax.axis_index("dp")
    if fits(n_dp, groups, queries, item_features, corpus, sample_ids, w1, w2):
        return fused(n_dp, queries, item_features, corpus, sample_ids, sample_shift, w1, w2)
    query_rows, emb = queries.shape
    quota = query_rows // groups
    negs = sample_ids.shape[0] // groups
    rows = quota + negs
    fg = item_features.shape[1]
    scale = emb ** (-0.5)

    def shift(x, s):
        return lax.ppermute(x, "group", [(i, (i + s) % groups) for i in range(groups)])

    def at(x, i):
        return lax.dynamic_index_in_dim(x, lax.rem(i, groups), 0, keepdims=False)

    def place_columns(parts):
        if groups == 2:
            swap = member == 0
            return jnp.concatenate(
                [jnp.where(swap, parts[0], parts[1]), jnp.where(swap, parts[1], parts[0])], 1)
        out = jnp.zeros((parts[0].shape[0], groups * fg), BF16)
        for s in range(groups):
            start = lax.rem(member + groups - s, groups) * fg
            out = lax.dynamic_update_slice_in_dim(out, parts[s], start, 1)
        return out

    q_all = lax.all_gather(queries, "dp", axis=0, tiled=True)

    def swap_dp(x, step):
        return lax.ppermute(x, "dp", [(i, i ^ step) for i in range(n_dp)])

    def beside(x, cols):
        if x.shape[1] <= cols:
            return jnp.concatenate(jnp.split(x, cols // x.shape[1], 0), 1)
        return jnp.concatenate(jnp.split(x, x.shape[1] // cols, 1), 0)

    def restored(x, cols):
        if cols <= x.shape[1]:
            return jnp.concatenate(jnp.split(x, x.shape[1] // cols, 1), 0)
        return jnp.concatenate(jnp.split(x, cols // x.shape[1], 0), 1)

    quarter = lax.rem(d, 4)
    odd, high = lax.rem(quarter, 2) == 1, quarter >= 2
    w1_rows, w2_rows = w1.shape[0] // 4, w2.shape[0] // 4
    piece = jnp.concatenate([
        lax.dynamic_slice_in_dim(w1, quarter * w1_rows, w1_rows),
        beside(lax.dynamic_slice_in_dim(w2, quarter * w2_rows, w2_rows), w1.shape[1]),
    ], 0)
    items = item_features.reshape(groups, quota, fg)
    sample_ids, piece = lax.optimization_barrier((sample_ids, piece))
    got = [shift(piece, s) for s in range(1, groups)]
    ids = sample_ids.reshape(groups, negs)
    far_rows = [
        corpus.at[at(ids, member + s)].get(mode="promise_in_bounds") for s in range(1, groups)
    ]
    far_rows, items, got = lax.optimization_barrier((far_rows, items, got))
    item_parts = [shift(at(items, member + s), s) for s in range(1, groups)]
    picked_parts = [shift(far_rows[s - 1], s) for s in range(1, groups)]
    own_rows = corpus.at[at(ids, member)].get(mode="promise_in_bounds")
    blocks = [jnp.concatenate([at(items, member), own_rows], 0)]
    for s in range(1, groups):
        blocks.append(jnp.concatenate([at(items, member + s), far_rows[s - 1]], 0))
    local = jnp.stack(blocks[:1] if groups == 2 else blocks)

    w1s, w2s = [w1], [w2]
    for p0 in got:
        p2 = swap_dp(p0, 2)
        p1, p3 = swap_dp(p0, 1), swap_dp(p2, 1)
        low = [jnp.where(odd, p1, p0), jnp.where(odd, p0, p1)]
        upp = [jnp.where(odd, p3, p2), jnp.where(odd, p2, p3)]
        placed = [jnp.where(high, u, l) for u, l in zip(upp, low)]
        placed += [jnp.where(high, l, u) for u, l in zip(upp, low)]
        w1s.append(jnp.concatenate([p[:w1_rows] for p in placed], 0))
        w2s.append(jnp.concatenate([restored(p[w1_rows:], emb) for p in placed], 0))

    feats = place_columns(
        blocks[:1]
        + [jnp.concatenate([a, b], 0) for a, b in zip(item_parts, picked_parts)]
    )

    embedded = jnp.zeros((rows, emb), F32)
    pre_own = None
    for s in range(groups):
        pre = mm(feats, w1s[s])
        hid = jnp.maximum(pre, 0.0).astype(BF16)
        if s == 0:
            pre_own, hid_own = pre, hid
        embedded = embedded + mm(hid, w2s[s])
    inverse = lax.rsqrt(jnp.mean(embedded * embedded, -1, keepdims=True) + 1e-06)
    normed = (embedded * inverse).astype(BF16)
    shift_own = lax.dynamic_slice_in_dim(sample_shift, member * negs, negs).astype(F32)
    bias = jnp.concatenate([jnp.zeros((quota,), F32), -shift_own])

    log_total, grad_hat, query_part, landed = score(
        groups, n_dp, local, q_all, normed, bias[:, None])
    log_total = log_total.reshape(-1)
    rest = place_columns(
        [jnp.concatenate(blocks[1:], 0)] + [landed[s - 1].reshape(-1, fg) for s in range(1, groups)]
    )

    query_own = lax.dynamic_slice_in_dim(queries, member * quota, quota).astype(F32)
    positive_own = normed[:quota].astype(F32)
    positive = scale * jnp.sum(query_own * positive_own, -1)
    query_loss = (
        lax.dynamic_slice_in_dim(log_total, d * query_rows + member * quota, quota) - positive
    )
    target = jnp.concatenate([query_own, jnp.zeros((negs, emb), F32)], 0)
    grad_normed = scale * (grad_hat - target)
    along = jnp.sum(grad_normed * embedded, -1, keepdims=True)
    grad_embed = (
        inverse * grad_normed - inverse**3 * embedded * along / emb
    ).astype(BF16)

    pre_rest = mm(rest, w1)
    hid_rest = jnp.maximum(pre_rest, 0.0).astype(BF16)
    back = jnp.concatenate(
        [grad_embed] + [shift(grad_embed, (groups - t) % groups) for t in range(1, groups)], 0
    )
    mask = jnp.concatenate([pre_own, pre_rest], 0) > 0
    grad_pre = jnp.where(mask, mm(back, w2.T), 0.0).astype(BF16)
    hid_all = jnp.concatenate([hid_own, hid_rest], 0)
    over_rows = (((0,), (0,)), ((), ()))
    grad_w2 = lax.dot_general(hid_all, back, over_rows, preferred_element_type=F32)
    feats_all = jnp.concatenate([feats, rest], 0)
    grad_w1 = lax.dot_general(feats_all, grad_pre, over_rows, preferred_element_type=F32)
    dp_bits = bits_of(n_dp)
    near, far = dp_bits[:1], dp_bits[:1:-1]
    along_first = [("dp", b) for b in near + dp_bits[1:2] + far]
    along_last = [("dp", b) for b in near + far + dp_bits[1:2]]
    query_order = (
        [("dp", near[0])]
        + [("group", b) for b in bits_of(groups)]
        + [("dp", b) for b in dp_bits[1:2] + far]
    )
    pad = -grad_w2.shape[0] % (16 * n_dp)
    padded = jnp.pad(grad_w2, ((0, pad), (0, 0)))
    xs = [
        grad_w1.reshape(2 * n_dp, -1, grad_w1.shape[1]),
        padded.reshape(n_dp, -1, emb),
        query_part.reshape(n_dp * groups, quota, emb),
    ]
    out_a, out_b, out_w2, query_sum = reduce_all(groups, n_dp, xs, [
        (0, 0, n_dp, along_last, True),
        (0, n_dp, n_dp, along_first, True),
        (1, 0, n_dp, along_first, True),
        (2, 0, n_dp * groups, query_order, False),
    ])
    grad_query = scale * (query_sum[0] - positive_own)
    grad_w1 = jnp.concatenate([out_a, out_b], 0).reshape(grad_w1.shape).astype(F32)
    grad_w2 = out_w2.reshape(padded.shape)[: grad_w2.shape[0]].astype(F32)
    return (query_loss, grad_query, grad_w1, grad_w2)


def solution(mesh):
    in_specs = (
        P("dp", None),
        P("dp", "group"),
        P("dp", "group"),
        P("dp"),
        P("dp"),
        P(None, "group"),
        P("group", None),
    )
    out_specs = (P(("dp", "group")), P(("dp", "group"), None), P(None, "group"), P("group", None))
    return jax.shard_map(
        per_device, mesh=mesh, in_specs=in_specs, out_specs=out_specs, check_vma=False
    )
```

```python
import functools

import jax
import jax.numpy as jnp
from jax import lax
from jax.experimental import pallas as pl
from jax.experimental.pallas import tpu as pltpu
from jax.sharding import PartitionSpec as P

F32 = jnp.float32
BF16 = jnp.bfloat16
MESH = pl.DeviceIdType.MESH
ANY = pl.BlockSpec(memory_space=pl.ANY)
VMEM = pl.BlockSpec(memory_space=pltpu.VMEM)


def mm(a, b):
    return jnp.dot(a, b, preferred_element_type=F32)


def bits_of(n):
    return [1 << i for i in range(n.bit_length() - 1)]


def partner(axis, step):
    i = lax.axis_index(axis)
    bit = lax.rem(lax.div(i, step), 2)
    return bit, {axis: i + step - 2 * step * bit}


def greet(peers):
    barrier = pltpu.get_barrier_semaphore()
    for peer in peers:
        pl.semaphore_signal(barrier, inc=1, device_id=peer, device_id_type=MESH)
    pl.semaphore_wait(barrier, len(peers))


def score_kernel(groups, n_dp, local, queries_in, normed, normed_t, bias,
                 total_ref, hat_ref, part_ref, rest_ref,
                 queries, logits, stats, arrived, qsem, send_sem, recv_sem, fsend, frecv):
    tiles, cols, width = logits.shape
    emb = normed.shape[1]
    scale = emb ** (-0.5)
    member = lax.axis_index("group")
    rounds = [("dp", b) for b in bits_of(n_dp)] + [("group", b) for b in bits_of(groups)]
    peers = [partner(a, b)[1] for a, b in rounds]
    others = [lax.rem(member + s, groups) for s in range(1, groups)]
    extra = [{"group": o} for o in others] if groups > 2 else []
    fetch = pltpu.make_async_copy(queries_in, queries, qsem)
    fetch.start()
    greet(peers + extra)
    copies = []
    for s in range(1, groups):
        for t in range(1, groups):
            k = (s - 1) * (groups - 1) + t - 1
            copy = pltpu.make_async_remote_copy(
                src_ref=local.at[(s + t) % groups],
                dst_ref=rest_ref.at[s - 1, t - 1],
                send_sem=fsend.at[k], recv_sem=frecv.at[k],
                device_id={"group": others[s - 1]}, device_id_type=MESH)
            copy.start()
            copies.append(copy)

    def first(i, carry):
        q = queries[pl.ds(pl.multiple_of(i * width, width), width), :]
        block = scale * lax.dot_general(
            normed[...], q, (((1,), (1,)), ((), ())), preferred_element_type=F32) + bias[...]
        logits[i] = block
        top = jnp.max(block, 0, keepdims=True)
        stats[0, 0, pl.ds(i, 1), :] = top
        stats[0, 1, pl.ds(i, 1), :] = jnp.sum(jnp.exp(block - top), 0, keepdims=True)
        return carry

    fetch.wait()
    lax.fori_loop(0, tiles, first, 0)
    for r, peer in enumerate(peers):
        copy = pltpu.make_async_remote_copy(
            src_ref=stats.at[r], dst_ref=arrived.at[r],
            send_sem=send_sem.at[r], recv_sem=recv_sem.at[r],
            device_id=peer, device_id_type=MESH)
        copy.start()
        copy.wait()
        m0, s0, m1, s1 = stats[r, 0], stats[r, 1], arrived[r, 0], arrived[r, 1]
        top = jnp.maximum(m0, m1)
        stats[r + 1, 0] = top
        stats[r + 1, 1] = s0 * jnp.exp(m0 - top) + s1 * jnp.exp(m1 - top)
    last = len(peers)
    total_ref[...] = stats[last, 0] + jnp.log(stats[last, 1])
    hat_ref[...] = jnp.zeros_like(hat_ref)

    def second(i, carry):
        at_i = pl.ds(pl.multiple_of(i * width, width), width)
        p = jnp.exp(logits[i] - total_ref[pl.ds(i, 1), :]).astype(BF16)
        hat_ref[...] += mm(p, queries[at_i, :])
        part_ref[at_i, :] = mm(normed_t[...], p).T
        return carry

    lax.fori_loop(0, tiles, second, 0)
    for copy in copies:
        copy.wait()


def score(groups, n_dp, local, queries, normed, bias):
    rows, fg = local.shape[1:]
    width = 256
    total, emb = queries.shape
    tiles = total // width
    rounds = len(bits_of(n_dp)) + len(bits_of(groups))
    n_copies = (groups - 1) ** 2
    return pl.pallas_call(
        functools.partial(score_kernel, groups, n_dp),
        out_shape=(
            jax.ShapeDtypeStruct((tiles, width), F32),
            jax.ShapeDtypeStruct((rows, emb), F32),
            jax.ShapeDtypeStruct((total, emb), F32),
            jax.ShapeDtypeStruct((groups - 1, groups - 1, rows, fg), BF16),
        ),
        in_specs=[ANY, ANY, VMEM, VMEM, VMEM],
        out_specs=(VMEM, VMEM, VMEM, ANY),
        scratch_shapes=[
            pltpu.VMEM((total, emb), BF16),
            pltpu.VMEM((tiles, rows, width), F32),
            pltpu.VMEM((rounds + 1, 2, tiles, width), F32),
            pltpu.VMEM((rounds, 2, tiles, width), F32),
            pltpu.SemaphoreType.DMA,
            pltpu.SemaphoreType.DMA((rounds,)),
            pltpu.SemaphoreType.DMA((rounds,)),
            pltpu.SemaphoreType.DMA((n_copies,)),
            pltpu.SemaphoreType.DMA((n_copies,)),
        ],
        compiler_params=pltpu.CompilerParams(
            collective_id=0, has_side_effects=True, vmem_limit_bytes=44 << 20),
        name="score",
    )(local, queries, normed, normed.T, bias)


def reduce_kernel(plans, n_in, n_peers_of, *refs):
    n = len(plans)
    ins, refs = refs[:n_in], refs[n_in:]
    outs = refs[:n]
    accs, sends, recvs = (refs[n + i * n : 2 * n + i * n] for i in range(3))
    send_sem, recv_sem, gsend, grecv = refs[4 * n :]
    greet([partner(a, b)[1] for a, b in n_peers_of])
    live = {}

    def begin(i, r):
        rounds, bases, _, source, start, count = plans[i]
        bit, peer = partner(*rounds[r])
        half = count >> (r + 1)
        at0 = count - 2 * half

        def stage(j, carry):
            if r == 0:
                block = ins[source][start + bases(j) + (1 - bit) * bases(half)]
            else:
                block = accs[i][(1 - bit) * half + j]
            sends[i][at0 + j] = block.astype(BF16)
            return carry

        lax.fori_loop(0, half, stage, 0)
        copy = pltpu.make_async_remote_copy(
            src_ref=sends[i].at[pl.ds(at0, half)], dst_ref=recvs[i].at[pl.ds(at0, half)],
            send_sem=send_sem.at[i, r], recv_sem=recv_sem.at[i, r],
            device_id=peer, device_id_type=MESH)
        copy.start()
        live[i] = copy

    def finish(i, r):
        rounds, bases, _, source, start, count = plans[i]
        bit, _ = partner(*rounds[r])
        half = count >> (r + 1)
        at0 = count - 2 * half
        live[i].wait()

        def add(j, carry):
            if r == 0:
                block = ins[source][start + bases(j) + bit * bases(half)]
            else:
                block = accs[i][bit * half + j]
            accs[i][j] = block + recvs[i][at0 + j].astype(F32)
            return carry

        lax.fori_loop(0, half, add, 0)

    def place(i, r):
        rounds = plans[i][0]
        return sum(partner(*rounds[k])[0] * (plans[i][5] >> (k + 1)) for k in range(r + 1))

    def share(i, r):
        peer = partner(*plans[i][0][r])[1]
        span = pl.ds(place(i, r), plans[i][5] >> (r + 1))
        copy = pltpu.make_async_remote_copy(
            src_ref=outs[i].at[span], dst_ref=outs[i].at[span],
            send_sem=gsend.at[i, r], recv_sem=grecv.at[i, r],
            device_id=peer, device_id_type=MESH)
        copy.start()
        live[i] = copy

    def advance(i, step):
        rounds, _, gather = plans[i][:3]
        k = len(rounds)
        if 0 < step <= k:
            finish(i, step - 1)
        if step < k:
            begin(i, step)
        elif step == k and not gather:
            outs[i][0] = accs[i][0]
        elif gather and step <= 2 * k:
            if step == k:
                outs[i][place(i, k - 1)] = accs[i][0].astype(BF16)
            else:
                live[i].wait()
            if step < 2 * k:
                share(i, 2 * k - 1 - step)

    steps = max(len(p[0]) * (2 if p[2] else 1) for p in plans) + 1
    for step in range(steps):
        for i in range(n):
            advance(i, step)


def bit_place(steps, j):
    k = len(steps)
    out = 0
    for i, step in enumerate(steps):
        weight = 1 << (k - 1 - i)
        if isinstance(j, int):
            out += (j // weight) % 2 * step
        else:
            out = out + lax.rem(lax.div(j, weight), 2) * step
    return out


def reduce_all(groups, n_dp, xs, parts):
    plans = []
    for source, start, n, rounds, gather in parts:
        if gather:
            steps = [n >> (k + 1) for k in range(len(rounds))]
        else:
            steps = [b * groups if a == "dp" else b for a, b in rounds]
        bases = functools.partial(bit_place, steps)
        plans.append((rounds, bases, gather, source, start, n))
    shapes = [(p[5],) + xs[p[3]].shape[1:] for p in plans]
    most = max(len(p[0]) for p in plans)
    peers = [("dp", b) for b in bits_of(n_dp)] + [("group", b) for b in bits_of(groups)]
    sems = pltpu.SemaphoreType.DMA((len(plans), most))
    return pl.pallas_call(
        functools.partial(reduce_kernel, plans, len(xs), peers),
        out_shape=tuple(
            jax.ShapeDtypeStruct(shape, BF16) if p[2] else jax.ShapeDtypeStruct((1,) + shape[1:], F32)
            for shape, p in zip(shapes, plans)),
        in_specs=[VMEM] * len(xs),
        out_specs=(VMEM,) * len(plans),
        scratch_shapes=[pltpu.VMEM((s[0] // 2,) + s[1:], F32) for s in shapes]
        + [pltpu.VMEM(s, BF16) for s in shapes] * 2 + [sems] * 4,
        compiler_params=pltpu.CompilerParams(
            collective_id=1, has_side_effects=True, vmem_limit_bytes=48 << 20),
        name="reduce_all",
    )(*xs)


def nt(a, b):
    return lax.dot_general(a, b, (((1,), (1,)), ((), ())), preferred_element_type=F32)


def tn(a, b):
    return lax.dot_general(a, b, (((0,), (0,)), ((), ())), preferred_element_type=F32)


def loop(n, body):
    def step(i, carry):
        body(i)
        return carry

    lax.fori_loop(0, n, step, 0)


def loop_by(k, n, body):
    def step(i, carry):
        for u in range(k):
            body(i * k + u)
        return carry

    lax.fori_loop(0, n // k, step, 0)


def weights_of(order):
    return {axis_step: 1 << (len(order) - 1 - k) for k, axis_step in enumerate(order)}


class Plan:
    def __init__(self, n_dp, queries, items, corpus, w1, w2):
        self.n_dp = n_dp
        self.query_rows, self.emb = queries.shape
        self.quota = self.query_rows // 2
        self.fg = items.shape[1]
        self.slab = corpus.shape[0]
        self.feats, self.hg = w1.shape
        bits = bits_of(n_dp)
        core, x, z = bits[0], bits[1], bits[2:]
        dp = lambda steps: [("dp", s) for s in steps]
        y = [("group", 1)]
        self.gather_orders = [[x] + z[::-1] + [core], z[::-1] + [x, core]]
        self.w_gathers = [[x, z[0], core], [z[0], x, core]]
        self.phases = [dp([core, x]), dp(z[:1]) + y, dp(z[1:])]
        self.q_orders = [dp([core, x]) + y + dp(z), dp([core]) + y + dp([x]) + dp(z)]
        zn, zf = z[:1], z[1:]
        far_first, x_first = z[::-1] + [x, core], [x] + z[::-1] + [core]
        y_red = dp([core]) + y + dp(zn + [x] + zf)
        x_red = dp([core, x]) + y + dp(z)
        z_red = dp([core] + zn + [x] + zf) + y
        z_gat = zf[::-1] + [x] + zn + [core]
        self.groups = [
            [(32, y_red, far_first), (16, x_red, far_first), (16, z_red, z_gat)],
            [(16, y_red, far_first), (32, x_red, x_first), (16, z_red, z_gat)],
        ]
        self.parts = self.groups[0] + self.groups[1]
        self.w2_part = (y_red, far_first)
        self.bits = bits


ROW_PARTS = (0, 384, 512, 640)
CH = 128


def fused_kernel(pn, rows, queries, items, corpus, ids_in, shift_in, w1, w2,
                 loss_ref, gq_ref, gw1_ref, gw2_ref,
                 big, q_all, w1v, w2v, mine, peer, far, hot, ids_v, shift_v, pre, hid, emb, nrm, nrms, nrm_t,
                 bias, hat, logits, qpt, stats, lse, arrived, total_ref, fac, featt, gp, ge,
                 recv, ag, qsend, qrecv, acc2, send2, recv2, ag2, lsem, ssem, rsem):
    n_dp, width, fg, hg, slab = pn.n_dp, pn.query_rows, pn.fg, pn.hg, pn.slab
    quota, e_dim = pn.quota, pn.emb
    negs = rows - quota
    chunks = negs // CH
    scale = e_dim ** (-0.5)
    m = lax.axis_index("group")
    d = lax.axis_index("dp")
    other = 1 - m
    ypeer = partner("group", 1)[1]
    core, xbit = pn.bits[0], pn.bits[1]
    rounds = [("dp", s) for s in pn.bits] + [("group", 1)]
    count = iter(range(1000))

    def across(subset):
        to = {}
        for axis, step in subset:
            at = to.get(axis, lax.axis_index(axis))
            to[axis] = at + step - 2 * step * lax.rem(lax.div(lax.axis_index(axis), step), 2)
        return to

    def subsets(phase):
        return [[r for k, r in enumerate(phase) if mask >> k & 1] for mask in range(1, 1 << len(phase))]

    met = [across(sub) for phase in pn.phases for sub in subsets(phase)]
    lcount = iter(range(100))

    def bit(step):
        return lax.rem(lax.div(d, step), 2)

    def remote(src, dst, to, k=None):
        k = next(count) if k is None else k
        return pltpu.make_async_remote_copy(
            src_ref=src, dst_ref=dst, send_sem=ssem.at[k], recv_sem=rsem.at[k],
            device_id=to, device_id_type=MESH)

    def local(src, dst):
        copy = pltpu.make_async_copy(src, dst, lsem.at[next(lcount)])
        copy.start()
        return copy

    gws = [{s: 1 << k for k, s in enumerate(order)} for order in pn.gather_orders]
    poss = [sum(bit(s) * gw[s] for s in pn.bits) for gw in gws]
    tiles = n_dp

    c_q = [local(queries.at[g * quota : (g + 1) * quota], q_all.at[g, poss[g]]) for g in range(2)]
    c_meta = [local(ids_in, ids_v)]
    c_slab = [local(corpus.at[:, n * 256 : (n + 1) * 256], big.at[n * slab : (n + 1) * slab])
              for n in range(fg // 256)]
    c_mine = local(items.at[pl.ds(pl.multiple_of(m * quota, quota), quota)], mine.at[0:quota])
    c_w1 = local(w1, w1v.at[0])
    c_w2 = local(w2, w2v.at[0])
    greet(met)

    class Spread:
        def __init__(self, first, follow, n):
            self.follow, self.n, self.k = follow, n, 0
            self.live = first
            for c in first:
                c.start()

        def go(self):
            for c in self.live:
                c.wait()
            self.live = []
            if self.k < self.n:
                self.live = self.follow(self.k)
                for c in self.live:
                    c.start()
                self.k += 1

    n_piece = 1 << len(pn.w_gathers[0])
    es = [sum(bit(s) << k for k, s in enumerate(gather)) for gather in pn.w_gathers]
    q1, q2 = fg // n_piece, hg // 2 // n_piece

    def w_rows(u, half, size):
        base = lax.div(es[u], size) * size
        return (pl.ds(pl.multiple_of(half * fg + base * q1, q1), size * q1),
                pl.ds(pl.multiple_of(half * (hg // 2) + base * q2, q2), size * q2))

    def w_spread(u, half, far_half):
        a, b = w_rows(u, far_half, 1)

        def follow(k):
            at1, at2 = w_rows(u, half, 1 << k)
            to = partner("dp", pn.w_gathers[u][k])[1]
            return [remote(w1v.at[1, at1], w1v.at[1, at1], to),
                    remote(w2v.at[1, at2], w2v.at[1, at2], to)]

        return Spread([remote(w1.at[a], w1v.at[1, a], ypeer), remote(w2.at[b], w2v.at[1, b], ypeer)],
                      follow, len(pn.w_gathers[u]))

    def q_spread(g):
        def follow(k):
            view = q_all.at[g, pl.ds(lax.div(poss[g], 1 << k) * (1 << k), 1 << k)]
            return [remote(view, view, partner("dp", pn.gather_orders[g][k])[1])]

        return Spread(follow(0), lambda k: follow(k + 1), len(pn.bits) - 1)

    ws = [w_spread(0, m, other), w_spread(1, other, m)]
    for c in c_q:
        c.wait()
    qs = [q_spread(0), q_spread(1)]
    item_send = remote(items.at[pl.ds(pl.multiple_of(other * quota, quota), quota)],
                       peer.at[0:quota], ypeer)
    item_send.start()
    k_far = [next(count) for _ in range(chunks)][0]

    def rows_at(k):
        return pl.ds(pl.multiple_of(quota + k * CH, CH), CH)

    def far_copy(k):
        return remote(far.at[pl.ds(pl.multiple_of(k * CH, CH), CH)], peer.at[rows_at(k)],
                      ypeer, k_far + k)

    def column(ref, r):
        return jnp.broadcast_to(ref[pl.ds(r, 1), :].astype(F32), (8, CH)).T[:, :1]

    def pick(who, k, dst, at):
        ids = column(ids_v, who * chunks + k)
        where = lax.broadcasted_iota(jnp.int32, (CH, slab), 1).astype(F32)
        hot[...] = jnp.where(ids == where, 1.0, 0.0).astype(BF16)
        for n in range(fg // 256):
            dst[at, n * 256 : (n + 1) * 256] = mm(
                hot[...], big[n * slab : (n + 1) * slab, :]).astype(BF16)

    for c in c_meta + c_slab:
        c.wait()
    loop(chunks, lambda k: pick(other, k, far, pl.ds(pl.multiple_of(k * CH, CH), CH)))
    qs[0].go()
    qs[1].go()
    ws[0].go()
    ws[1].go()
    loop(chunks, lambda k: far_copy(k).start())
    loop(chunks, lambda k: pick(m, k, mine, rows_at(k)))
    ws[0].go()
    qs[0].go()
    ws[1].go()
    shift_v[...] = shift_in[...].astype(F32)
    bias[0:quota, :] = jnp.zeros((quota, width), F32)

    def put_bias(k):
        bias[rows_at(k), :] = jnp.broadcast_to(
            -column(shift_v, m * chunks + k), (CH, width))

    loop(chunks, put_bias)
    c_mine.wait()
    c_w1.wait()
    c_w2.wait()

    nj = hg // 256

    def tower_add(r0, r1, feat, half, c, first):
        for j in range(nj):
            part = mm(feat[r0:r1, :], w1v[c, pl.ds(pl.multiple_of(half * fg, fg), fg),
                                         j * 256 : (j + 1) * 256])
            if first:
                pre[c * nj + j, r0:r1, :] = part
            else:
                pre[c * nj + j, r0:r1, :] += part

    tower_add(0, rows, mine, m, 0, True)
    qs[1].go()

    hb = CH // 2

    def turn(src, half, n):
        at = pl.multiple_of(n * 256, 256)
        block = src[:, pl.ds(at, 256)].T
        for b in range(256 // CH):
            for k in range(2):
                row = half * fg + k * (fg // 2) + (n * (256 // CH) + b) * hb
                featt[pl.ds(pl.multiple_of(row, hb), hb), :] = block[
                    b * CH + k * hb : b * CH + (k + 1) * hb, :]

    loop(fg // 256, lambda n: turn(mine, m, n))
    ws[0].go()
    ws[1].go()
    qs[0].go()
    qs[1].go()
    ws[0].go()
    tower_add(0, rows, mine, m, 1, True)
    ws[1].go()

    def finish_tower(r0, r1):
        loop(2, lambda c: tower_add(r0, r1, peer, other, c, False))
        emb[r0:r1, :] = jnp.zeros((r1 - r0, e_dim), F32)

        def second_layer(c):
            for j in range(nj):
                h = jnp.maximum(pre[c * nj + j, r0:r1, :], 0.0).astype(BF16)
                hid[c * nj + j, r0:r1, :] = h
                emb[r0:r1, :] += mm(h, w2v[c, j * 256 : (j + 1) * 256, :])

        loop(2, second_layer)
        em = emb[r0:r1, :]
        inv = lax.rsqrt(jnp.mean(em * em, -1, keepdims=True) + 1e-06)
        no = (em * inv).astype(BF16)
        nrm[r0:r1, :] = no
        nrms[r0:r1, :] = (no.astype(F32) * scale).astype(BF16)
        nrm_t[:, r0:r1] = no.astype(F32).T.astype(BF16)

    oqs = [weights_of(order) for order in pn.q_orders]
    he = e_dim // 2

    def shard_of(i, g, h):
        return g * oqs[h][("group", 1)] + sum(
            lax.rem(lax.div(i, gws[g][s]), 2) * oqs[h][("dp", s)] for s in pn.bits)

    half_q = width // 2

    def queries_at(i):
        return jnp.concatenate([q_all[0, i], q_all[1, i]], 0)

    def score(r0, r1):
        def one(i):
            block = nt(nrms[r0:r1, :], queries_at(i)) + bias[r0:r1, :]
            logits[i, r0:r1, :] = block
            top = jnp.max(block, 0, keepdims=True)
            at = pl.ds(i, 1)
            if r0 == 0:
                stats[0, 1, at, :] = jnp.sum(jnp.exp(block - top), 0, keepdims=True)
            else:
                before = stats[0, 0, at, :]
                top = jnp.maximum(before, top)
                stats[0, 1, at, :] = stats[0, 1, at, :] * jnp.exp(before - top) + jnp.sum(
                    jnp.exp(block - top), 0, keepdims=True)
            stats[0, 0, at, :] = top

        loop_by(4, tiles, one)

    item_send.wait()
    done = 0
    for r0, r1 in zip(ROW_PARTS[:-1], ROW_PARTS[1:]):
        upto = (r1 - quota) // CH
        for k in range(done, upto):
            far_copy(k).wait()
        done = upto
        finish_tower(r0, r1)
        if r0 == 0:
            qs[0].go()
            qs[1].go()
        score(r0, r1)

    def query_part(i):
        p = jnp.exp(logits[i] - stats[0, 0, pl.ds(i, 1), :])
        part = mm(nrm_t[...], p.astype(BF16))
        for g in range(2):
            for h in range(2):
                qpt[h, shard_of(i, g, h)] = part[
                    h * he : (h + 1) * he, g * half_q : (g + 1) * half_q]

    lse[0] = stats[0, 0] + jnp.log(stats[0, 1])
    slot = 0
    for ph, phase in enumerate(pn.phases):
        copies = []
        for sub in subsets(phase):
            copies.append(remote(lse.at[ph], arrived.at[slot + len(copies)], across(sub)))
            copies[-1].start()
        if ph < 2:
            loop_by(4, tiles // 2, lambda i: query_part(ph * (tiles // 2) + i))
        else:
            loop(fg // 256, lambda n: turn(peer, other, n))
        for c in copies:
            c.wait()
        held = [lse[ph]] + [arrived[slot + k] for k in range(len(copies))]
        slot += len(copies)
        top = functools.reduce(jnp.maximum, held)
        lse[ph + 1] = top + jnp.log(sum(jnp.exp(a - top) for a in held))
    total_ref[...] = lse[len(pn.phases)]
    fac[...] = jnp.exp(stats[0, 0] - total_ref[...])

    class Chain:
        def __init__(self, order, put, add, send_at, recv_at):
            self.order, self.put, self.add = order, put, add
            self.send_at, self.recv_at = send_at, recv_at
            self.n = 1 << len(order)
            self.base = 0

        def launch(self, r):
            half = self.n >> (r + 1)
            at0 = self.n - 2 * half
            self.copy = remote(self.send_at(at0, half), self.recv_at(at0, half),
                               partner(*self.order[r])[1])
            self.copy.start()

        def send(self, r):
            half = self.n >> (r + 1)
            at0, came = self.n - 2 * half, self.n - 4 * half
            self.copy.wait()
            skip = (1 - partner(*self.order[r])[0]) * half
            base = self.base + skip
            loop_by(min(4, half), half, lambda j: self.put(at0 + j, base + j, came + skip + j))
            self.launch(r)

        def keep(self, r):
            half = self.n >> (r + 1)
            came = self.n - 4 * half
            skip = partner(*self.order[r])[0] * half
            base = self.base + skip
            loop_by(min(4, half), half, lambda j: self.add(base + j, came + skip + j))
            self.base = base

        def finish(self):
            self.copy.wait()
            self.add(self.base, self.n - 2)

    def advance(some, r):
        for ch in some:
            if r < len(ch.order):
                ch.send(r)
            else:
                ch.finish()
        for ch in some:
            if r < len(ch.order):
                ch.keep(r)

    cb = bit(core)
    own16 = cb * n_dp

    def q_chain(h):
        def put(slot, a, got):
            qsend[h, slot] = (qpt[h, own16 + a] + qrecv[h, got].astype(F32)).astype(BF16)

        def add(a, got):
            qpt[h, own16 + a] = qpt[h, own16 + a] + qrecv[h, got].astype(F32)

        return Chain(pn.q_orders[h], put, add,
                     lambda a, n: qsend.at[h, pl.ds(a, n)], lambda a, n: qrecv.at[h, pl.ds(a, n)])

    q_chains = [q_chain(0), q_chain(1)]

    def scale_q(i):
        f = fac[pl.ds(i, 1), :]
        for g in range(2):
            for h in range(2):
                j = shard_of(i, g, h)
                qpt[h, j] = qpt[h, j] * f[:, g * half_q : (g + 1) * half_q]

    def q_first(h, j):
        qsend[h, j] = qpt[h, (1 - cb) * n_dp + j].astype(BF16)

    loop_by(4, tiles, scale_q)
    for h in range(2):
        loop_by(4, n_dp, functools.partial(q_first, h))
        q_chains[h].launch(0)

    hat[...] = jnp.zeros_like(hat)

    def second(i):
        p = jnp.exp(logits[i] - total_ref[pl.ds(i, 1), :]).astype(BF16)
        hat[...] += mm(p, queries_at(i))

    loop_by(4, tiles // 2, second)
    advance(q_chains, 1)
    loop_by(4, tiles // 2, lambda i: second(tiles // 2 + i))

    pos = jnp.where(m == 0, poss[0], poss[1])
    q_own = q_all[m, pos].astype(F32)
    positive = nrm[0:quota, :].astype(F32)
    mine_total = total_ref[pl.ds(pos, 1), :]
    mine_total = jnp.where(m == 0, mine_total[:, :half_q], mine_total[:, half_q:])
    loss_ref[...] = mine_total - scale * jnp.sum((q_own * positive).T, 0, keepdims=True)

    hat[0:quota, :] = hat[0:quota, :] - q_own
    em = emb[...]
    inv = lax.rsqrt(jnp.mean(em * em, -1, keepdims=True) + 1e-06)
    gn = scale * hat[...]
    along = jnp.sum(gn * em, -1, keepdims=True)
    ge[...] = (inv * gn - inv**3 * em * along / e_dim).astype(BF16)

    def back(c):
        for j in range(nj):
            g = nt(ge[...], w2v[c, j * 256 : (j + 1) * 256, :])
            gp[c * nj + j] = jnp.where(pre[c * nj + j] > 0, g, 0.0).astype(BF16)

    loop(2, back)

    half_f = pn.feats // 2
    per_core = n_dp // 2
    n_all = 2 * n_dp

    def place(fb, g, order, spread):
        w = weights_of(order)
        return g * w[("group", 1)] + sum(
            (fb >> k) % 2 * w[("dp", s)] for k, s in enumerate(spread[:-1]))

    def group_of(c):
        return m if c == 0 else other

    starts = [sum(p[0] for p in pn.parts[:k]) for k in range(len(pn.parts))]

    def w1_half(cbit, k, sink):
        own = range(k * len(pn.groups[0]), (k + 1) * len(pn.groups[0]))
        span = pl.ds(pl.multiple_of(cbit * half_f + k * (half_f // 2), half_f // 2), half_f // 2)
        for c in range(2):
            for t in range(nj):
                r = mm(featt[span, :], gp[c * nj + t])
                for fb in range(per_core):
                    for p in own:
                        pr, order, spread = pn.parts[p]
                        at = fb * hb + starts[p] - k * hb
                        sink(p, place(fb, group_of(c), order, spread), t, r[at : at + pr, :])

    def piece_at(p, n, slot, t, size):
        pr = pn.parts[p][0]
        return pl.ds(pl.multiple_of(n * nj * starts[p] + slot * (nj * pr) + t * pr, 16), size * pr)

    def sink_send(p, j, t, v):
        big[piece_at(p, n_all - 1, j, t, 1), :] = v.astype(BF16)

    def cut_of(p, t):
        return slice(t * CH + starts[p], t * CH + starts[p] + pn.parts[p][0])

    def sink_acc(p, j, t, v):
        logits[j, cut_of(p, t), :] = v

    def w_chain(p):
        def total(a, got, t):
            return logits[a, cut_of(p, t), :] + recv[
                piece_at(p, n_all - 1, got, t, 1), :].astype(F32)

        def put(slot, a, got):
            for t in range(nj):
                sink_send(p, slot, t, total(a, got, t))

        def add(a, got):
            for t in range(nj):
                logits[a, cut_of(p, t), :] = total(a, got, t)

        return Chain(pn.parts[p][1], put, add,
                     lambda s, n: big.at[piece_at(p, n_all - 1, s, 0, n * nj)],
                     lambda s, n: recv.at[piece_at(p, n_all - 1, s, 0, n * nj)])

    h2 = 256 // per_core

    def w2_half(cbit, sink):
        for c in range(2):
            r = tn(hid[c * nj + cbit], ge[...])
            for fb in range(per_core):
                sink(place(fb, group_of(c), *pn.w2_part), r[fb * h2 : (fb + 1) * h2, :])

    def w2_send(j, v):
        send2[j] = v.astype(BF16)

    def w2_acc(j, v):
        acc2[j] = v

    def w2_put(slot, a, got):
        send2[slot] = (acc2[a] + recv2[got].astype(F32)).astype(BF16)

    def w2_add(a, got):
        acc2[a] = acc2[a] + recv2[got].astype(F32)

    chains = [w_chain(p) for p in range(len(pn.parts))]
    w2_chain = Chain(pn.w2_part[0], w2_put, w2_add,
                     lambda a, n: send2.at[pl.ds(a, n)], lambda a, n: recv2.at[pl.ds(a, n)])
    teams = [chains[:3], chains[3:] + [w2_chain]]
    for k in range(2):
        w1_half(1 - cb, k, sink_send)
        for ch in chains[3 * k : 3 * k + 3]:
            ch.launch(0)
    w2_half(1 - cb, w2_send)
    w2_chain.launch(0)
    advance(q_chains, 2)
    w1_half(cb, 0, sink_acc)
    advance(teams[0], 1)
    w1_half(cb, 1, sink_acc)
    w2_half(cb, w2_acc)
    advance(teams[1], 1)
    advance(q_chains, 3)
    every = chains + [w2_chain]
    steps = len(rounds)
    for r in range(2, steps):
        for team in teams:
            advance(team, r)
        if r + 2 <= steps:
            advance(q_chains, r + 2)

    def block_of(spread):
        return sum(bit(s) << k for k, s in enumerate(spread))

    def w1_view(p, b, n):
        return ag.at[piece_at(p, n_dp, b, 0, n * nj)]

    def start_gather(i):
        p = every.index(i)
        if i is w2_chain:
            spread = pn.w2_part[1]
            fb = block_of(spread)
            ag2[fb] = acc2[i.base].astype(BF16)
            return spread, fb, lambda b, n: ag2.at[pl.ds(b, n)]
        spread = pn.parts[p][2]
        fb = block_of(spread)
        for t in range(nj):
            ag[piece_at(p, n_dp, fb, t, 1), :] = logits[i.base, cut_of(p, t), :].astype(BF16)
        return spread, fb, functools.partial(w1_view, p)

    def share(one, k):
        spread, fb, view = one
        size = 1 << k
        v = view(lax.div(fb, size) * size, size)
        c = remote(v, v, partner("dp", spread[k])[1])
        c.start()
        return c

    live, views = [], []
    for team in teams:
        group = []
        for ch in team:
            ch.finish()
            group.append(start_gather(ch))
        views.append(group)
        live.append([share(one, 0) for one in group])
    for k in range(1, len(pn.bits) + 1):
        for i, group in enumerate(views):
            for j, one in enumerate(group):
                live[i][j].wait()
                if k < len(pn.bits):
                    live[i][j] = share(one, k)

    for h in range(2):
        gq_ref[:, h * he : (h + 1) * he] = scale * (
            qpt[h, own16 + q_chains[h].base].T - positive[:, h * he : (h + 1) * he])

    for p in range(len(chains)):
        def out_rows(fb):
            for t in range(nj):
                gw1_ref[pl.ds(pl.multiple_of(fb * CH + starts[p], 16), pn.parts[p][0]),
                        t * 256 : (t + 1) * 256] = ag[piece_at(p, n_dp, fb, t, 1), :]

        loop_by(4, n_dp, out_rows)
    gw2_ref[...] = ag2[...].reshape(gw2_ref.shape)


def fused(n_dp, queries, items, corpus, sample_ids, sample_shift, w1, w2):
    pn = Plan(n_dp, queries, items, corpus, w1, w2)
    width, emb = queries.shape
    negs = sample_ids.shape[0] // 2
    rows = pn.quota + negs
    fg, feats, hg = pn.fg, pn.feats, pn.hg
    nj = hg // 256
    n_all = 2 * n_dp
    rounds = n_all.bit_length() - 1
    ids = sample_ids.reshape(-1, CH)
    shifts = sample_shift.reshape(-1, CH)
    half = feats // 2
    sends = (n_all - 1) * nj * CH
    big = -(-max(sends, (fg // 256) * pn.slab) // 16) * 16
    hp = hg // n_dp
    n_sem = 128
    S = pltpu.VMEM
    loss, gq, gw1, gw2 = pl.pallas_call(
        functools.partial(fused_kernel, pn, rows),
        out_shape=(
            jax.ShapeDtypeStruct((1, pn.quota), F32),
            jax.ShapeDtypeStruct((pn.quota, emb), F32),
            jax.ShapeDtypeStruct((feats, hg), BF16),
            jax.ShapeDtypeStruct((hg, emb), BF16),
        ),
        in_specs=[ANY] * 4 + [VMEM] + [ANY] * 2,
        out_specs=(VMEM,) * 4,
        scratch_shapes=[
            S((big, 256), BF16),
            S((2, n_dp, width // 2, emb), BF16),
            S((2, feats, hg), BF16),
            S((2, hg, emb), BF16),
            S((rows, fg), BF16),
            S((rows, fg), BF16),
            S((negs, fg), BF16),
            S((CH, pn.slab), BF16),
            S(ids.shape, jnp.int32),
            S(shifts.shape, F32),
            S((2 * nj, rows, 256), F32),
            S((2 * nj, rows, 256), BF16),
            S((rows, emb), F32),
            S((rows, emb), BF16),
            S((rows, emb), BF16),
            S((emb, rows), BF16),
            S((rows, width), F32),
            S((rows, emb), F32),
            S((n_dp, rows, width), F32),
            S((2, n_all, emb // 2, width // 2), F32),
            S((1, 2, n_dp, width), F32),
            S((len(pn.phases) + 1, n_dp, width), F32),
            S((sum((1 << len(p)) - 1 for p in pn.phases), n_dp, width), F32),
            S((n_dp, width), F32),
            S((n_dp, width), F32),
            S((feats, rows), BF16),
            S((2 * nj, rows, 256), BF16),
            S((rows, emb), BF16),
            S((sends, 256), BF16),
            S((n_dp * nj * CH, 256), BF16),
            S((2, n_all - 1, emb // 2, width // 2), BF16),
            S((2, n_all - 1, emb // 2, width // 2), BF16),
            S((n_dp, hp, emb), F32),
            S((n_all - 1, hp, emb), BF16),
            S((n_all - 1, hp, emb), BF16),
            S((n_dp, hp, emb), BF16),
            pltpu.SemaphoreType.DMA((16,)),
            pltpu.SemaphoreType.DMA((n_sem,)),
            pltpu.SemaphoreType.DMA((n_sem,)),
        ],
        compiler_params=pltpu.CompilerParams(
            collective_id=2, has_side_effects=True, vmem_limit_bytes=62 << 20),
        name="fused",
    )(queries, items, corpus, ids, shifts, w1, w2)
    return widen(loss, gq, gw1, gw2)


def widen_kernel(*refs):
    n = len(refs) // 2
    for a, b in zip(refs[:n], refs[n:]):
        b[...] = a[...].astype(F32)


def widen(loss, *grads):
    parts = 2
    specs = [pl.BlockSpec(loss.shape, lambda i: (0, 0))] + [
        pl.BlockSpec((x.shape[0] // parts, x.shape[1]), lambda i: (i, 0)) for x in grads]
    loss, *grads = pl.pallas_call(
        widen_kernel,
        grid=(parts,),
        out_shape=tuple(jax.ShapeDtypeStruct(x.shape, F32) for x in (loss, *grads)),
        in_specs=specs,
        out_specs=tuple(specs),
        name="widen",
    )(loss, *grads)
    return (loss.reshape(-1), *grads)


def fits(n_dp, groups, queries, items, corpus, sample_ids, w1, w2):
    negs = sample_ids.shape[0] // groups
    return (
        groups == 2 and n_dp == 16 and queries.shape == (256, 256)
        and (256 // groups + negs) == ROW_PARTS[-1]
        and w1.shape == (n_dp * CH, 512) and w2.shape == (512, 256)
        and items.shape[1] * 2 == w1.shape[0] and corpus.shape[0] % 256 == 0
    )


def per_device(queries, item_features, corpus, sample_ids, sample_shift, w1, w2):
    groups = lax.axis_size("group")
    member = lax.axis_index("group")
    n_dp = lax.axis_size("dp")
    d = lax.axis_index("dp")
    if fits(n_dp, groups, queries, item_features, corpus, sample_ids, w1, w2):
        return fused(n_dp, queries, item_features, corpus, sample_ids, sample_shift, w1, w2)
    query_rows, emb = queries.shape
    quota = query_rows // groups
    negs = sample_ids.shape[0] // groups
    rows = quota + negs
    fg = item_features.shape[1]
    scale = emb ** (-0.5)

    def shift(x, s):
        return lax.ppermute(x, "group", [(i, (i + s) % groups) for i in range(groups)])

    def at(x, i):
        return lax.dynamic_index_in_dim(x, lax.rem(i, groups), 0, keepdims=False)

    def place_columns(parts):
        if groups == 2:
            swap = member == 0
            return jnp.concatenate(
                [jnp.where(swap, parts[0], parts[1]), jnp.where(swap, parts[1], parts[0])], 1)
        out = jnp.zeros((parts[0].shape[0], groups * fg), BF16)
        for s in range(groups):
            start = lax.rem(member + groups - s, groups) * fg
            out = lax.dynamic_update_slice_in_dim(out, parts[s], start, 1)
        return out

    q_all = lax.all_gather(queries, "dp", axis=0, tiled=True)

    def swap_dp(x, step):
        return lax.ppermute(x, "dp", [(i, i ^ step) for i in range(n_dp)])

    def beside(x, cols):
        if x.shape[1] <= cols:
            return jnp.concatenate(jnp.split(x, cols // x.shape[1], 0), 1)
        return jnp.concatenate(jnp.split(x, x.shape[1] // cols, 1), 0)

    def restored(x, cols):
        if cols <= x.shape[1]:
            return jnp.concatenate(jnp.split(x, x.shape[1] // cols, 1), 0)
        return jnp.concatenate(jnp.split(x, cols // x.shape[1], 0), 1)

    quarter = lax.rem(d, 4)
    odd, high = lax.rem(quarter, 2) == 1, quarter >= 2
    w1_rows, w2_rows = w1.shape[0] // 4, w2.shape[0] // 4
    piece = jnp.concatenate([
        lax.dynamic_slice_in_dim(w1, quarter * w1_rows, w1_rows),
        beside(lax.dynamic_slice_in_dim(w2, quarter * w2_rows, w2_rows), w1.shape[1]),
    ], 0)
    items = item_features.reshape(groups, quota, fg)
    sample_ids, piece = lax.optimization_barrier((sample_ids, piece))
    got = [shift(piece, s) for s in range(1, groups)]
    ids = sample_ids.reshape(groups, negs)
    far_rows = [
        corpus.at[at(ids, member + s)].get(mode="promise_in_bounds") for s in range(1, groups)
    ]
    far_rows, items, got = lax.optimization_barrier((far_rows, items, got))
    item_parts = [shift(at(items, member + s), s) for s in range(1, groups)]
    picked_parts = [shift(far_rows[s - 1], s) for s in range(1, groups)]
    own_rows = corpus.at[at(ids, member)].get(mode="promise_in_bounds")
    blocks = [jnp.concatenate([at(items, member), own_rows], 0)]
    for s in range(1, groups):
        blocks.append(jnp.concatenate([at(items, member + s), far_rows[s - 1]], 0))
    local = jnp.stack(blocks[:1] if groups == 2 else blocks)

    w1s, w2s = [w1], [w2]
    for p0 in got:
        p2 = swap_dp(p0, 2)
        p1, p3 = swap_dp(p0, 1), swap_dp(p2, 1)
        low = [jnp.where(odd, p1, p0), jnp.where(odd, p0, p1)]
        upp = [jnp.where(odd, p3, p2), jnp.where(odd, p2, p3)]
        placed = [jnp.where(high, u, l) for u, l in zip(upp, low)]
        placed += [jnp.where(high, l, u) for u, l in zip(upp, low)]
        w1s.append(jnp.concatenate([p[:w1_rows] for p in placed], 0))
        w2s.append(jnp.concatenate([restored(p[w1_rows:], emb) for p in placed], 0))

    feats = place_columns(
        blocks[:1]
        + [jnp.concatenate([a, b], 0) for a, b in zip(item_parts, picked_parts)]
    )

    embedded = jnp.zeros((rows, emb), F32)
    pre_own = None
    for s in range(groups):
        pre = mm(feats, w1s[s])
        hid = jnp.maximum(pre, 0.0).astype(BF16)
        if s == 0:
            pre_own, hid_own = pre, hid
        embedded = embedded + mm(hid, w2s[s])
    inverse = lax.rsqrt(jnp.mean(embedded * embedded, -1, keepdims=True) + 1e-06)
    normed = (embedded * inverse).astype(BF16)
    shift_own = lax.dynamic_slice_in_dim(sample_shift, member * negs, negs).astype(F32)
    bias = jnp.concatenate([jnp.zeros((quota,), F32), -shift_own])

    log_total, grad_hat, query_part, landed = score(
        groups, n_dp, local, q_all, normed, bias[:, None])
    log_total = log_total.reshape(-1)
    rest = place_columns(
        [jnp.concatenate(blocks[1:], 0)] + [landed[s - 1].reshape(-1, fg) for s in range(1, groups)]
    )

    query_own = lax.dynamic_slice_in_dim(queries, member * quota, quota).astype(F32)
    positive_own = normed[:quota].astype(F32)
    positive = scale * jnp.sum(query_own * positive_own, -1)
    query_loss = (
        lax.dynamic_slice_in_dim(log_total, d * query_rows + member * quota, quota) - positive
    )
    target = jnp.concatenate([query_own, jnp.zeros((negs, emb), F32)], 0)
    grad_normed = scale * (grad_hat - target)
    along = jnp.sum(grad_normed * embedded, -1, keepdims=True)
    grad_embed = (
        inverse * grad_normed - inverse**3 * embedded * along / emb
    ).astype(BF16)

    pre_rest = mm(rest, w1)
    hid_rest = jnp.maximum(pre_rest, 0.0).astype(BF16)
    back = jnp.concatenate(
        [grad_embed] + [shift(grad_embed, (groups - t) % groups) for t in range(1, groups)], 0
    )
    mask = jnp.concatenate([pre_own, pre_rest], 0) > 0
    grad_pre = jnp.where(mask, mm(back, w2.T), 0.0).astype(BF16)
    hid_all = jnp.concatenate([hid_own, hid_rest], 0)
    over_rows = (((0,), (0,)), ((), ()))
    grad_w2 = lax.dot_general(hid_all, back, over_rows, preferred_element_type=F32)
    feats_all = jnp.concatenate([feats, rest], 0)
    grad_w1 = lax.dot_general(feats_all, grad_pre, over_rows, preferred_element_type=F32)
    dp_bits = bits_of(n_dp)
    near, far = dp_bits[:1], dp_bits[:1:-1]
    along_first = [("dp", b) for b in near + dp_bits[1:2] + far]
    along_last = [("dp", b) for b in near + far + dp_bits[1:2]]
    query_order = (
        [("dp", near[0])]
        + [("group", b) for b in bits_of(groups)]
        + [("dp", b) for b in dp_bits[1:2] + far]
    )
    pad = -grad_w2.shape[0] % (16 * n_dp)
    padded = jnp.pad(grad_w2, ((0, pad), (0, 0)))
    xs = [
        grad_w1.reshape(2 * n_dp, -1, grad_w1.shape[1]),
        padded.reshape(n_dp, -1, emb),
        query_part.reshape(n_dp * groups, quota, emb),
    ]
    out_a, out_b, out_w2, query_sum = reduce_all(groups, n_dp, xs, [
        (0, 0, n_dp, along_last, True),
        (0, n_dp, n_dp, along_first, True),
        (1, 0, n_dp, along_first, True),
        (2, 0, n_dp * groups, query_order, False),
    ])
    grad_query = scale * (query_sum[0] - positive_own)
    grad_w1 = jnp.concatenate([out_a, out_b], 0).reshape(grad_w1.shape).astype(F32)
    grad_w2 = out_w2.reshape(padded.shape)[: grad_w2.shape[0]].astype(F32)
    return (query_loss, grad_query, grad_w1, grad_w2)


def solution(mesh):
    in_specs = (
        P("dp", None),
        P("dp", "group"),
        P("dp", "group"),
        P("dp"),
        P("dp"),
        P(None, "group"),
        P("group", None),
    )
    out_specs = (P(("dp", "group")), P(("dp", "group"), None), P(None, "group"), P("group", None))
    return jax.shard_map(
        per_device, mesh=mesh, in_specs=in_specs, out_specs=out_specs, check_vma=False
    )
```

```python
import functools

import jax
import jax.numpy as jnp
from jax import lax
from jax.experimental import pallas as pl
from jax.experimental.pallas import tpu as pltpu
from jax.sharding import PartitionSpec as P

F32 = jnp.float32
BF16 = jnp.bfloat16
MESH = pl.DeviceIdType.MESH
ANY = pl.BlockSpec(memory_space=pl.ANY)
VMEM = pl.BlockSpec(memory_space=pltpu.VMEM)


def mm(a, b):
    return jnp.dot(a, b, preferred_element_type=F32)


def bits_of(n):
    return [1 << i for i in range(n.bit_length() - 1)]


def partner(axis, step):
    i = lax.axis_index(axis)
    bit = lax.rem(lax.div(i, step), 2)
    return bit, {axis: i + step - 2 * step * bit}


def greet(peers):
    barrier = pltpu.get_barrier_semaphore()
    for peer in peers:
        pl.semaphore_signal(barrier, inc=1, device_id=peer, device_id_type=MESH)
    pl.semaphore_wait(barrier, len(peers))


def score_kernel(groups, n_dp, local, queries_in, normed, normed_t, bias,
                 total_ref, hat_ref, part_ref, rest_ref,
                 queries, logits, stats, arrived, qsem, send_sem, recv_sem, fsend, frecv):
    tiles, cols, width = logits.shape
    emb = normed.shape[1]
    scale = emb ** (-0.5)
    member = lax.axis_index("group")
    rounds = [("dp", b) for b in bits_of(n_dp)] + [("group", b) for b in bits_of(groups)]
    peers = [partner(a, b)[1] for a, b in rounds]
    others = [lax.rem(member + s, groups) for s in range(1, groups)]
    extra = [{"group": o} for o in others] if groups > 2 else []
    fetch = pltpu.make_async_copy(queries_in, queries, qsem)
    fetch.start()
    greet(peers + extra)
    copies = []
    for s in range(1, groups):
        for t in range(1, groups):
            k = (s - 1) * (groups - 1) + t - 1
            copy = pltpu.make_async_remote_copy(
                src_ref=local.at[(s + t) % groups],
                dst_ref=rest_ref.at[s - 1, t - 1],
                send_sem=fsend.at[k], recv_sem=frecv.at[k],
                device_id={"group": others[s - 1]}, device_id_type=MESH)
            copy.start()
            copies.append(copy)

    def first(i, carry):
        q = queries[pl.ds(pl.multiple_of(i * width, width), width), :]
        block = scale * lax.dot_general(
            normed[...], q, (((1,), (1,)), ((), ())), preferred_element_type=F32) + bias[...]
        logits[i] = block
        top = jnp.max(block, 0, keepdims=True)
        stats[0, 0, pl.ds(i, 1), :] = top
        stats[0, 1, pl.ds(i, 1), :] = jnp.sum(jnp.exp(block - top), 0, keepdims=True)
        return carry

    fetch.wait()
    lax.fori_loop(0, tiles, first, 0)
    for r, peer in enumerate(peers):
        copy = pltpu.make_async_remote_copy(
            src_ref=stats.at[r], dst_ref=arrived.at[r],
            send_sem=send_sem.at[r], recv_sem=recv_sem.at[r],
            device_id=peer, device_id_type=MESH)
        copy.start()
        copy.wait()
        m0, s0, m1, s1 = stats[r, 0], stats[r, 1], arrived[r, 0], arrived[r, 1]
        top = jnp.maximum(m0, m1)
        stats[r + 1, 0] = top
        stats[r + 1, 1] = s0 * jnp.exp(m0 - top) + s1 * jnp.exp(m1 - top)
    last = len(peers)
    total_ref[...] = stats[last, 0] + jnp.log(stats[last, 1])
    hat_ref[...] = jnp.zeros_like(hat_ref)

    def second(i, carry):
        at_i = pl.ds(pl.multiple_of(i * width, width), width)
        p = jnp.exp(logits[i] - total_ref[pl.ds(i, 1), :]).astype(BF16)
        hat_ref[...] += mm(p, queries[at_i, :])
        part_ref[at_i, :] = mm(normed_t[...], p).T
        return carry

    lax.fori_loop(0, tiles, second, 0)
    for copy in copies:
        copy.wait()


def score(groups, n_dp, local, queries, normed, bias):
    rows, fg = local.shape[1:]
    width = 256
    total, emb = queries.shape
    tiles = total // width
    rounds = len(bits_of(n_dp)) + len(bits_of(groups))
    n_copies = (groups - 1) ** 2
    return pl.pallas_call(
        functools.partial(score_kernel, groups, n_dp),
        out_shape=(
            jax.ShapeDtypeStruct((tiles, width), F32),
            jax.ShapeDtypeStruct((rows, emb), F32),
            jax.ShapeDtypeStruct((total, emb), F32),
            jax.ShapeDtypeStruct((groups - 1, groups - 1, rows, fg), BF16),
        ),
        in_specs=[ANY, ANY, VMEM, VMEM, VMEM],
        out_specs=(VMEM, VMEM, VMEM, ANY),
        scratch_shapes=[
            pltpu.VMEM((total, emb), BF16),
            pltpu.VMEM((tiles, rows, width), F32),
            pltpu.VMEM((rounds + 1, 2, tiles, width), F32),
            pltpu.VMEM((rounds, 2, tiles, width), F32),
            pltpu.SemaphoreType.DMA,
            pltpu.SemaphoreType.DMA((rounds,)),
            pltpu.SemaphoreType.DMA((rounds,)),
            pltpu.SemaphoreType.DMA((n_copies,)),
            pltpu.SemaphoreType.DMA((n_copies,)),
        ],
        compiler_params=pltpu.CompilerParams(
            collective_id=0, has_side_effects=True, vmem_limit_bytes=44 << 20),
        name="score",
    )(local, queries, normed, normed.T, bias)


def reduce_kernel(plans, n_in, n_peers_of, *refs):
    n = len(plans)
    ins, refs = refs[:n_in], refs[n_in:]
    outs = refs[:n]
    accs, sends, recvs = (refs[n + i * n : 2 * n + i * n] for i in range(3))
    send_sem, recv_sem, gsend, grecv = refs[4 * n :]
    greet([partner(a, b)[1] for a, b in n_peers_of])
    live = {}

    def begin(i, r):
        rounds, bases, _, source, start, count = plans[i]
        bit, peer = partner(*rounds[r])
        half = count >> (r + 1)
        at0 = count - 2 * half

        def stage(j, carry):
            if r == 0:
                block = ins[source][start + bases(j) + (1 - bit) * bases(half)]
            else:
                block = accs[i][(1 - bit) * half + j]
            sends[i][at0 + j] = block.astype(BF16)
            return carry

        lax.fori_loop(0, half, stage, 0)
        copy = pltpu.make_async_remote_copy(
            src_ref=sends[i].at[pl.ds(at0, half)], dst_ref=recvs[i].at[pl.ds(at0, half)],
            send_sem=send_sem.at[i, r], recv_sem=recv_sem.at[i, r],
            device_id=peer, device_id_type=MESH)
        copy.start()
        live[i] = copy

    def finish(i, r):
        rounds, bases, _, source, start, count = plans[i]
        bit, _ = partner(*rounds[r])
        half = count >> (r + 1)
        at0 = count - 2 * half
        live[i].wait()

        def add(j, carry):
            if r == 0:
                block = ins[source][start + bases(j) + bit * bases(half)]
            else:
                block = accs[i][bit * half + j]
            accs[i][j] = block + recvs[i][at0 + j].astype(F32)
            return carry

        lax.fori_loop(0, half, add, 0)

    def place(i, r):
        rounds = plans[i][0]
        return sum(partner(*rounds[k])[0] * (plans[i][5] >> (k + 1)) for k in range(r + 1))

    def share(i, r):
        peer = partner(*plans[i][0][r])[1]
        span = pl.ds(place(i, r), plans[i][5] >> (r + 1))
        copy = pltpu.make_async_remote_copy(
            src_ref=outs[i].at[span], dst_ref=outs[i].at[span],
            send_sem=gsend.at[i, r], recv_sem=grecv.at[i, r],
            device_id=peer, device_id_type=MESH)
        copy.start()
        live[i] = copy

    def advance(i, step):
        rounds, _, gather = plans[i][:3]
        k = len(rounds)
        if 0 < step <= k:
            finish(i, step - 1)
        if step < k:
            begin(i, step)
        elif step == k and not gather:
            outs[i][0] = accs[i][0]
        elif gather and step <= 2 * k:
            if step == k:
                outs[i][place(i, k - 1)] = accs[i][0].astype(BF16)
            else:
                live[i].wait()
            if step < 2 * k:
                share(i, 2 * k - 1 - step)

    steps = max(len(p[0]) * (2 if p[2] else 1) for p in plans) + 1
    for step in range(steps):
        for i in range(n):
            advance(i, step)


def bit_place(steps, j):
    k = len(steps)
    out = 0
    for i, step in enumerate(steps):
        weight = 1 << (k - 1 - i)
        if isinstance(j, int):
            out += (j // weight) % 2 * step
        else:
            out = out + lax.rem(lax.div(j, weight), 2) * step
    return out


def reduce_all(groups, n_dp, xs, parts):
    plans = []
    for source, start, n, rounds, gather in parts:
        if gather:
            steps = [n >> (k + 1) for k in range(len(rounds))]
        else:
            steps = [b * groups if a == "dp" else b for a, b in rounds]
        bases = functools.partial(bit_place, steps)
        plans.append((rounds, bases, gather, source, start, n))
    shapes = [(p[5],) + xs[p[3]].shape[1:] for p in plans]
    most = max(len(p[0]) for p in plans)
    peers = [("dp", b) for b in bits_of(n_dp)] + [("group", b) for b in bits_of(groups)]
    sems = pltpu.SemaphoreType.DMA((len(plans), most))
    return pl.pallas_call(
        functools.partial(reduce_kernel, plans, len(xs), peers),
        out_shape=tuple(
            jax.ShapeDtypeStruct(shape, BF16) if p[2] else jax.ShapeDtypeStruct((1,) + shape[1:], F32)
            for shape, p in zip(shapes, plans)),
        in_specs=[VMEM] * len(xs),
        out_specs=(VMEM,) * len(plans),
        scratch_shapes=[pltpu.VMEM((s[0] // 2,) + s[1:], F32) for s in shapes]
        + [pltpu.VMEM(s, BF16) for s in shapes] * 2 + [sems] * 4,
        compiler_params=pltpu.CompilerParams(
            collective_id=1, has_side_effects=True, vmem_limit_bytes=48 << 20),
        name="reduce_all",
    )(*xs)


def nt(a, b):
    return lax.dot_general(a, b, (((1,), (1,)), ((), ())), preferred_element_type=F32)


def tn(a, b):
    return lax.dot_general(a, b, (((0,), (0,)), ((), ())), preferred_element_type=F32)


def loop(n, body):
    def step(i, carry):
        body(i)
        return carry

    lax.fori_loop(0, n, step, 0)


def loop_by(k, n, body):
    def step(i, carry):
        for u in range(k):
            body(i * k + u)
        return carry

    lax.fori_loop(0, n // k, step, 0)


def weights_of(order):
    return {axis_step: 1 << (len(order) - 1 - k) for k, axis_step in enumerate(order)}


class Plan:
    def __init__(self, n_dp, queries, items, corpus, w1, w2):
        self.n_dp = n_dp
        self.query_rows, self.emb = queries.shape
        self.quota = self.query_rows // 2
        self.fg = items.shape[1]
        self.slab = corpus.shape[0]
        self.feats, self.hg = w1.shape
        bits = bits_of(n_dp)
        core, x, z = bits[0], bits[1], bits[2:]
        dp = lambda steps: [("dp", s) for s in steps]
        y = [("group", 1)]
        self.gather_orders = [[x] + z[::-1] + [core], z[::-1] + [x, core]]
        self.w_gathers = [[x, z[0], core], [z[0], x, core]]
        self.phases = [dp([core, x]), dp(z[:1]) + y, dp(z[1:])]
        self.q_orders = [dp([core, x]) + y + dp(z), dp([core]) + y + dp([x]) + dp(z)]
        zn, zf = z[:1], z[1:]
        far_first, x_first = z[::-1] + [x, core], [x] + z[::-1] + [core]
        y_red = dp([core]) + y + dp(zn + [x] + zf)
        x_red = dp([core, x]) + y + dp(z)
        z_red = dp([core] + zn + [x] + zf) + y
        z_gat = zf[::-1] + [x] + zn + [core]
        self.groups = [
            [(32, y_red, far_first), (16, x_red, far_first), (16, z_red, z_gat)],
            [(16, y_red, far_first), (32, x_red, x_first), (16, z_red, z_gat)],
        ]
        self.parts = self.groups[0] + self.groups[1]
        self.w2_part = (y_red, far_first)
        self.bits = bits


ROW_PARTS = (0, 384, 512, 640)
CH = 128


def fused_kernel(pn, rows, queries, items, corpus, ids_in, shift_in, w1, w2,
                 loss_ref, gq_ref, gw1_ref, gw2_ref,
                 big, q_all, w1v, w2v, mine, peer, far, hot, ids_v, shift_v, pre, hid, emb, nrm, nrms, nrm_t,
                 bias, hat, logits, qpt, stats, lse, arrived, total_ref, fac, featt, gp, ge,
                 recv, ag, qsend, qrecv, acc2, send2, recv2, ag2, lsem, ssem, rsem):
    n_dp, width, fg, hg, slab = pn.n_dp, pn.query_rows, pn.fg, pn.hg, pn.slab
    quota, e_dim = pn.quota, pn.emb
    negs = rows - quota
    chunks = negs // CH
    scale = e_dim ** (-0.5)
    m = lax.axis_index("group")
    d = lax.axis_index("dp")
    other = 1 - m
    ypeer = partner("group", 1)[1]
    core, xbit = pn.bits[0], pn.bits[1]
    rounds = [("dp", s) for s in pn.bits] + [("group", 1)]
    count = iter(range(1000))

    def across(subset):
        to = {}
        for axis, step in subset:
            at = to.get(axis, lax.axis_index(axis))
            to[axis] = at + step - 2 * step * lax.rem(lax.div(lax.axis_index(axis), step), 2)
        return to

    def subsets(phase):
        return [[r for k, r in enumerate(phase) if mask >> k & 1] for mask in range(1, 1 << len(phase))]

    met = [across(sub) for phase in pn.phases for sub in subsets(phase)]
    lcount = iter(range(100))

    def bit(step):
        return lax.rem(lax.div(d, step), 2)

    def remote(src, dst, to, k=None):
        k = next(count) if k is None else k
        return pltpu.make_async_remote_copy(
            src_ref=src, dst_ref=dst, send_sem=ssem.at[k], recv_sem=rsem.at[k],
            device_id=to, device_id_type=MESH)

    def local(src, dst):
        copy = pltpu.make_async_copy(src, dst, lsem.at[next(lcount)])
        copy.start()
        return copy

    gws = [{s: 1 << k for k, s in enumerate(order)} for order in pn.gather_orders]
    poss = [sum(bit(s) * gw[s] for s in pn.bits) for gw in gws]
    tiles = n_dp

    c_q = [local(queries.at[g * quota : (g + 1) * quota], q_all.at[g, poss[g]]) for g in range(2)]
    c_meta = [local(ids_in, ids_v)]
    c_slab = [local(corpus.at[:, n * 256 : (n + 1) * 256], big.at[n * slab : (n + 1) * slab])
              for n in range(fg // 256)]
    c_mine = local(items.at[pl.ds(pl.multiple_of(m * quota, quota), quota)], mine.at[0:quota])
    c_w1 = local(w1, w1v.at[0])
    c_w2 = local(w2, w2v.at[0])
    greet(met)

    class Spread:
        def __init__(self, first, follow, n):
            self.follow, self.n, self.k = follow, n, 0
            self.live = first
            for c in first:
                c.start()

        def go(self):
            for c in self.live:
                c.wait()
            self.live = []
            if self.k < self.n:
                self.live = self.follow(self.k)
                for c in self.live:
                    c.start()
                self.k += 1

    n_piece = 1 << len(pn.w_gathers[0])
    es = [sum(bit(s) << k for k, s in enumerate(gather)) for gather in pn.w_gathers]
    q1, q2 = fg // n_piece, hg // 2 // n_piece

    def w_rows(u, half, size):
        base = lax.div(es[u], size) * size
        return (pl.ds(pl.multiple_of(half * fg + base * q1, q1), size * q1),
                pl.ds(pl.multiple_of(half * (hg // 2) + base * q2, q2), size * q2))

    def w_spread(u, half, far_half):
        a, b = w_rows(u, far_half, 1)

        def follow(k):
            at1, at2 = w_rows(u, half, 1 << k)
            to = partner("dp", pn.w_gathers[u][k])[1]
            return [remote(w1v.at[1, at1], w1v.at[1, at1], to),
                    remote(w2v.at[1, at2], w2v.at[1, at2], to)]

        return Spread([remote(w1.at[a], w1v.at[1, a], ypeer), remote(w2.at[b], w2v.at[1, b], ypeer)],
                      follow, len(pn.w_gathers[u]))

    def q_spread(g):
        def follow(k):
            view = q_all.at[g, pl.ds(lax.div(poss[g], 1 << k) * (1 << k), 1 << k)]
            return [remote(view, view, partner("dp", pn.gather_orders[g][k])[1])]

        return Spread(follow(0), lambda k: follow(k + 1), len(pn.bits) - 1)

    ws = [w_spread(0, m, other), w_spread(1, other, m)]
    for c in c_q:
        c.wait()
    qs = [q_spread(0), q_spread(1)]
    item_send = remote(items.at[pl.ds(pl.multiple_of(other * quota, quota), quota)],
                       peer.at[0:quota], ypeer)
    item_send.start()
    k_far = [next(count) for _ in range(chunks)][0]

    def rows_at(k):
        return pl.ds(pl.multiple_of(quota + k * CH, CH), CH)

    def far_copy(k):
        return remote(far.at[pl.ds(pl.multiple_of(k * CH, CH), CH)], peer.at[rows_at(k)],
                      ypeer, k_far + k)

    def column(ref, r):
        return jnp.broadcast_to(ref[pl.ds(r, 1), :].astype(F32), (8, CH)).T[:, :1]

    def pick(who, k, dst, at):
        ids = column(ids_v, who * chunks + k)
        where = lax.broadcasted_iota(jnp.int32, (CH, slab), 1).astype(F32)
        hot[...] = jnp.where(ids == where, 1.0, 0.0).astype(BF16)
        for n in range(fg // 256):
            dst[at, n * 256 : (n + 1) * 256] = mm(
                hot[...], big[n * slab : (n + 1) * slab, :]).astype(BF16)

    for c in c_meta + c_slab:
        c.wait()
    loop(chunks, lambda k: pick(other, k, far, pl.ds(pl.multiple_of(k * CH, CH), CH)))
    qs[0].go()
    qs[1].go()
    ws[0].go()
    ws[1].go()
    loop(chunks, lambda k: far_copy(k).start())
    loop(chunks, lambda k: pick(m, k, mine, rows_at(k)))
    ws[0].go()
    qs[0].go()
    ws[1].go()
    shift_v[...] = shift_in[...].astype(F32)
    bias[0:quota, :] = jnp.zeros((quota, width), F32)

    def put_bias(k):
        bias[rows_at(k), :] = jnp.broadcast_to(
            -column(shift_v, m * chunks + k), (CH, width))

    loop(chunks, put_bias)
    c_mine.wait()
    c_w1.wait()
    c_w2.wait()

    nj = hg // 256

    def tower_add(r0, r1, feat, half, c, first):
        for j in range(nj):
            part = mm(feat[r0:r1, :], w1v[c, pl.ds(pl.multiple_of(half * fg, fg), fg),
                                         j * 256 : (j + 1) * 256])
            if first:
                pre[c * nj + j, r0:r1, :] = part
            else:
                pre[c * nj + j, r0:r1, :] += part

    tower_add(0, rows, mine, m, 0, True)
    qs[1].go()

    hb = CH // 2

    def turn(src, half, n):
        at = pl.multiple_of(n * 256, 256)
        block = src[:, pl.ds(at, 256)].T
        for b in range(256 // CH):
            for k in range(2):
                row = half * fg + k * (fg // 2) + (n * (256 // CH) + b) * hb
                featt[pl.ds(pl.multiple_of(row, hb), hb), :] = block[
                    b * CH + k * hb : b * CH + (k + 1) * hb, :]

    loop(fg // 256, lambda n: turn(mine, m, n))
    ws[0].go()
    ws[1].go()
    qs[0].go()
    qs[1].go()
    ws[0].go()
    tower_add(0, rows, mine, m, 1, True)
    ws[1].go()

    def finish_tower(r0, r1):
        loop(2, lambda c: tower_add(r0, r1, peer, other, c, False))
        emb[r0:r1, :] = jnp.zeros((r1 - r0, e_dim), F32)

        def second_layer(c):
            for j in range(nj):
                h = jnp.maximum(pre[c * nj + j, r0:r1, :], 0.0).astype(BF16)
                hid[c * nj + j, r0:r1, :] = h
                emb[r0:r1, :] += mm(h, w2v[c, j * 256 : (j + 1) * 256, :])

        loop(2, second_layer)
        em = emb[r0:r1, :]
        inv = lax.rsqrt(jnp.mean(em * em, -1, keepdims=True) + 1e-06)
        no = (em * inv).astype(BF16)
        nrm[r0:r1, :] = no
        nrms[r0:r1, :] = (no.astype(F32) * scale).astype(BF16)
        nrm_t[:, r0:r1] = no.astype(F32).T.astype(BF16)

    oqs = [weights_of(order) for order in pn.q_orders]
    he = e_dim // 2

    def shard_of(i, g, h):
        return g * oqs[h][("group", 1)] + sum(
            lax.rem(lax.div(i, gws[g][s]), 2) * oqs[h][("dp", s)] for s in pn.bits)

    half_q = width // 2

    def queries_at(i):
        return jnp.concatenate([q_all[0, i], q_all[1, i]], 0)

    def score(r0, r1):
        def one(i):
            block = nt(nrms[r0:r1, :], queries_at(i)) + bias[r0:r1, :]
            logits[i, r0:r1, :] = block
            top = jnp.max(block, 0, keepdims=True)
            at = pl.ds(i, 1)
            if r0 == 0:
                stats[0, 1, at, :] = jnp.sum(jnp.exp(block - top), 0, keepdims=True)
            else:
                before = stats[0, 0, at, :]
                top = jnp.maximum(before, top)
                stats[0, 1, at, :] = stats[0, 1, at, :] * jnp.exp(before - top) + jnp.sum(
                    jnp.exp(block - top), 0, keepdims=True)
            stats[0, 0, at, :] = top

        loop_by(4, tiles, one)

    item_send.wait()
    done = 0
    for r0, r1 in zip(ROW_PARTS[:-1], ROW_PARTS[1:]):
        upto = (r1 - quota) // CH
        for k in range(done, upto):
            far_copy(k).wait()
        done = upto
        finish_tower(r0, r1)
        if r0 == 0:
            qs[0].go()
            qs[1].go()
        score(r0, r1)

    def query_part(i):
        p = jnp.exp(logits[i] - stats[0, 0, pl.ds(i, 1), :])
        part = mm(nrm_t[...], p.astype(BF16))
        for g in range(2):
            for h in range(2):
                qpt[h, shard_of(i, g, h)] = part[
                    h * he : (h + 1) * he, g * half_q : (g + 1) * half_q]

    lse[0] = stats[0, 0] + jnp.log(stats[0, 1])
    slot = 0
    for ph, phase in enumerate(pn.phases):
        copies = []
        for sub in subsets(phase):
            copies.append(remote(lse.at[ph], arrived.at[slot + len(copies)], across(sub)))
            copies[-1].start()
        if ph < 2:
            loop_by(4, tiles // 2, lambda i: query_part(ph * (tiles // 2) + i))
        else:
            loop(fg // 256, lambda n: turn(peer, other, n))
        for c in copies:
            c.wait()
        held = [lse[ph]] + [arrived[slot + k] for k in range(len(copies))]
        slot += len(copies)
        top = functools.reduce(jnp.maximum, held)
        lse[ph + 1] = top + jnp.log(sum(jnp.exp(a - top) for a in held))
    total_ref[...] = lse[len(pn.phases)]
    fac[...] = jnp.exp(stats[0, 0] - total_ref[...])

    class Chain:
        def __init__(self, order, put, add, send_at, recv_at):
            self.order, self.put, self.add = order, put, add
            self.send_at, self.recv_at = send_at, recv_at
            self.n = 1 << len(order)
            self.base = 0

        def launch(self, r):
            half = self.n >> (r + 1)
            at0 = self.n - 2 * half
            self.copy = remote(self.send_at(at0, half), self.recv_at(at0, half),
                               partner(*self.order[r])[1])
            self.copy.start()

        def send(self, r):
            half = self.n >> (r + 1)
            at0, came = self.n - 2 * half, self.n - 4 * half
            self.copy.wait()
            skip = (1 - partner(*self.order[r])[0]) * half
            base = self.base + skip
            loop_by(min(4, half), half, lambda j: self.put(at0 + j, base + j, came + skip + j))
            self.launch(r)

        def keep(self, r):
            half = self.n >> (r + 1)
            came = self.n - 4 * half
            skip = partner(*self.order[r])[0] * half
            base = self.base + skip
            loop_by(min(4, half), half, lambda j: self.add(base + j, came + skip + j))
            self.base = base

        def finish(self):
            self.copy.wait()
            self.add(self.base, self.n - 2)

    def advance(some, r):
        for ch in some:
            if r < len(ch.order):
                ch.send(r)
            else:
                ch.finish()
        for ch in some:
            if r < len(ch.order):
                ch.keep(r)

    cb = bit(core)
    own16 = cb * n_dp

    def q_chain(h):
        def put(slot, a, got):
            qsend[h, slot] = (qpt[h, own16 + a] + qrecv[h, got].astype(F32)).astype(BF16)

        def add(a, got):
            qpt[h, own16 + a] = qpt[h, own16 + a] + qrecv[h, got].astype(F32)

        return Chain(pn.q_orders[h], put, add,
                     lambda a, n: qsend.at[h, pl.ds(a, n)], lambda a, n: qrecv.at[h, pl.ds(a, n)])

    q_chains = [q_chain(0), q_chain(1)]

    def scaled(i, g, h):
        f = fac[pl.ds(i, 1), :][:, g * half_q : (g + 1) * half_q]
        return qpt[h, shard_of(i, g, h)] * f

    def q_first(h, k):
        i = (1 - cb) * (tiles // 2) + k
        for g in range(2):
            qsend[h, shard_of(i, g, h) - (1 - cb) * n_dp] = scaled(i, g, h).astype(BF16)

    def q_keep(k):
        i = cb * (tiles // 2) + k
        for g in range(2):
            for h in range(2):
                qpt[h, shard_of(i, g, h)] = scaled(i, g, h)

    for h in range(2):
        loop_by(4, tiles // 2, functools.partial(q_first, h))
        q_chains[h].launch(0)
    loop_by(4, tiles // 2, q_keep)

    hat[...] = jnp.zeros_like(hat)

    def second(i):
        p = jnp.exp(logits[i] - total_ref[pl.ds(i, 1), :]).astype(BF16)
        hat[...] += mm(p, queries_at(i))

    loop_by(4, tiles // 2, second)
    advance(q_chains, 1)
    loop_by(4, tiles // 2, lambda i: second(tiles // 2 + i))

    pos = jnp.where(m == 0, poss[0], poss[1])
    q_own = q_all[m, pos].astype(F32)
    positive = nrm[0:quota, :].astype(F32)
    mine_total = total_ref[pl.ds(pos, 1), :]
    mine_total = jnp.where(m == 0, mine_total[:, :half_q], mine_total[:, half_q:])
    loss_ref[...] = mine_total - scale * jnp.sum((q_own * positive).T, 0, keepdims=True)

    hat[0:quota, :] = hat[0:quota, :] - q_own
    em = emb[...]
    inv = lax.rsqrt(jnp.mean(em * em, -1, keepdims=True) + 1e-06)
    gn = scale * hat[...]
    along = jnp.sum(gn * em, -1, keepdims=True)
    ge[...] = (inv * gn - inv**3 * em * along / e_dim).astype(BF16)

    def back(c):
        for j in range(nj):
            g = nt(ge[...], w2v[c, j * 256 : (j + 1) * 256, :])
            gp[c * nj + j] = jnp.where(pre[c * nj + j] > 0, g, 0.0).astype(BF16)

    loop(2, back)

    half_f = pn.feats // 2
    per_core = n_dp // 2
    n_all = 2 * n_dp

    def place(fb, g, order, spread):
        w = weights_of(order)
        return g * w[("group", 1)] + sum(
            (fb >> k) % 2 * w[("dp", s)] for k, s in enumerate(spread[:-1]))

    def group_of(c):
        return m if c == 0 else other

    starts = [sum(p[0] for p in pn.parts[:k]) for k in range(len(pn.parts))]

    def w1_half(cbit, k, sink):
        own = range(k * len(pn.groups[0]), (k + 1) * len(pn.groups[0]))
        span = pl.ds(pl.multiple_of(cbit * half_f + k * (half_f // 2), half_f // 2), half_f // 2)
        for c in range(2):
            for t in range(nj):
                r = mm(featt[span, :], gp[c * nj + t])
                for fb in range(per_core):
                    for p in own:
                        pr, order, spread = pn.parts[p]
                        at = fb * hb + starts[p] - k * hb
                        sink(p, place(fb, group_of(c), order, spread), t, r[at : at + pr, :])

    def piece_at(p, n, slot, t, size):
        pr = pn.parts[p][0]
        return pl.ds(pl.multiple_of(n * nj * starts[p] + slot * (nj * pr) + t * pr, 16), size * pr)

    def sink_send(p, j, t, v):
        big[piece_at(p, n_all - 1, j, t, 1), :] = v.astype(BF16)

    def cut_of(p, t):
        return slice(t * CH + starts[p], t * CH + starts[p] + pn.parts[p][0])

    def sink_acc(p, j, t, v):
        logits[j, cut_of(p, t), :] = v

    def w_chain(p):
        def total(a, got, t):
            return logits[a, cut_of(p, t), :] + recv[
                piece_at(p, n_all - 1, got, t, 1), :].astype(F32)

        def put(slot, a, got):
            for t in range(nj):
                sink_send(p, slot, t, total(a, got, t))

        def add(a, got):
            for t in range(nj):
                logits[a, cut_of(p, t), :] = total(a, got, t)

        return Chain(pn.parts[p][1], put, add,
                     lambda s, n: big.at[piece_at(p, n_all - 1, s, 0, n * nj)],
                     lambda s, n: recv.at[piece_at(p, n_all - 1, s, 0, n * nj)])

    h2 = 256 // per_core

    def w2_half(cbit, sink):
        for c in range(2):
            r = tn(hid[c * nj + cbit], ge[...])
            for fb in range(per_core):
                sink(place(fb, group_of(c), *pn.w2_part), r[fb * h2 : (fb + 1) * h2, :])

    def w2_send(j, v):
        send2[j] = v.astype(BF16)

    def w2_acc(j, v):
        acc2[j] = v

    def w2_put(slot, a, got):
        send2[slot] = (acc2[a] + recv2[got].astype(F32)).astype(BF16)

    def w2_add(a, got):
        acc2[a] = acc2[a] + recv2[got].astype(F32)

    chains = [w_chain(p) for p in range(len(pn.parts))]
    w2_chain = Chain(pn.w2_part[0], w2_put, w2_add,
                     lambda a, n: send2.at[pl.ds(a, n)], lambda a, n: recv2.at[pl.ds(a, n)])
    teams = [chains[:3], chains[3:] + [w2_chain]]
    for k in range(2):
        w1_half(1 - cb, k, sink_send)
        for ch in chains[3 * k : 3 * k + 3]:
            ch.launch(0)
    w2_half(1 - cb, w2_send)
    w2_chain.launch(0)
    advance(q_chains, 2)
    w1_half(cb, 0, sink_acc)
    advance(teams[0], 1)
    w1_half(cb, 1, sink_acc)
    w2_half(cb, w2_acc)
    advance(teams[1], 1)
    advance(q_chains, 3)
    every = chains + [w2_chain]
    steps = len(rounds)
    for r in range(2, steps):
        for team in teams:
            advance(team, r)
        if r + 2 <= steps:
            advance(q_chains, r + 2)

    def block_of(spread):
        return sum(bit(s) << k for k, s in enumerate(spread))

    def w1_view(p, b, n):
        return ag.at[piece_at(p, n_dp, b, 0, n * nj)]

    def start_gather(i):
        p = every.index(i)
        if i is w2_chain:
            spread = pn.w2_part[1]
            fb = block_of(spread)
            ag2[fb] = acc2[i.base].astype(BF16)
            return spread, fb, lambda b, n: ag2.at[pl.ds(b, n)]
        spread = pn.parts[p][2]
        fb = block_of(spread)
        for t in range(nj):
            ag[piece_at(p, n_dp, fb, t, 1), :] = logits[i.base, cut_of(p, t), :].astype(BF16)
        return spread, fb, functools.partial(w1_view, p)

    def share(one, k):
        spread, fb, view = one
        size = 1 << k
        v = view(lax.div(fb, size) * size, size)
        c = remote(v, v, partner("dp", spread[k])[1])
        c.start()
        return c

    live, views = [], []
    for team in teams:
        group = []
        for ch in team:
            ch.finish()
            group.append(start_gather(ch))
        views.append(group)
        live.append([share(one, 0) for one in group])
    for k in range(1, len(pn.bits) + 1):
        for i, group in enumerate(views):
            for j, one in enumerate(group):
                live[i][j].wait()
                if k < len(pn.bits):
                    live[i][j] = share(one, k)

    for h in range(2):
        gq_ref[:, h * he : (h + 1) * he] = scale * (
            qpt[h, own16 + q_chains[h].base].T - positive[:, h * he : (h + 1) * he])

    for p in range(len(chains)):
        def out_rows(fb):
            for t in range(nj):
                gw1_ref[pl.ds(pl.multiple_of(fb * CH + starts[p], 16), pn.parts[p][0]),
                        t * 256 : (t + 1) * 256] = ag[piece_at(p, n_dp, fb, t, 1), :]

        loop_by(4, n_dp, out_rows)
    gw2_ref[...] = ag2[...].reshape(gw2_ref.shape)


def fused(n_dp, queries, items, corpus, sample_ids, sample_shift, w1, w2):
    pn = Plan(n_dp, queries, items, corpus, w1, w2)
    width, emb = queries.shape
    negs = sample_ids.shape[0] // 2
    rows = pn.quota + negs
    fg, feats, hg = pn.fg, pn.feats, pn.hg
    nj = hg // 256
    n_all = 2 * n_dp
    rounds = n_all.bit_length() - 1
    ids = sample_ids.reshape(-1, CH)
    shifts = sample_shift.reshape(-1, CH)
    half = feats // 2
    sends = (n_all - 1) * nj * CH
    big = -(-max(sends, (fg // 256) * pn.slab) // 16) * 16
    hp = hg // n_dp
    n_sem = 128
    S = pltpu.VMEM
    loss, gq, gw1, gw2 = pl.pallas_call(
        functools.partial(fused_kernel, pn, rows),
        out_shape=(
            jax.ShapeDtypeStruct((1, pn.quota), F32),
            jax.ShapeDtypeStruct((pn.quota, emb), F32),
            jax.ShapeDtypeStruct((feats, hg), BF16),
            jax.ShapeDtypeStruct((hg, emb), BF16),
        ),
        in_specs=[ANY] * 4 + [VMEM] + [ANY] * 2,
        out_specs=(VMEM,) * 4,
        scratch_shapes=[
            S((big, 256), BF16),
            S((2, n_dp, width // 2, emb), BF16),
            S((2, feats, hg), BF16),
            S((2, hg, emb), BF16),
            S((rows, fg), BF16),
            S((rows, fg), BF16),
            S((negs, fg), BF16),
            S((CH, pn.slab), BF16),
            S(ids.shape, jnp.int32),
            S(shifts.shape, F32),
            S((2 * nj, rows, 256), F32),
            S((2 * nj, rows, 256), BF16),
            S((rows, emb), F32),
            S((rows, emb), BF16),
            S((rows, emb), BF16),
            S((emb, rows), BF16),
            S((rows, width), F32),
            S((rows, emb), F32),
            S((n_dp, rows, width), F32),
            S((2, n_all, emb // 2, width // 2), F32),
            S((1, 2, n_dp, width), F32),
            S((len(pn.phases) + 1, n_dp, width), F32),
            S((sum((1 << len(p)) - 1 for p in pn.phases), n_dp, width), F32),
            S((n_dp, width), F32),
            S((n_dp, width), F32),
            S((feats, rows), BF16),
            S((2 * nj, rows, 256), BF16),
            S((rows, emb), BF16),
            S((sends, 256), BF16),
            S((n_dp * nj * CH, 256), BF16),
            S((2, n_all - 1, emb // 2, width // 2), BF16),
            S((2, n_all - 1, emb // 2, width // 2), BF16),
            S((n_dp, hp, emb), F32),
            S((n_all - 1, hp, emb), BF16),
            S((n_all - 1, hp, emb), BF16),
            S((n_dp, hp, emb), BF16),
            pltpu.SemaphoreType.DMA((16,)),
            pltpu.SemaphoreType.DMA((n_sem,)),
            pltpu.SemaphoreType.DMA((n_sem,)),
        ],
        compiler_params=pltpu.CompilerParams(
            collective_id=2, has_side_effects=True, vmem_limit_bytes=62 << 20),
        name="fused",
    )(queries, items, corpus, ids, shifts, w1, w2)
    return widen(loss, gq, gw1, gw2)


def widen_kernel(*refs):
    n = len(refs) // 2
    for a, b in zip(refs[:n], refs[n:]):
        b[...] = a[...].astype(F32)


def widen(loss, *grads):
    parts = 2
    specs = [pl.BlockSpec(loss.shape, lambda i: (0, 0))] + [
        pl.BlockSpec((x.shape[0] // parts, x.shape[1]), lambda i: (i, 0)) for x in grads]
    loss, *grads = pl.pallas_call(
        widen_kernel,
        grid=(parts,),
        out_shape=tuple(jax.ShapeDtypeStruct(x.shape, F32) for x in (loss, *grads)),
        in_specs=specs,
        out_specs=tuple(specs),
        name="widen",
    )(loss, *grads)
    return (loss.reshape(-1), *grads)


def fits(n_dp, groups, queries, items, corpus, sample_ids, w1, w2):
    negs = sample_ids.shape[0] // groups
    return (
        groups == 2 and n_dp == 16 and queries.shape == (256, 256)
        and (256 // groups + negs) == ROW_PARTS[-1]
        and w1.shape == (n_dp * CH, 512) and w2.shape == (512, 256)
        and items.shape[1] * 2 == w1.shape[0] and corpus.shape[0] % 256 == 0
    )


def per_device(queries, item_features, corpus, sample_ids, sample_shift, w1, w2):
    groups = lax.axis_size("group")
    member = lax.axis_index("group")
    n_dp = lax.axis_size("dp")
    d = lax.axis_index("dp")
    if fits(n_dp, groups, queries, item_features, corpus, sample_ids, w1, w2):
        return fused(n_dp, queries, item_features, corpus, sample_ids, sample_shift, w1, w2)
    query_rows, emb = queries.shape
    quota = query_rows // groups
    negs = sample_ids.shape[0] // groups
    rows = quota + negs
    fg = item_features.shape[1]
    scale = emb ** (-0.5)

    def shift(x, s):
        return lax.ppermute(x, "group", [(i, (i + s) % groups) for i in range(groups)])

    def at(x, i):
        return lax.dynamic_index_in_dim(x, lax.rem(i, groups), 0, keepdims=False)

    def place_columns(parts):
        if groups == 2:
            swap = member == 0
            return jnp.concatenate(
                [jnp.where(swap, parts[0], parts[1]), jnp.where(swap, parts[1], parts[0])], 1)
        out = jnp.zeros((parts[0].shape[0], groups * fg), BF16)
        for s in range(groups):
            start = lax.rem(member + groups - s, groups) * fg
            out = lax.dynamic_update_slice_in_dim(out, parts[s], start, 1)
        return out

    q_all = lax.all_gather(queries, "dp", axis=0, tiled=True)

    def swap_dp(x, step):
        return lax.ppermute(x, "dp", [(i, i ^ step) for i in range(n_dp)])

    def beside(x, cols):
        if x.shape[1] <= cols:
            return jnp.concatenate(jnp.split(x, cols // x.shape[1], 0), 1)
        return jnp.concatenate(jnp.split(x, x.shape[1] // cols, 1), 0)

    def restored(x, cols):
        if cols <= x.shape[1]:
            return jnp.concatenate(jnp.split(x, x.shape[1] // cols, 1), 0)
        return jnp.concatenate(jnp.split(x, cols // x.shape[1], 0), 1)

    quarter = lax.rem(d, 4)
    odd, high = lax.rem(quarter, 2) == 1, quarter >= 2
    w1_rows, w2_rows = w1.shape[0] // 4, w2.shape[0] // 4
    piece = jnp.concatenate([
        lax.dynamic_slice_in_dim(w1, quarter * w1_rows, w1_rows),
        beside(lax.dynamic_slice_in_dim(w2, quarter * w2_rows, w2_rows), w1.shape[1]),
    ], 0)
    items = item_features.reshape(groups, quota, fg)
    sample_ids, piece = lax.optimization_barrier((sample_ids, piece))
    got = [shift(piece, s) for s in range(1, groups)]
    ids = sample_ids.reshape(groups, negs)
    far_rows = [
        corpus.at[at(ids, member + s)].get(mode="promise_in_bounds") for s in range(1, groups)
    ]
    far_rows, items, got = lax.optimization_barrier((far_rows, items, got))
    item_parts = [shift(at(items, member + s), s) for s in range(1, groups)]
    picked_parts = [shift(far_rows[s - 1], s) for s in range(1, groups)]
    own_rows = corpus.at[at(ids, member)].get(mode="promise_in_bounds")
    blocks = [jnp.concatenate([at(items, member), own_rows], 0)]
    for s in range(1, groups):
        blocks.append(jnp.concatenate([at(items, member + s), far_rows[s - 1]], 0))
    local = jnp.stack(blocks[:1] if groups == 2 else blocks)

    w1s, w2s = [w1], [w2]
    for p0 in got:
        p2 = swap_dp(p0, 2)
        p1, p3 = swap_dp(p0, 1), swap_dp(p2, 1)
        low = [jnp.where(odd, p1, p0), jnp.where(odd, p0, p1)]
        upp = [jnp.where(odd, p3, p2), jnp.where(odd, p2, p3)]
        placed = [jnp.where(high, u, l) for u, l in zip(upp, low)]
        placed += [jnp.where(high, l, u) for u, l in zip(upp, low)]
        w1s.append(jnp.concatenate([p[:w1_rows] for p in placed], 0))
        w2s.append(jnp.concatenate([restored(p[w1_rows:], emb) for p in placed], 0))

    feats = place_columns(
        blocks[:1]
        + [jnp.concatenate([a, b], 0) for a, b in zip(item_parts, picked_parts)]
    )

    embedded = jnp.zeros((rows, emb), F32)
    pre_own = None
    for s in range(groups):
        pre = mm(feats, w1s[s])
        hid = jnp.maximum(pre, 0.0).astype(BF16)
        if s == 0:
            pre_own, hid_own = pre, hid
        embedded = embedded + mm(hid, w2s[s])
    inverse = lax.rsqrt(jnp.mean(embedded * embedded, -1, keepdims=True) + 1e-06)
    normed = (embedded * inverse).astype(BF16)
    shift_own = lax.dynamic_slice_in_dim(sample_shift, member * negs, negs).astype(F32)
    bias = jnp.concatenate([jnp.zeros((quota,), F32), -shift_own])

    log_total, grad_hat, query_part, landed = score(
        groups, n_dp, local, q_all, normed, bias[:, None])
    log_total = log_total.reshape(-1)
    rest = place_columns(
        [jnp.concatenate(blocks[1:], 0)] + [landed[s - 1].reshape(-1, fg) for s in range(1, groups)]
    )

    query_own = lax.dynamic_slice_in_dim(queries, member * quota, quota).astype(F32)
    positive_own = normed[:quota].astype(F32)
    positive = scale * jnp.sum(query_own * positive_own, -1)
    query_loss = (
        lax.dynamic_slice_in_dim(log_total, d * query_rows + member * quota, quota) - positive
    )
    target = jnp.concatenate([query_own, jnp.zeros((negs, emb), F32)], 0)
    grad_normed = scale * (grad_hat - target)
    along = jnp.sum(grad_normed * embedded, -1, keepdims=True)
    grad_embed = (
        inverse * grad_normed - inverse**3 * embedded * along / emb
    ).astype(BF16)

    pre_rest = mm(rest, w1)
    hid_rest = jnp.maximum(pre_rest, 0.0).astype(BF16)
    back = jnp.concatenate(
        [grad_embed] + [shift(grad_embed, (groups - t) % groups) for t in range(1, groups)], 0
    )
    mask = jnp.concatenate([pre_own, pre_rest], 0) > 0
    grad_pre = jnp.where(mask, mm(back, w2.T), 0.0).astype(BF16)
    hid_all = jnp.concatenate([hid_own, hid_rest], 0)
    over_rows = (((0,), (0,)), ((), ()))
    grad_w2 = lax.dot_general(hid_all, back, over_rows, preferred_element_type=F32)
    feats_all = jnp.concatenate([feats, rest], 0)
    grad_w1 = lax.dot_general(feats_all, grad_pre, over_rows, preferred_element_type=F32)
    dp_bits = bits_of(n_dp)
    near, far = dp_bits[:1], dp_bits[:1:-1]
    along_first = [("dp", b) for b in near + dp_bits[1:2] + far]
    along_last = [("dp", b) for b in near + far + dp_bits[1:2]]
    query_order = (
        [("dp", near[0])]
        + [("group", b) for b in bits_of(groups)]
        + [("dp", b) for b in dp_bits[1:2] + far]
    )
    pad = -grad_w2.shape[0] % (16 * n_dp)
    padded = jnp.pad(grad_w2, ((0, pad), (0, 0)))
    xs = [
        grad_w1.reshape(2 * n_dp, -1, grad_w1.shape[1]),
        padded.reshape(n_dp, -1, emb),
        query_part.reshape(n_dp * groups, quota, emb),
    ]
    out_a, out_b, out_w2, query_sum = reduce_all(groups, n_dp, xs, [
        (0, 0, n_dp, along_last, True),
        (0, n_dp, n_dp, along_first, True),
        (1, 0, n_dp, along_first, True),
        (2, 0, n_dp * groups, query_order, False),
    ])
    grad_query = scale * (query_sum[0] - positive_own)
    grad_w1 = jnp.concatenate([out_a, out_b], 0).reshape(grad_w1.shape).astype(F32)
    grad_w2 = out_w2.reshape(padded.shape)[: grad_w2.shape[0]].astype(F32)
    return (query_loss, grad_query, grad_w1, grad_w2)


def solution(mesh):
    in_specs = (
        P("dp", None),
        P("dp", "group"),
        P("dp", "group"),
        P("dp"),
        P("dp"),
        P(None, "group"),
        P("group", None),
    )
    out_specs = (P(("dp", "group")), P(("dp", "group"), None), P(None, "group"), P("group", None))
    return jax.shard_map(
        per_device, mesh=mesh, in_specs=in_specs, out_specs=out_specs, check_vma=False
    )
```
